32 devices in a mesh: head: 4 (over y, x), blk: 8 (over z, core).
Axes of the slice: x: 2, y: 2, z: 4, core: 2. Of those that a mesh axis runs over, the one named last changes fastest.
Arguments:
- tokens: bfloat16 [4096, 2048], P(('blk', 'head')), may hold values from -8 to 8
- segments: int32 [4096], P(('blk', 'head')), may hold values from 0 to 32, as said below
- cotangent: bfloat16 [4096, 2048], P(('blk', 'head')), may hold values from -8 to 8
- first_gain: bfloat16 [2048], P(('head', 'blk')), may hold values from 0.5 to 1.5
- first_shift: bfloat16 [2048], P(('head', 'blk')), may hold values from -1.25 to 1.25
- query_proj: bfloat16 [2048, 2048], P(('head', 'blk')), may hold values from -0.1875 to 0.1875
- key_proj: bfloat16 [2048, 2048], P(('head', 'blk')), may hold values from -0.1875 to 0.1875
- value_proj: bfloat16 [2048, 2048], P(('head', 'blk')), may hold values from -0.125 to 0.125
- query_bias: bfloat16 [2048], P(('head', 'blk')), may hold values from -1.75 to 1.75
- value_bias: bfloat16 [2048], P(('head', 'blk')), may hold values from -0.625 to 0.625
- out_proj: bfloat16 [2048, 2048], P(('head', 'blk')), may hold values from -0.5 to 0.5
- out_bias: bfloat16 [2048], P(('head', 'blk')), may hold values from -1.75 to 1.75
- second_gain: bfloat16 [2048], P(('head', 'blk')), may hold values from 0.5 to 1.5
- second_shift: bfloat16 [2048], P(('head', 'blk')), may hold values from -1.25 to 1.25
- up_proj: bfloat16 [2048, 8192], P(('head', 'blk')), may hold values from -0.125 to 0.125
- up_bias: bfloat16 [8192], P(('head', 'blk')), may hold values from -1.75 to 1.75
- down_proj: bfloat16 [8192, 2048], P(('head', 'blk')), may hold values from -0.0625 to 0.0625
- down_bias: bfloat16 [2048], P(('head', 'blk')), may hold values from -1.75 to 1.75
Outputs:
- output: bfloat16 [4096, 2048], P(('blk', 'head'))
- tokens_grad: bfloat16 [4096, 2048], P(('blk', 'head'))
- first_gain_grad: float32 [2048], P(('head', 'blk'))
- first_shift_grad: float32 [2048], P(('head', 'blk'))
- query_proj_grad: float32 [2048, 2048], P(('head', 'blk'))
- key_proj_grad: float32 [2048, 2048], P(('head', 'blk'))
- value_proj_grad: float32 [2048, 2048], P(('head', 'blk'))
- query_bias_grad: float32 [2048], P(('head', 'blk'))
- value_bias_grad: float32 [2048], P(('head', 'blk'))
- out_proj_grad: float32 [2048, 2048], P(('head', 'blk'))
- out_bias_grad: float32 [2048], P(('head', 'blk'))
- second_gain_grad: float32 [2048], P(('head', 'blk'))
- second_shift_grad: float32 [2048], P(('head', 'blk'))
- up_proj_grad: float32 [2048, 8192], P(('head', 'blk'))
- up_bias_grad: float32 [8192], P(('head', 'blk'))
- down_proj_grad: float32 [8192, 2048], P(('head', 'blk'))
- down_bias_grad: float32 [2048], P(('head', 'blk'))
The draws below stay inside these ranges and needn't reach their ends.
Inputs may be any that keep to these rules, and one draw needn't show every extreme that they name: `segments`: segment numbers never fall along the sequence, and every number from 0 to 32 names at least one token. Document 16 begins within the first 512 tokens and ends within the last 512 tokens; the documents numbered below it lie before it and those numbered above it after it.
All inputs are finite; a program needn't handle non-finite values.
Results may differ from the reference program's by a relative error of at most 0.017.
Values may be sent and summed in bfloat16 or wider, within the bound.
No kernel may reach another device: no remote copies, remote signals or barrier semaphores. Data moves between devices by JAX's collectives and lax.ppermute only.
A program may use at most 384 MiB of HBM per device.

```python
import math
import jax
import jax.numpy as jnp
from jax import lax

D = 2048
H = 16
DH = 128
FF = 8192
SEQ = 4096
SPAN = 512
ENDS = 16


def end_documents(key):
    keys = jax.random.split(key, 2)
    region = jax.random.randint(keys[0], (), ENDS, SPAN // 2 + 1)
    spots = jnp.arange(1, SPAN, dtype=jnp.int32)
    noise = jax.random.randint(keys[1], (SPAN - 1,), 0, 4096)
    scores = noise * SPAN + spots + jnp.where(spots >= region, 4097 * SPAN, 0)
    order = jnp.argsort(scores, stable=True)
    cuts = spots[order[:ENDS - 1]]
    return (region, cuts)


def draw_segments(key, part):
    key = jax.random.fold_in(key, 7)
    first_key, last_key = jax.random.split(key)
    head_region, head_cuts = end_documents(first_key)
    tail_region, tail_cuts = end_documents(last_key)
    positions = jnp.arange(SEQ, dtype=jnp.int32)
    tail_start = SEQ - tail_region
    counted = jnp.sum((positions[:, None] >= head_cuts[None, :]).astype(jnp.int32), axis=1)
    counted = counted + (positions >= head_region).astype(jnp.int32) + (positions >= tail_start).astype(jnp.int32)
    counted = counted + jnp.sum((positions[:, None] >= tail_start + tail_cuts[None, :]).astype(jnp.int32), axis=1)
    return counted


def with_spikes(values, rng, source, target, shards_of, factor):
    def block_of(dim):
        return (jnp.arange(values.shape[dim]) // (values.shape[dim] // shards_of)).reshape((-1,) + (1,) * (values.ndim - 1 - dim))

    near = jax.random.permutation(rng, shards_of)[block_of(target)]
    far = (block_of(target) + shards_of // 2) % shards_of
    return jnp.where((block_of(source) == near) | (block_of(source) == far), factor * values, values)


def steps_of(stream_key, extent, shards, smallest, largest):
    loudness = 1.0
    for axis_at, parts in shards:
        heights = jax.random.uniform(jax.random.fold_in(jax.random.fold_in(stream_key, 6), axis_at), (parts,), jnp.float32, smallest / len(shards), largest / len(shards))
        loudness = loudness * jnp.repeat(jnp.exp(heights), extent[axis_at] // parts).reshape((-1,) + (1,) * (len(extent) - 1 - axis_at))
    return loudness


def bell_draw(stream_key, dims, scale, reach, pieces=(), held_as=jnp.bfloat16):
    level = steps_of(stream_key, dims, pieces, -0.22, 0.18) if pieces else 1.0
    array = jax.random.normal(stream_key, dims, jnp.float32) * scale * level
    return jnp.minimum(jnp.maximum(array, -reach), reach).astype(held_as)


def gaussian_with(own_key, dims, scale, limit, pieces, heavy, kind=jnp.bfloat16):
    array = scale * jax.random.normal(own_key, dims, jnp.float32)
    if pieces:
        array = array * steps_of(own_key, dims, pieces, -0.22, 0.18)
    return jnp.clip(with_spikes(array, jax.random.fold_in(own_key, 3), *heavy), -limit, limit).astype(kind)


def setup_inputs(seed: int = 0) -> dict:
    seeds = jax.random.split(jax.random.key(seed), 19)
    tokens = bell_draw(seeds[0], (SEQ, D), 1.0, 8.0, ((0, 32),))
    segments = draw_segments(jax.random.fold_in(seeds[18], 71), 0)
    cotangent = gaussian_with(seeds[2], (SEQ, D), 1.0, 8.0, ((0, 32),), (0, 1, 32, 2.75))
    first_gain = jnp.clip(1.0 + 0.1 * jax.random.normal(seeds[3], (D,), jnp.float32), 0.5, 1.5).astype(jnp.bfloat16)
    first_shift = bell_draw(seeds[4], (D,), 0.2, 1.25, ((0, 32),))
    query_proj = bell_draw(seeds[5], (D, D), (D // 2) ** -0.5, 0.1875, ((0, 32),))
    key_proj = bell_draw(seeds[6], (D, D), (D // 2) ** -0.5, 0.1875, ((0, 32),))
    value_proj = bell_draw(seeds[7], (D, D), D ** -0.5, 0.125, ((0, 32),))
    query_bias = bell_draw(seeds[8], (D,), 0.3, 1.75, ((0, 32),))
    value_bias = bell_draw(seeds[9], (D,), 0.1, 0.625, ((0, 32),))
    out_proj = bell_draw(seeds[10], (D, D), (D // 16) ** -0.5, 0.5, ((0, 32),))
    out_bias = bell_draw(seeds[11], (D,), 0.3, 1.75, ((0, 32),))
    second_gain = jnp.clip(1.0 + 0.1 * jax.random.normal(seeds[12], (D,), jnp.float32), 0.5, 1.5).astype(jnp.bfloat16)
    second_shift = bell_draw(seeds[13], (D,), 0.2, 1.25, ((0, 32),))
    up_proj = bell_draw(seeds[14], (D, FF), D ** -0.5, 0.125, ((0, 32),))
    up_bias = bell_draw(seeds[15], (FF,), 0.3, 1.75, ((0, 32),))
    down_proj = bell_draw(seeds[16], (FF, D), FF ** -0.5, 0.0625, ((0, 32),))
    down_bias = bell_draw(seeds[17], (D,), 0.3, 1.75, ((0, 32),))
    return {"tokens": tokens, "segments": segments, "cotangent": cotangent, "first_gain": first_gain, "first_shift": first_shift, "query_proj": query_proj, "key_proj": key_proj, "value_proj": value_proj, "query_bias": query_bias, "value_bias": value_bias, "out_proj": out_proj, "out_bias": out_bias, "second_gain": second_gain, "second_shift": second_shift, "up_proj": up_proj, "up_bias": up_bias, "down_proj": down_proj, "down_bias": down_bias}


@jax.custom_vjp
def low(v):
    return lax.optimization_barrier(v.astype(jnp.bfloat16)).astype(jnp.float32)

@jax.custom_vjp
def low_back(v):
    return v

def low_keep(v):
    return (low(v), None)

def low_pass(kept, grad):
    return (grad,)

def back_keep(v):
    return (v, None)

def back_low(kept, grad):
    return (low(grad),)
low.defvjp(low_keep, low_pass)
low_back.defvjp(back_keep, back_low)
norm_epsilon = 1e-05
masked_fill = -1e+30
highest = lax.Precision.HIGHEST

def matmul(left, right):
    return jnp.dot(left, right, precision=highest, preferred_element_type=jnp.float32)

def normalize(values, gain, shift):
    row_mean = lax.optimization_barrier(jnp.mean(values, axis=-1, keepdims=True))
    centered = values - row_mean
    row_var = lax.optimization_barrier(jnp.mean(centered * centered, axis=-1, keepdims=True))
    return centered * lax.rsqrt(row_var + norm_epsilon) * gain + shift

def attend(query_heads, key_heads, value_heads, segments):
    length = query_heads.shape[0]
    block_rows = math.gcd(length, 512)
    positions = jnp.arange(length, dtype=jnp.int32)
    scaling = DH ** (-0.5)

    def score_block(inputs):
        query_block, query_pos, query_seg = inputs
        raw_scores = jnp.einsum('qhd,khd->hqk', query_block, key_heads, precision=highest)
        scores = low_back(scaling * raw_scores)
        allowed = (positions[None, :] <= query_pos[:, None]) & (segments[None, :] == query_seg[:, None])
        scores = jnp.where(allowed[None], scores, masked_fill)
        weights = low(jax.nn.softmax(scores, axis=-1))
        return jnp.einsum('hqk,khd->qhd', weights, value_heads, precision=highest)
    blocks_in = (query_heads.reshape(length // block_rows, block_rows, H, DH), positions.reshape(length // block_rows, block_rows), segments.reshape(length // block_rows, block_rows))
    mixed_out = lax.map(jax.checkpoint(score_block), blocks_in)
    return mixed_out.reshape(length, H, DH)

def forward(inputs, segments, first_gain, first_shift, query_proj, key_proj, value_proj, query_bias, value_bias, out_proj, out_bias, second_gain, second_shift, up_proj, up_bias, down_proj, down_bias):
    length = inputs.shape[0]
    head_shape = (length, H, DH)
    normed = low(normalize(inputs, first_gain, first_shift))
    query_tok = low(low_back(matmul(normed, query_proj) + query_bias))
    key_tok = low(low_back(matmul(normed, key_proj)))
    value_tok = low(low_back(matmul(normed, value_proj) + value_bias))
    mixed_heads = attend(query_tok.reshape(head_shape), key_tok.reshape(head_shape), value_tok.reshape(head_shape), segments)
    mixed_tok = low(low_back(mixed_heads.reshape(length, D)))
    branch = low_back(matmul(mixed_tok, out_proj) + out_bias)
    hidden = inputs + branch
    second = low(normalize(hidden, second_gain, second_shift))
    up_value = low_back(matmul(second, up_proj) + up_bias)
    active = low(jax.nn.gelu(up_value, approximate=False))
    return hidden + low_back(matmul(active, down_proj) + down_bias)

def reference(tokens, segments, cotangent, first_gain, first_shift, query_proj, key_proj, value_proj, query_bias, value_bias, out_proj, out_bias, second_gain, second_shift, up_proj, up_bias, down_proj, down_bias):
    floats = [tokens, first_gain, first_shift, query_proj, key_proj, value_proj, query_bias, value_bias, out_proj, out_bias, second_gain, second_shift, up_proj, up_bias, down_proj, down_bias]
    floats = [item.astype(jnp.float32) for item in floats]

    def run_layer(*params):
        return forward(params[0], segments, *params[1:])
    result, pullback = jax.vjp(run_layer, *floats)
    gradients = pullback(cotangent.astype(jnp.float32))
    return (result.astype(jnp.bfloat16), gradients[0].astype(jnp.bfloat16), gradients[1], gradients[2], gradients[3], gradients[4], gradients[5], gradients[6], gradients[7], gradients[8], gradients[9], gradients[10], gradients[11], gradients[12], gradients[13], gradients[14], gradients[15])
```

```python
import functools

import jax
import jax.numpy as jnp
from jax import lax
from jax.experimental import pallas as pl
from jax.experimental.pallas import tpu as pltpu
from jax.sharding import PartitionSpec as P

D = 2048
H = 16
DH = 128

norm_epsilon = 1e-05
masked_fill = -1e30
tile = 256
bf16 = jnp.bfloat16
f32 = jnp.float32
log2_e = 1.4426950408889634
vmem_bytes = 48 * 1024 * 1024


def matmul(left, right):
    return jnp.dot(left, right, preferred_element_type=f32)


def cross_rows(left, right):
    return lax.dot_general(left, right, (((0,), (0,)), ((), ())), preferred_element_type=f32)


def times_transposed(left, right):
    return lax.dot_general(left, right, (((1,), (1,)), ((), ())), preferred_element_type=f32)


def norm_parts(values):
    row_mean = jnp.mean(values, axis=-1, keepdims=True)
    centered = values - row_mean
    row_var = jnp.mean(centered * centered, axis=-1, keepdims=True)
    inverse = lax.rsqrt(row_var + norm_epsilon)
    return (centered * inverse, inverse)


def norm_back(grad_out, normal_hat, inverse, gain):
    scaled_grad = grad_out * gain
    return inverse * (
        scaled_grad
        - jnp.mean(scaled_grad, axis=-1, keepdims=True)
        - normal_hat * jnp.mean(scaled_grad * normal_hat, axis=-1, keepdims=True)
    )


def swap(v, axis, mask):
    size = lax.axis_size(axis)
    return lax.ppermute(v, axis, [(i, i ^ mask) for i in range(size)])


def next_chip(v):
    size = lax.axis_size("blk")
    return lax.ppermute(v, "blk", [(i, (i + 2) % size) for i in range(size)])


def pick(v, index):
    return lax.dynamic_index_in_dim(v, index, 0, keepdims=False)


def put(v, part, index):
    return lax.dynamic_update_index_in_dim(v, part, index, 0)


def bits_of(size):
    return [1 << k for k in range(size.bit_length() - 1)]


def gather_ring(v):
    chips = lax.axis_size("blk") // 2
    pairs = []
    held = v
    for step in range(chips):
        later = next_chip(held) if step < chips - 1 else None
        pairs.append((held, swap(held, "blk", 1)))
        held = later
    return pairs


def scatter_ring(chunk, parts):
    chips = lax.axis_size("blk") // 2
    moving = [None] * parts
    for step in list(range(1, chips)) + [0]:
        term = chunk(step)
        rows = term.shape[0] // 2
        sub = rows // parts
        sums = []
        for part in range(parts):
            low, high = part * sub, (part + 1) * sub
            crossing = swap(term[rows + low : rows + high].astype(bf16), "blk", 1)
            total = term[low:high] + crossing.astype(f32)
            if moving[part] is not None:
                total = total + moving[part].astype(f32)
            if step != 0:
                moving[part] = next_chip(total.astype(bf16))
            else:
                sums.append(total)
    return jnp.concatenate(sums, axis=0) if parts > 1 else sums[0]


def gather_head(v):
    size = lax.axis_size("head")
    if size == 4:
        half = v.shape[0] // 2
        one, two = swap(v, "head", 1), swap(v, "head", 2)
        low = swap(two[:half], "head", 1)
        high = swap(one[half:], "head", 2)
        return [v, one, two, jnp.concatenate([low, high], axis=0)]
    held = [v]
    for bit in bits_of(size):
        held = held + [swap(part, "head", bit) for part in held]
    return held


def scatter_head(chunk):
    size = lax.axis_size("head")
    if size == 4:
        far = chunk(3).astype(bf16)
        half = far.shape[0] // 2
        low = swap(far[:half], "head", 1)
        high = swap(far[half:], "head", 2)
        one, two = chunk(1), chunk(2)
        one = jnp.concatenate([one[:half], one[half:] + high.astype(f32)], axis=0)
        two = jnp.concatenate([two[:half] + low.astype(f32), two[half:]], axis=0)
        one = swap(one.astype(bf16), "head", 1)
        two = swap(two.astype(bf16), "head", 2)
        return chunk(0) + one.astype(f32) + two.astype(f32)
    terms = [chunk(m) for m in range(size)]
    for bit in reversed(bits_of(size)):
        terms = [
            terms[m] + swap(terms[m | bit].astype(bf16), "head", bit).astype(f32) for m in range(bit)
        ]
    return terms[0]


def place_head(blocks, mine):
    out = jnp.zeros((len(blocks),) + blocks[0].shape, blocks[0].dtype)
    for mask, block in enumerate(blocks):
        out = put(out, block, mine ^ mask)
    return out


def exchange(pieces, axis, mine, group):
    out = pieces
    for mask in range(1, group):
        out = put(out, swap(pick(pieces, mine ^ mask), axis, mask), mine ^ mask)
    return out


def spread_rows(row, head, blk):
    n_head, n_blk = lax.axis_size("head"), lax.axis_size("blk")
    table = jnp.zeros((n_head * n_blk, row.shape[0]), row.dtype)
    table = put(table, row, head * n_blk + blk)
    for axis, size in (("head", n_head), ("blk", n_blk)):
        for bit in bits_of(size):
            table = table + swap(table, axis, bit)
    return table.reshape(n_head, n_blk, row.shape[0])


def sum_rows(table, head, blk):
    for axis, mine in (("head", head), ("blk", blk)):
        size = table.shape[0]
        for bit in reversed(bits_of(size)):
            halves = table.reshape((2, bit) + table.shape[1:])
            side = (mine // bit) % 2
            table = pick(halves, side) + swap(pick(halves, 1 - side), axis, bit)
        table = table[0]
    return table


def attend_tile(t, groups, factor, refs):
    q_pos, first, query = refs[:3]
    key_pos = refs[3 : 3 + groups]
    keys = refs[3 + groups : 3 + 2 * groups]
    values = refs[3 + 2 * groups : 3 + 3 * groups]
    out, log_total = refs[3 + 3 * groups :]
    high = jnp.full((tile, 1), masked_fill, f32)
    total = jnp.zeros((tile, 1), f32)
    acc = jnp.zeros((tile, DH), f32)
    seen = pl.ds(0, (t + 1) * tile)
    for m in range(groups):
        scores = times_transposed(query[...], keys[m][seen, :]) * factor
        pos = key_pos[m][:, seen]
        keep = (pos >= first[...]) & (pos <= q_pos[...])
        scores = jnp.where(keep, scores, masked_fill)
        new_high = jnp.maximum(high, jnp.max(scores, axis=-1, keepdims=True))
        weights = jnp.exp2(scores - new_high)
        shrink = jnp.exp2(high - new_high)
        total = total * shrink + jnp.sum(weights, axis=-1, keepdims=True)
        acc = acc * shrink + matmul(weights.astype(bf16), values[m][seen, :])
        high = new_high
    out[...] = (acc / total).astype(bf16)
    log_row = jnp.transpose(jnp.broadcast_to(high + jnp.log2(total), (tile, DH)))
    log_total[0] = log_row[0:1, :]


def attend_kernel(tiles, groups, factor, *refs):
    for t in range(tiles):
        pl.when(pl.program_id(1) == t)(functools.partial(attend_tile, t, groups, factor, refs))


def attend(q_pos, first, key_pos, query, keys, values):
    rows, width = query.shape
    groups = len(keys)
    heads = width // DH
    tiles = rows // tile
    column = pl.BlockSpec((tile, 1), lambda i, t: (t, 0))
    line = pl.BlockSpec((1, rows), lambda i, t: (0, 0))
    some = pl.BlockSpec((tile, DH), lambda i, t: (t, i))
    block = pl.BlockSpec((rows, DH), lambda i, t: (0, i))
    pairs = rows * rows * groups * heads // 2
    return pl.pallas_call(
        functools.partial(attend_kernel, tiles, groups, log2_e * DH**-0.5),
        grid=(heads, tiles),
        in_specs=[column, column, some] + [line] * groups + [block] * (2 * groups),
        out_specs=[some, pl.BlockSpec((1, 1, tile), lambda i, t: (i, 0, t))],
        out_shape=[
            jax.ShapeDtypeStruct((rows, width), bf16),
            jax.ShapeDtypeStruct((heads, 1, rows), f32),
        ],
        compiler_params=pltpu.CompilerParams(vmem_limit_bytes=vmem_bytes),
        cost_estimate=pl.CostEstimate(
            flops=4 * pairs * DH, bytes_accessed=4 * rows * width * groups, transcendentals=pairs
        ),
        name="attend",
    )(q_pos, first, query, *key_pos, *keys, *values)


def attend_back_tile(t, factor, scaling, carried, refs):
    q_pos, first, k_pos, log_total, delta, query, d_out, keys, values = refs[:9]
    dq, dk, dv = refs[-3:]
    rows = query.shape[0]
    ahead = pl.ds(t * tile, rows - t * tile)
    k_tile, v_tile = keys[...], values[...]
    q_part, d_part = query[ahead, :], d_out[ahead, :]
    scores = times_transposed(k_tile, q_part) * factor
    pos = k_pos[...]
    keep = (pos >= first[:, ahead]) & (pos <= q_pos[:, ahead])
    probs = jnp.where(keep, jnp.exp2(scores - log_total[0, :, ahead]), 0.0)
    dv[...] = matmul(probs.astype(bf16), d_part).astype(bf16)
    d_probs = times_transposed(v_tile, d_part)
    d_scores = (probs * (d_probs - delta[0, :, ahead])).astype(bf16)
    dk[...] = (scaling * matmul(d_scores, q_part)).astype(bf16)
    term = scaling * cross_rows(d_scores, k_tile)
    if t > 0:
        dq[ahead, :] += term
    elif carried:
        dq[...] = refs[9][...] + term
    else:
        dq[...] = term


def attend_back_kernel(tiles, factor, scaling, carried, *refs):
    for t in range(tiles):
        pl.when(pl.program_id(1) == t)(
            functools.partial(attend_back_tile, t, factor, scaling, carried, refs)
        )


def attend_back(q_pos, first, k_pos, log_total, delta, query, d_out, keys, values, dq_in):
    rows, width = query.shape
    heads = width // DH
    tiles = rows // tile
    column = pl.BlockSpec((tile, 1), lambda i, t: (t, 0))
    line = pl.BlockSpec((1, rows), lambda i, t: (0, 0))
    stat = pl.BlockSpec((1, 1, rows), lambda i, t: (i, 0, 0))
    some = pl.BlockSpec((tile, DH), lambda i, t: (t, i))
    block = pl.BlockSpec((rows, DH), lambda i, t: (0, i))
    pairs = rows * rows * heads // 2
    carried = dq_in is not None
    return pl.pallas_call(
        functools.partial(
            attend_back_kernel, tiles, log2_e * DH**-0.5, DH**-0.5, carried
        ),
        grid=(heads, tiles),
        in_specs=[line, line, column, stat, stat, block, block, some, some]
        + [block] * (1 if carried else 0),
        out_specs=[block, some, some],
        out_shape=[
            jax.ShapeDtypeStruct((rows, width), f32),
            jax.ShapeDtypeStruct((rows, width), bf16),
            jax.ShapeDtypeStruct((rows, width), bf16),
        ],
        compiler_params=pltpu.CompilerParams(vmem_limit_bytes=vmem_bytes),
        cost_estimate=pl.CostEstimate(
            flops=10 * pairs * DH, bytes_accessed=20 * rows * width, transcendentals=pairs
        ),
        name="attend_back",
    )(q_pos, first, k_pos, log_total, delta, query, d_out, keys, values, *([dq_in] if carried else []))


def local(
    tokens,
    segments,
    cotangent,
    first_gain,
    first_shift,
    query_proj,
    key_proj,
    value_proj,
    query_bias,
    value_bias,
    out_proj,
    out_bias,
    second_gain,
    second_shift,
    up_proj,
    up_bias,
    down_proj,
    down_bias,
):
    n_head, n_blk = lax.axis_size("head"), lax.axis_size("blk")
    head, blk = lax.axis_index("head"), lax.axis_index("blk")
    chips = n_blk // 2
    chip, core = blk // 2, blk % 2
    tok = tokens.shape[0]
    rows = tok * n_blk
    w_rows = query_proj.shape[0]
    ff_rows = down_proj.shape[0]
    team = DH // w_rows
    sets = n_blk // team
    each = n_head // team
    place = blk % team
    own_heads = each * DH

    def block_at(step, other):
        return 2 * ((chip - step + chips) % chips) + (core ^ other)

    with jax.named_scope("vectors"):
        small = [
            first_gain,
            first_shift,
            query_bias,
            value_bias,
            out_bias,
            second_gain,
            second_shift,
            down_bias,
            up_bias,
            segments.astype(bf16),
        ]
        table = spread_rows(jnp.concatenate(small), head, blk)

        def vector(index):
            return table[:, :, index * w_rows : (index + 1) * w_rows].reshape(D).astype(f32)

        def own_head_part(full):
            part = full.reshape(n_head, sets, DH)
            part = lax.dynamic_index_in_dim(part, blk // team, 1, keepdims=False)
            return lax.dynamic_slice_in_dim(part, place * each, each, 0).reshape(own_heads)

        gain_first, shift_first = vector(0), vector(1)
        q_bias, v_bias = own_head_part(vector(2)), own_head_part(vector(3))
        o_bias, gain_second, shift_second, d_bias = vector(4), vector(5), vector(6), vector(7)
        base = 8 * w_rows
        u_bias = table[:, :, base : base + ff_rows]
        u_bias = lax.dynamic_index_in_dim(u_bias, blk, 1, keepdims=False).reshape(-1).astype(f32)
        seq = table[:, :, base + ff_rows :].astype(f32)
        seg_rows = pick(seq, head).reshape(rows)
        seg_all = seq.transpose(1, 0, 2).reshape(-1)
        first_pos = jnp.sum((seg_all[None, :] < seg_rows[:, None]).astype(f32), axis=1)
        order = jnp.arange(rows, dtype=jnp.int32)

        def positions(of_head):
            return ((order // tok * n_head + of_head) * tok + order % tok).astype(f32)

        q_pos = positions(head)
        k_pos = [positions(head ^ m) for m in range(n_head)]

    with jax.named_scope("qkv_weights"):
        fused = jnp.stack([query_proj, key_proj, value_proj], axis=1)
        fused = fused.reshape(w_rows, 3, team, each, sets, DH).transpose(4, 2, 0, 1, 3, 5)
        fused = exchange(fused.reshape(n_blk, w_rows, 3 * own_heads), "blk", blk, n_blk)
        fused = gather_head(fused.reshape(n_blk * w_rows, 3 * own_heads))
        qkv_w = place_head(fused, head).reshape(D, 3 * own_heads)

    with jax.named_scope("tokens_gather"):
        tokens_all = jnp.zeros((n_blk, tok, D), bf16)
        for step, (mine, other) in enumerate(gather_ring(tokens)):
            tokens_all = put(tokens_all, mine, block_at(step, 0))
            tokens_all = put(tokens_all, other, block_at(step, 1))
        tokens_all = tokens_all.reshape(rows, D)

    with jax.named_scope("qkv"):
        hat_all, _ = norm_parts(tokens_all.astype(f32))
        normed = (hat_all * gain_first + shift_first).astype(bf16)
        qkv_bias = jnp.concatenate([q_bias, jnp.zeros_like(q_bias), v_bias])
        qkv = (matmul(normed, qkv_w) + qkv_bias).astype(bf16)
        query = qkv[:, :own_heads]

    with jax.named_scope("kv_gather"):
        pairs = gather_head(qkv[:, own_heads:])
        keys = [pair[:, :own_heads] for pair in pairs]
        values = [pair[:, own_heads:] for pair in pairs]

    with jax.named_scope("out_weights"):
        blocks = place_head(gather_head(out_proj), head)
        blocks = blocks.reshape(team, each, w_rows, D)
        out_w = exchange(blocks, "blk", place, team)
        out_w = out_w.transpose(1, 0, 2, 3).reshape(own_heads, D)

    with jax.named_scope("up_weights"):
        up_part = up_proj.reshape(w_rows, n_head, n_blk, ff_rows).transpose(2, 0, 1, 3)
        up_part = up_part.reshape(n_blk, w_rows, n_head * ff_rows)
        up_part = exchange(up_part, "blk", blk, n_blk)
        up_part = gather_head(up_part.reshape(n_blk * w_rows, n_head * ff_rows))
        up_w = place_head(up_part, head).reshape(D, n_head * ff_rows)

    with jax.named_scope("down_weights"):
        down_w = place_head(gather_head(down_proj), head).reshape(n_head * ff_rows, D)

    with jax.named_scope("dy_gather"):
        dy = [jnp.concatenate(pair, axis=0) for pair in gather_ring(cotangent)]

    with jax.named_scope("attention"):
        mixed, log_total = attend(
            q_pos[:, None],
            first_pos[:, None],
            [pos[None, :] for pos in k_pos],
            query,
            keys,
            values,
        )

    def two_blocks(array, step):
        part = array.reshape((n_blk, tok) + array.shape[1:])
        return jnp.concatenate([pick(part, block_at(step, 0)), pick(part, block_at(step, 1))], axis=0)

    with jax.named_scope("branch"):
        branch = scatter_ring(lambda step: matmul(two_blocks(mixed, step), out_w), 2)
        own = tokens.astype(f32)
        hidden = own + (branch + o_bias)
        hat_second, inv_second = norm_parts(hidden)
        second_own = (hat_second * gain_second + shift_second).astype(bf16)

    with jax.named_scope("mlp"):
        second = [jnp.concatenate(pair, axis=0) for pair in gather_ring(second_own)]
        active, d_upper = [None] * chips, [None] * chips

        def mlp_chunk(step):
            upper = matmul(second[step], up_w) + u_bias
            phi = 0.5 * (1.0 + lax.erf(upper * 0.7071067811865476))
            active[step] = (upper * phi).astype(bf16)
            slope = phi + upper * jnp.exp(-0.5 * upper * upper) * 0.3989422804014327
            d_active = times_transposed(dy[step], down_w)
            d_upper[step] = (d_active * slope).astype(bf16)
            return times_transposed(d_upper[step], up_w)

        d_second = scatter_ring(mlp_chunk, 2)
        upstream = cotangent.astype(f32)
        d_hidden = upstream + norm_back(d_second, hat_second, inv_second, gain_second)
        d_branch_own = d_hidden.astype(bf16)

    with jax.named_scope("d_branch_gather"):
        d_branch = jnp.zeros((n_blk, tok, D), bf16)
        for step, (mine, other) in enumerate(gather_ring(d_branch_own)):
            d_branch = put(d_branch, mine, block_at(step, 0))
            d_branch = put(d_branch, other, block_at(step, 1))
        d_branch = d_branch.reshape(rows, D)
        d_mixed = times_transposed(d_branch, out_w).astype(bf16)
        delta = jnp.sum(
            (d_mixed.astype(f32) * mixed.astype(f32)).reshape(rows, each, DH), axis=-1
        ).T.reshape(each, 1, rows)

    with jax.named_scope("attention_back"):
        done = {}
        dq = None

        def kv_grad(m):
            nonlocal dq
            dq, dk, dv = attend_back(
                q_pos[None, :],
                first_pos[None, :],
                k_pos[m][:, None],
                log_total,
                delta,
                query,
                d_mixed,
                keys[m],
                values[m],
                dq,
            )
            return jnp.concatenate([dk, dv], axis=1).astype(f32)

        d_kv = scatter_head(kv_grad).astype(bf16)
        d_qkv = jnp.concatenate([dq.astype(bf16), d_kv], axis=1)

    with jax.named_scope("d_normed"):
        first_sums = []

        def normed_chunk(step):
            term = times_transposed(two_blocks(d_qkv, step), qkv_w)
            hat = two_blocks(hat_all, step)
            first_sums.append((jnp.sum(term * hat, axis=0), jnp.sum(term, axis=0)))
            return term

        d_normed = scatter_ring(normed_chunk, 2)
        hat_first, inv_first = norm_parts(own)
        tokens_grad = (d_hidden + norm_back(d_normed, hat_first, inv_first, gain_first)).astype(bf16)

    with jax.named_scope("output"):
        out_sum = scatter_ring(lambda step: matmul(active[step], down_w), 2)
        output = (hidden + (out_sum + d_bias)).astype(bf16)

    def columns(array, m, width):
        return lax.dynamic_slice_in_dim(array, (head ^ m) * width, width, 1)

    with jax.named_scope("down_grad"):
        active_all, dy_all = jnp.concatenate(active, axis=0), jnp.concatenate(dy, axis=0)
        down_grad = scatter_head(lambda m: cross_rows(columns(active_all, m, ff_rows), dy_all))

    with jax.named_scope("up_grad"):
        second_all, d_upper_all = jnp.concatenate(second, axis=0), jnp.concatenate(d_upper, axis=0)
        slab = n_blk * w_rows
        up_grad = scatter_head(lambda m: cross_rows(columns(second_all, m, slab), d_upper_all))
        up_grad = up_grad.astype(bf16).reshape(n_blk, w_rows, n_head, ff_rows)
        up_grad = exchange(up_grad, "blk", blk, n_blk)
        up_grad = up_grad.transpose(1, 2, 0, 3).reshape(w_rows, -1).astype(f32)

    with jax.named_scope("out_grad"):
        out_term = cross_rows(mixed, d_branch).astype(bf16)
        out_term = out_term.reshape(each, team, w_rows, D).transpose(1, 0, 2, 3)
        out_term = exchange(out_term, "blk", place, team).reshape(n_head, w_rows, D).astype(f32)
        out_grad = scatter_head(lambda m: pick(out_term, head ^ m))

    with jax.named_scope("qkv_grad"):
        qkv_grad = scatter_head(lambda m: cross_rows(columns(normed, m, slab), d_qkv))
        qkv_grad = qkv_grad.astype(bf16).reshape(n_blk, w_rows, 3 * own_heads)
        qkv_grad = exchange(qkv_grad, "blk", blk, n_blk)
        qkv_grad = qkv_grad.reshape(sets, team, w_rows, 3, each, DH).transpose(3, 2, 1, 4, 0, 5)
        qkv_grad = qkv_grad.reshape(3, w_rows, D).astype(f32)

    with jax.named_scope("vector_grads"):
        full = [
            sum(pair[0] for pair in first_sums),
            sum(pair[1] for pair in first_sums),
            jnp.sum(d_branch_own.astype(f32), axis=0),
            jnp.sum(d_second * hat_second, axis=0),
            jnp.sum(d_second, axis=0),
            jnp.sum(upstream, axis=0),
        ]
        parts = [v.reshape(n_head, n_blk, w_rows) for v in full]
        up_sum = sum(jnp.sum(part.astype(f32), axis=0) for part in d_upper)
        up_table = jnp.zeros((n_blk, n_head, ff_rows), f32)
        up_table = put(up_table, up_sum.reshape(n_head, ff_rows), blk)
        parts.append(up_table.transpose(1, 0, 2))
        for v in (dq.astype(bf16), d_kv[:, own_heads:]):
            head_sum = jnp.sum(v.astype(f32), axis=0).reshape(each, 1, DH)
            head_table = jnp.zeros((n_head, sets, DH), f32)
            head_table = lax.dynamic_update_slice(
                head_table, head_sum, (place * each, blk // team, 0)
            )
            parts.append(head_table.reshape(n_head, n_blk, w_rows))
        sums = sum_rows(jnp.concatenate(parts, axis=2), head, blk)
        cuts = [sums[i * w_rows : (i + 1) * w_rows] for i in range(6)]
        up_bias_grad = sums[6 * w_rows : 6 * w_rows + ff_rows]
        rest = sums[6 * w_rows + ff_rows :]

    return (
        output,
        tokens_grad,
        cuts[0],
        cuts[1],
        qkv_grad[0],
        qkv_grad[1],
        qkv_grad[2],
        rest[:w_rows],
        rest[w_rows:],
        out_grad,
        cuts[2],
        cuts[3],
        cuts[4],
        up_grad,
        up_bias_grad,
        down_grad,
        cuts[5],
    )


def solution(mesh):
    by_token = P(("blk", "head"), None)
    matrix = P(("head", "blk"), None)
    vector = P(("head", "blk"))
    return jax.shard_map(
        local,
        mesh=mesh,
        in_specs=(
            by_token,
            P(("blk", "head")),
            by_token,
            vector,
            vector,
            matrix,
            matrix,
            matrix,
            vector,
            vector,
            matrix,
            vector,
            vector,
            vector,
            matrix,
            vector,
            matrix,
            vector,
        ),
        out_specs=(
            by_token,
            by_token,
            vector,
            vector,
            matrix,
            matrix,
            matrix,
            vector,
            vector,
            matrix,
            vector,
            vector,
            vector,
            matrix,
            vector,
            matrix,
            vector,
        ),
        check_vma=False,
    )
```

```python
import functools

import jax
import jax.numpy as jnp
from jax import lax
from jax.experimental import pallas as pl
from jax.experimental.pallas import tpu as pltpu
from jax.sharding import PartitionSpec as P

D = 2048
H = 16
DH = 128

norm_epsilon = 1e-05
masked_fill = -1e30
tile = 256
bf16 = jnp.bfloat16
f32 = jnp.float32
log2_e = 1.4426950408889634
vmem_bytes = 48 * 1024 * 1024


def matmul(left, right):
    return jnp.dot(left, right, preferred_element_type=f32)


def cross_rows(left, right):
    return lax.dot_general(left, right, (((0,), (0,)), ((), ())), preferred_element_type=f32)


def times_transposed(left, right):
    return lax.dot_general(left, right, (((1,), (1,)), ((), ())), preferred_element_type=f32)


def norm_parts(values):
    row_mean = jnp.mean(values, axis=-1, keepdims=True)
    centered = values - row_mean
    row_var = jnp.mean(centered * centered, axis=-1, keepdims=True)
    inverse = lax.rsqrt(row_var + norm_epsilon)
    return (centered * inverse, inverse)


def norm_back(grad_out, normal_hat, inverse, gain):
    scaled_grad = grad_out * gain
    return inverse * (
        scaled_grad
        - jnp.mean(scaled_grad, axis=-1, keepdims=True)
        - normal_hat * jnp.mean(scaled_grad * normal_hat, axis=-1, keepdims=True)
    )


def swap(v, axis, mask):
    size = lax.axis_size(axis)
    return lax.ppermute(v, axis, [(i, i ^ mask) for i in range(size)])


def ring_order(chips):
    return list(range(0, chips, 2)) + [k for k in range(chips - 1, 0, -1) if k % 2]


def next_chip(v):
    chips = lax.axis_size("blk") // 2
    order = ring_order(chips)
    moves = [(order[k], order[(k + 1) % chips]) for k in range(chips)]
    return lax.ppermute(v, "blk", [(2 * a + c, 2 * b + c) for a, b in moves for c in range(2)])


def pick(v, index):
    return lax.dynamic_index_in_dim(v, index, 0, keepdims=False)


def put(v, part, index):
    return lax.dynamic_update_index_in_dim(v, part, index, 0)


def bits_of(size):
    return [1 << k for k in range(size.bit_length() - 1)]


def blank(shape, dtype):
    return pl.pallas_call(
        lambda out: None,
        out_shape=jax.ShapeDtypeStruct(shape, dtype),
        out_specs=pl.BlockSpec(memory_space=pl.ANY),
        name="blank",
    )()


def hold(*values):
    return lax.optimization_barrier(values)


def gather_head(v):
    size = lax.axis_size("head")
    if size == 4:
        half = v.shape[0] // 2
        one, two = swap(v, "head", 1), swap(v, "head", 2)
        low = swap(two[:half], "head", 1)
        high = swap(one[half:], "head", 2)
        return [v, one, two, jnp.concatenate([low, high], axis=0)]
    held = [v]
    for bit in bits_of(size):
        held = held + [swap(part, "head", bit) for part in held]
    return held


def scatter_head(chunk):
    size = lax.axis_size("head")
    if size == 4:
        far = chunk(3).astype(bf16)
        half = far.shape[0] // 2
        low = swap(far[:half], "head", 1)
        high = swap(far[half:], "head", 2)
        one, two = chunk(1), chunk(2)
        one = jnp.concatenate([one[:half], one[half:] + high.astype(f32)], axis=0)
        two = jnp.concatenate([two[:half] + low.astype(f32), two[half:]], axis=0)
        one = swap(one.astype(bf16), "head", 1)
        two = swap(two.astype(bf16), "head", 2)
        return chunk(0) + one.astype(f32) + two.astype(f32)
    terms = [chunk(m) for m in range(size)]
    for bit in reversed(bits_of(size)):
        terms = [
            terms[m] + swap(terms[m | bit].astype(bf16), "head", bit).astype(f32) for m in range(bit)
        ]
    return terms[0]


def exchange(pieces, axis, mine, group):
    out = pieces
    for mask in range(1, group):
        out = put(out, swap(pick(pieces, mine ^ mask), axis, mask), mine ^ mask)
    return out


def scalars(*values):
    return jnp.stack([jnp.asarray(v, jnp.int32) for v in values])


def local_call(kernel, out_shapes, scalar, *arrays, name):
    return pl.pallas_call(
        kernel,
        in_specs=[pl.BlockSpec(memory_space=pltpu.SMEM)]
        + [pl.BlockSpec(memory_space=pltpu.VMEM)] * len(arrays),
        out_specs=[pl.BlockSpec(memory_space=pltpu.VMEM)] * len(out_shapes),
        out_shape=[jax.ShapeDtypeStruct(shape, dtype) for shape, dtype in out_shapes],
        compiler_params=pltpu.CompilerParams(vmem_limit_bytes=vmem_bytes),
        name=name,
    )(scalar, *arrays)


def place(blocks, at):
    count = len(blocks)

    def kernel(at_ref, *refs):
        for k in range(count):
            refs[count][at_ref[k]] = refs[k][...]

    shape = ((count,) + blocks[0].shape, blocks[0].dtype)
    return local_call(kernel, [shape], at, *blocks, name="place")[0]


def lanes(start, size):
    return pl.ds(pl.multiple_of(start, DH), size)


def split_columns(arrays, width, columns_of, core, chips, name):
    rows = arrays[0].shape[0]

    def kernel(core_ref, *refs):
        sources, (mine, other) = refs[:-2], refs[-2:]
        me = core_ref[0]
        for chip in range(chips):
            for out, index in ((mine, me), (other, 1 - me)):
                starts, run = columns_of(2 * chip + index)
                for p, source in enumerate(sources):
                    for i, start in enumerate(starts):
                        low = p * width + i * run
                        out[chip, :, low : low + run] = source[:, lanes(start, run)]

    shape = ((chips, rows, len(arrays) * width), arrays[0].dtype)
    return local_call(kernel, [shape, shape], scalars(core), *arrays, name=name)


def pair_up(mine, other, chip, core):
    chips = mine.shape[0]

    def kernel(at, mine_ref, other_ref, *outs):
        for m in range(chips):
            outs[m][at[1]] = mine_ref[at[0] ^ m]
            outs[m][1 - at[1]] = other_ref[at[0] ^ m]

    shape = ((2,) + mine.shape[1:], mine.dtype)
    return local_call(kernel, [shape] * chips, scalars(chip, core), mine, other, name="pair_up")


def swap_chips(pieces):
    return [pieces[0]] + [swap(pieces[m], "blk", 2 * m) for m in range(1, len(pieces))]


def merge_columns(pieces, count, width, columns_of, chip, name):
    chips = len(pieces)
    rows = pieces[0].shape[1]
    total = 2 * chips * width

    def kernel(at, *refs):
        sources, outs = refs[:chips], refs[chips:]
        for m in range(chips):
            for core in range(2):
                starts, run = columns_of(2 * (at[0] ^ m) + core)
                for p in range(count):
                    for i, start in enumerate(starts):
                        low = p * width + i * run
                        outs[p][:, lanes(start, run)] = sources[m][core, :, low : low + run].astype(
                            f32
                        )

    shapes = [((rows, total), f32)] * count
    return local_call(kernel, shapes, scalars(chip), *pieces, name=name)


def sum_rows(table, head, blk):
    for axis, mine in (("head", head), ("blk", blk)):
        size = table.shape[0]
        for bit in reversed(bits_of(size)):
            halves = table.reshape((2, bit) + table.shape[1:])
            side = (mine // bit) % 2
            table = pick(halves, side) + swap(pick(halves, 1 - side), axis, bit)
        table = table[0]
    return table


def attend_tile(t, groups, factor, refs):
    q_pos, first, query = refs[:3]
    key_pos = refs[3 : 3 + groups]
    keys = refs[3 + groups : 3 + 2 * groups]
    values = refs[3 + 2 * groups : 3 + 3 * groups]
    out, log_total = refs[3 + 3 * groups :]
    high = jnp.full((tile, 1), masked_fill, f32)
    total = jnp.zeros((tile, 1), f32)
    acc = jnp.zeros((tile, DH), f32)
    seen = pl.ds(0, (t + 1) * tile)
    for m in range(groups):
        scores = times_transposed(query[...], keys[m][0, seen, :]) * factor
        pos = key_pos[m][:, seen]
        keep = (pos >= first[...]) & (pos <= q_pos[...])
        scores = jnp.where(keep, scores, masked_fill)
        new_high = jnp.maximum(high, jnp.max(scores, axis=-1, keepdims=True))
        weights = jnp.exp2(scores - new_high)
        shrink = jnp.exp2(high - new_high)
        total = total * shrink + jnp.sum(weights, axis=-1, keepdims=True)
        acc = acc * shrink + matmul(weights.astype(bf16), values[m][0, seen, :])
        high = new_high
    out[...] = (acc / total).astype(bf16)
    log_row = jnp.transpose(jnp.broadcast_to(high + jnp.log2(total), (tile, DH)))
    log_total[0] = log_row[0:1, :]


def attend_kernel(tiles, groups, factor, *refs):
    for t in range(tiles):
        pl.when(pl.program_id(1) == t)(functools.partial(attend_tile, t, groups, factor, refs))


def attend(q_pos, first, key_pos, query, key_values):
    rows, width = query.shape
    groups = len(key_values)
    heads = width // DH
    tiles = rows // tile
    column = pl.BlockSpec((tile, 1), lambda i, t: (t, 0))
    line = pl.BlockSpec((1, rows), lambda i, t: (0, 0))
    some = pl.BlockSpec((tile, DH), lambda i, t: (t, i))
    key = pl.BlockSpec((1, rows, DH), lambda i, t: (0, 0, i))
    value = pl.BlockSpec((1, rows, DH), lambda i, t: (1, 0, i))
    pairs = rows * rows * groups * heads // 2
    return pl.pallas_call(
        functools.partial(attend_kernel, tiles, groups, log2_e * DH**-0.5),
        grid=(heads, tiles),
        in_specs=[column, column, some] + [line] * groups + [key] * groups + [value] * groups,
        out_specs=[some, pl.BlockSpec((1, 1, tile), lambda i, t: (i, 0, t))],
        out_shape=[
            jax.ShapeDtypeStruct((rows, width), bf16),
            jax.ShapeDtypeStruct((heads, 1, rows), f32),
        ],
        compiler_params=pltpu.CompilerParams(vmem_limit_bytes=vmem_bytes),
        cost_estimate=pl.CostEstimate(
            flops=4 * pairs * DH, bytes_accessed=4 * rows * width * groups, transcendentals=pairs
        ),
        name="attend",
    )(q_pos, first, query, *key_pos, *key_values, *key_values)


def row_dots_kernel(left, right, out):
    products = left[...].astype(f32) * right[...].astype(f32)
    out[0] = jnp.sum(jnp.transpose(products), axis=0, keepdims=True)


def row_dots(left, right):
    rows, width = left.shape
    heads = width // DH
    block = pl.BlockSpec((rows, DH), lambda i: (0, i))
    return pl.pallas_call(
        row_dots_kernel,
        grid=(heads,),
        in_specs=[block, block],
        out_specs=pl.BlockSpec((1, 1, rows), lambda i: (i, 0, 0)),
        out_shape=jax.ShapeDtypeStruct((heads, 1, rows), f32),
        compiler_params=pltpu.CompilerParams(vmem_limit_bytes=vmem_bytes),
        name="row_dots",
    )(left, right)


def attend_back_tile(t, factor, scaling, carried, refs):
    q_pos, first, k_pos, log_total, delta, query, d_out, keys, values = refs[:9]
    dq, d_kv = refs[-2:]
    rows = query.shape[0]
    ahead = pl.ds(t * tile, rows - t * tile)
    k_tile, v_tile = keys[0], values[0]
    q_part, d_part = query[ahead, :], d_out[ahead, :]
    scores = times_transposed(k_tile, q_part) * factor
    pos = k_pos[...]
    keep = (pos >= first[:, ahead]) & (pos <= q_pos[:, ahead])
    probs = jnp.where(keep, jnp.exp2(scores - log_total[0, :, ahead]), 0.0)
    d_kv[1] = matmul(probs.astype(bf16), d_part).astype(bf16)
    d_probs = times_transposed(v_tile, d_part)
    d_scores = (probs * (d_probs - delta[0, :, ahead])).astype(bf16)
    d_kv[0] = (scaling * matmul(d_scores, q_part)).astype(bf16)
    term = scaling * cross_rows(d_scores, k_tile)
    if t > 0:
        dq[ahead, :] += term
    elif carried:
        dq[...] = refs[9][...] + term
    else:
        dq[...] = term


def attend_back_kernel(tiles, factor, scaling, carried, *refs):
    for t in range(tiles):
        pl.when(pl.program_id(1) == t)(
            functools.partial(attend_back_tile, t, factor, scaling, carried, refs)
        )


def attend_back(q_pos, first, k_pos, log_total, delta, query, d_out, key_value, dq_in):
    rows, width = query.shape
    heads = width // DH
    tiles = rows // tile
    column = pl.BlockSpec((tile, 1), lambda i, t: (t, 0))
    line = pl.BlockSpec((1, rows), lambda i, t: (0, 0))
    stat = pl.BlockSpec((1, 1, rows), lambda i, t: (i, 0, 0))
    key = pl.BlockSpec((1, tile, DH), lambda i, t: (0, t, i))
    value = pl.BlockSpec((1, tile, DH), lambda i, t: (1, t, i))
    both = pl.BlockSpec((2, tile, DH), lambda i, t: (0, t, i))
    block = pl.BlockSpec((rows, DH), lambda i, t: (0, i))
    pairs = rows * rows * heads // 2
    carried = dq_in is not None
    return pl.pallas_call(
        functools.partial(attend_back_kernel, tiles, log2_e * DH**-0.5, DH**-0.5, carried),
        grid=(heads, tiles),
        in_specs=[line, line, column, stat, stat, block, block, key, value]
        + [block] * (1 if carried else 0),
        out_specs=[block, both],
        out_shape=[
            jax.ShapeDtypeStruct((rows, width), f32),
            jax.ShapeDtypeStruct((2, rows, width), bf16),
        ],
        compiler_params=pltpu.CompilerParams(vmem_limit_bytes=vmem_bytes),
        cost_estimate=pl.CostEstimate(
            flops=10 * pairs * DH, bytes_accessed=20 * rows * width, transcendentals=pairs
        ),
        name="attend_back",
    )(
        q_pos,
        first,
        k_pos,
        log_total,
        delta,
        query,
        d_out,
        key_value,
        key_value,
        *([dq_in] if carried else []),
    )


def local(
    tokens,
    segments,
    cotangent,
    first_gain,
    first_shift,
    query_proj,
    key_proj,
    value_proj,
    query_bias,
    value_bias,
    out_proj,
    out_bias,
    second_gain,
    second_shift,
    up_proj,
    up_bias,
    down_proj,
    down_bias,
):
    n_head, n_blk = lax.axis_size("head"), lax.axis_size("blk")
    head, blk = lax.axis_index("head"), lax.axis_index("blk")
    chips = n_blk // 2
    chip, core = blk // 2, blk % 2
    tok = tokens.shape[0]
    rows = tok * n_blk
    w_rows = query_proj.shape[0]
    ff_rows = down_proj.shape[0]
    team = DH // w_rows
    sets = n_blk // team
    each = n_head // team
    place_in = blk % team
    own_heads = each * DH

    ring = ring_order(chips)
    behind = jnp.array(
        [[ring[(ring.index(z) - k) % chips] for k in range(chips)] for z in range(chips)], jnp.int32
    )
    behind = pick(behind, chip)
    behind = [behind[k] for k in range(chips)]

    def chunk_of(array, step):
        return array[step * 2 * tok : (step + 1) * 2 * tok]

    def place_of(step, other):
        return (2 * behind[step] + (core ^ other)) * tok

    def ordered_chunk(array, step):
        return jnp.concatenate(
            [lax.dynamic_slice_in_dim(array, place_of(step, other), tok, 0) for other in (0, 1)]
        )

    def fill(buffer, chunk, step):
        return lax.dynamic_update_slice_in_dim(buffer, chunk, step * 2 * tok, 0)

    def fill_pair(buffer, mine, other, step):
        buffer = lax.dynamic_update_slice_in_dim(buffer, mine, step * 2 * tok, 0)
        return lax.dynamic_update_slice_in_dim(buffer, other, step * 2 * tok + tok, 0)

    order = jnp.arange(rows, dtype=jnp.int32)

    def positions(of_head):
        return ((order // tok * n_head + of_head) * tok + order % tok).astype(f32)

    square = n_head == 4

    def head_columns(b):
        at = (b % team) * each
        return [((at + i) * sets + b // team) * DH for i in range(each)], DH

    def ff_columns(b):
        return [(h * n_blk + b) * ff_rows for h in range(n_head)], ff_rows

    heads_at = scalars(*[head ^ m for m in range(n_head)])
    chips_at = scalars(*[chip ^ m for m in range(chips)])

    with jax.named_scope("tokens_gather"):
        tok_mine, tok_other = [tokens], []
        tok_mine.append(next_chip(tokens))

    with jax.named_scope("vectors"):
        small = [
            first_gain,
            first_shift,
            query_bias,
            value_bias,
            out_bias,
            second_gain,
            second_shift,
            down_bias,
            up_bias,
            segments.astype(bf16),
        ]
        small = jnp.concatenate(small)[None]
        for bit in bits_of(n_head):
            small = jnp.concatenate([small, swap(small, "head", bit)])
        small = jnp.concatenate([small, swap(small, "blk", 1)])
        small_parts = [small]
        small_parts.append(next_chip(small))

    with jax.named_scope("qkv_weights"):
        mine, other = split_columns(
            [query_proj, key_proj, value_proj], own_heads, head_columns, core, chips, "split_heads"
        )
        pieces = pair_up(mine, swap(other, "blk", 1), chip, core)

    pieces, small_parts, up_proj, tokens = hold(pieces, small_parts, up_proj, tokens)

    with jax.named_scope("qkv_weights"):
        pieces = swap_chips(pieces)
        fused = place(pieces, chips_at).reshape(n_blk * w_rows, 3 * own_heads)
    with jax.named_scope("tokens_gather"):
        tok_other.append(swap(tokens, "blk", 1))
    with jax.named_scope("vectors"):
        if len(small_parts) < chips:
            small_parts.append(next_chip(small_parts[-1]))

    fused, small_parts, tok_mine, tok_other, up_proj = hold(
        fused, small_parts, tok_mine, tok_other, up_proj
    )

    normed = blank((rows, D), bf16)
    stats = {}
    table = None

    def small_table():
        width = small_parts[0].shape[1]
        source = jnp.concatenate(small_parts)
        index = jnp.arange(n_head * n_blk, dtype=jnp.int32)
        from_chip = jnp.repeat(jnp.stack(behind), 2 * n_head)
        from_core = core ^ (index // n_head % 2)
        from_row = (head ^ (index % n_head)) * n_blk + 2 * from_chip + from_core
        select = (from_row[None, :] == index[:, None]).astype(bf16)
        return matmul(select, source).reshape(n_head, n_blk, width)

    def vector(index):
        return table[:, :, index * w_rows : (index + 1) * w_rows].reshape(D)

    def add_normed(buffer, step):
        for other, piece in enumerate((tok_mine[step], tok_other[step])):
            values = piece.astype(f32)
            row_mean = jnp.mean(values, axis=-1, keepdims=True)
            centered = values - row_mean
            inverse = lax.rsqrt(jnp.mean(centered * centered, axis=-1, keepdims=True) + norm_epsilon)
            stats[step, other] = (row_mean, inverse)
            out = (centered * inverse * gain_first + shift_first).astype(bf16)
            buffer = lax.dynamic_update_slice_in_dim(buffer, out, place_of(step, other), 0)
        return buffer

    filled = 0
    for step in range(1, chips):
        with jax.named_scope("tokens_gather"):
            if step < chips - 1:
                tok_mine.append(next_chip(tok_mine[step]))
            if step < chips - 1:
                tok_other.append(swap(tok_mine[step], "blk", 1))
        with jax.named_scope("qkv_weights"):
            if step == 1 and square:
                fused_parts = [fused, swap(fused, "head", 1), swap(fused, "head", 2)]
            if step == 2 and square:
                half = fused.shape[0] // 2
                low = swap(fused_parts[2][:half], "head", 1)
                high = swap(fused_parts[1][half:], "head", 2)
            if step == 1 and not square:
                fused_parts = gather_head(fused)
        with jax.named_scope("vectors"):
            if table is not None and filled == 0:
                gain_first, shift_first = vector(0), vector(1)
            if len(small_parts) < chips:
                small_parts.append(next_chip(small_parts[-1]))
            elif table is None:
                table = small_table()
                gain_first, shift_first = vector(0), vector(1)
        if table is not None and step < chips - 1:
            with jax.named_scope("qkv"):
                while filled < min(step, filled + 2):
                    normed = add_normed(normed, filled)
                    filled += 1
        if step == 1:
            with jax.named_scope("up_weights"):
                up_mine, up_other = split_columns(
                    [up_proj], n_head * ff_rows, ff_columns, core, chips, "split_up"
                )
        if step < chips - 1:
            tok_mine, tok_other, small_parts, normed, stats, table, up_mine, up_other = hold(
                tok_mine, tok_other, small_parts, normed, stats, table, up_mine, up_other
            )
            if step == 2 and square:
                fused_parts, low, high = hold(fused_parts, low, high)
        if step == chips - 2:
            (fused_parts, tok_mine, tok_other, normed, stats, cotangent, up_other, table) = hold(
                fused_parts, tok_mine, tok_other, normed, stats, cotangent, up_other, table
            )
            if square and step == 2:
                low, high, cotangent, out_proj = hold(low, high, cotangent, out_proj)

    with jax.named_scope("tokens_gather"):
        tok_other.append(swap(tok_mine[chips - 1], "blk", 1))
    with jax.named_scope("vectors"):

        def own_head_part(full):
            part = full.reshape(n_head, sets, DH)
            part = lax.dynamic_index_in_dim(part, blk // team, 1, keepdims=False)
            return lax.dynamic_slice_in_dim(part, place_in * each, each, 0).reshape(own_heads)

        q_bias, v_bias = own_head_part(vector(2)), own_head_part(vector(3))
        qkv_bias = jnp.concatenate([q_bias, jnp.zeros_like(q_bias), v_bias])
    with jax.named_scope("dy_gather"):
        dy_mine, dy_other = [cotangent], []
        dy_mine.append(next_chip(cotangent))
    with jax.named_scope("up_weights"):
        up_pieces = pair_up(up_mine, swap(up_other, "blk", 1), chip, core)
    with jax.named_scope("out_weights"):
        if square:
            out_parts = [out_proj, swap(out_proj, "head", 1), swap(out_proj, "head", 2)]
        else:
            out_parts = gather_head(out_proj)
    with jax.named_scope("qkv"):
        if square:
            half = fused.shape[0] // 2
            fused_parts = [part.reshape(2, half, -1) for part in fused_parts]
            blocks = [part[k] for part in fused_parts for k in (0, 1)] + [low, high]
            qkv_w = place(blocks, jnp.stack([2 * heads_at, 2 * heads_at + 1], axis=1).reshape(-1))
        else:
            qkv_w = place(fused_parts, heads_at)
        qkv_w = qkv_w.reshape(D, 3 * own_heads)
        while filled < chips:
            normed = add_normed(normed, filled)
            filled += 1
        qkv = (matmul(normed, qkv_w) + qkv_bias).astype(bf16)
        query = qkv[:, :own_heads]
        kv = jnp.stack([qkv[:, own_heads : 2 * own_heads], qkv[:, 2 * own_heads :]])

    query, kv, up_pieces, normed, stats, out_parts, cotangent, dy_mine, down_proj, qkv_w = hold(
        query, kv, up_pieces, normed, stats, out_parts, cotangent, dy_mine, down_proj, qkv_w
    )

    with jax.named_scope("kv_gather"):
        if square:
            kv_parts = [kv, swap(kv, "head", 1), swap(kv, "head", 2)]
        else:
            kv_parts = gather_head(kv)
    with jax.named_scope("up_weights"):
        up_pieces = swap_chips(up_pieces)
        up_part = place(up_pieces, chips_at).reshape(n_blk * w_rows, n_head * ff_rows)
    with jax.named_scope("vectors"):
        o_bias, gain_second, shift_second, d_bias = vector(4), vector(5), vector(6), vector(7)
        base = 8 * w_rows
        u_bias = table[:, :, base : base + ff_rows]
        u_bias = lax.dynamic_index_in_dim(u_bias, blk, 1, keepdims=False).reshape(-1)
        seq = table[:, :, base + ff_rows :]
        seg_all = seq.transpose(1, 0, 2).reshape(-1)
        seg_rows = pick(seq, head).reshape(rows)
        first_pos = jnp.sum((seg_all[None, :] < seg_rows[:, None]).astype(f32), axis=1)
        q_pos = positions(head)
        k_pos = [positions(head ^ m) for m in range(n_head)]
        vectors = (o_bias, gain_second, shift_second, d_bias, u_bias)
        as_column = lambda v: v[:, None]
        as_line = lambda v: v[None, :]
        spots = (
            as_column(q_pos),
            as_column(first_pos),
            as_line(q_pos),
            as_line(first_pos),
            [as_line(pos) for pos in k_pos],
            [as_column(pos) for pos in k_pos],
        )
    kv_parts, up_part, dy_mine, vectors, spots = hold(kv_parts, up_part, dy_mine, vectors, spots)
    o_bias, gain_second, shift_second, d_bias, u_bias = vectors

    dy_all = blank((rows, D), bf16)
    with jax.named_scope("kv_gather"):
        if square:
            low = swap(kv_parts[2][0], "head", 1)
            high = swap(kv_parts[1][1], "head", 2)
            kv_parts = kv_parts + [jnp.stack([low, high])]
    with jax.named_scope("out_weights"):
        if square:
            half = w_rows // 2
            low = swap(out_parts[2][:half], "head", 1)
            high = swap(out_parts[1][half:], "head", 2)
            out_parts = out_parts + [jnp.concatenate([low, high])]
    with jax.named_scope("dy_gather"):
        if chips > 2:
            dy_mine.append(next_chip(dy_mine[1]))
    kv_parts, dy_mine, up_part, out_parts, down_proj, cotangent = hold(
        kv_parts, dy_mine, up_part, out_parts, down_proj, cotangent
    )

    with jax.named_scope("up_weights"):
        up_w = lax.all_gather(up_part, "head", axis=0, tiled=True)
    with jax.named_scope("down_weights"):
        if square:
            down_parts = [down_proj, swap(down_proj, "head", 1), swap(down_proj, "head", 2)]
        else:
            down_parts = gather_head(down_proj)
    with jax.named_scope("dy_gather"):
        dy_other.append(swap(cotangent, "blk", 1))
        for step in range(2, chips - 1):
            dy_mine.append(next_chip(dy_mine[step]))
    with jax.named_scope("out_weights"):
        out_w = place(out_parts, heads_at).reshape(team, each, w_rows, D)
        out_w = exchange(out_w, "blk", place_in, team)
        out_w = out_w.transpose(1, 0, 2, 3).reshape(own_heads, D)
    with jax.named_scope("attention"):
        mixed, log_total = attend(spots[0], spots[1], spots[4], query, kv_parts)
    mixed, dy_mine, dy_other, out_w = hold(mixed, dy_mine, dy_other, out_w)

    def cross(term):
        return (term[0], swap(term[1], "blk", 1))

    def sum_of(pair):
        return pair[0].astype(f32) + pair[1].astype(f32)

    def onward(ready, moving):
        total = ready if moving is None else ready + moving.astype(f32)
        return next_chip(total.astype(bf16))

    with jax.named_scope("branch"):

        def branch_term(step):
            return [
                matmul(lax.dynamic_slice_in_dim(mixed, place_of(step, other), tok, 0), out_w).astype(bf16)
                for other in (0, 1)
            ]

        ready = sum_of(cross(branch_term(1)))
        term = branch_term(2 % chips)
        ready, term, dy_mine, dy_other = hold(ready, term, dy_mine, dy_other)
        moving = None
        for step in range(1, chips):
            moving = onward(ready, moving)
            ready = sum_of(cross(term))
            if step < chips - 1:
                term = branch_term((step + 2) % chips)
            with jax.named_scope("dy_gather"):
                if step == 1:
                    dy_all = fill_pair(dy_all, dy_mine[0], dy_other[0], 0)
                if step < chips - 1:
                    dy_other.append(swap(dy_mine[step], "blk", 1))
                    if step > 1:
                        dy_all = fill_pair(dy_all, dy_mine[step - 1], dy_other[step - 1], step - 1)
                else:
                    dy_all = fill_pair(dy_all, dy_mine[step - 1], dy_other[step - 1], step - 1)
            with jax.named_scope("down_weights"):
                if square and step == 3:
                    half = ff_rows // 2
                    low = swap(down_parts[2][:half], "head", 1)
                    high = swap(down_parts[1][half:], "head", 2)
                    down_parts = [part.reshape(2, half, D) for part in down_parts]
                    blocks = [part[k] for part in down_parts for k in (0, 1)] + [low, high]
                    at = jnp.stack([2 * heads_at, 2 * heads_at + 1], axis=1).reshape(-1)
                    down_w = place(blocks, at).reshape(n_head * ff_rows, D)
                if not square and step == 1:
                    down_w = place(down_parts, heads_at).reshape(n_head * ff_rows, D)
            if square and step == 2:
                down_parts, moving, ready, term, dy_mine, dy_other, dy_all = hold(
                    down_parts, moving, ready, term, dy_mine, dy_other, dy_all
                )
            else:
                moving, ready, term, dy_mine, dy_other, dy_all = hold(
                    moving, ready, term, dy_mine, dy_other, dy_all
                )
        with jax.named_scope("dy_gather"):
            dy_other.append(swap(dy_mine[chips - 1], "blk", 1))
            dy_all = fill_pair(dy_all, dy_mine[chips - 1], dy_other[chips - 1], chips - 1)
        own = tokens.astype(f32)
        hidden = own + (ready + moving.astype(f32) + o_bias)
        hat_second, inv_second = norm_parts(hidden)
        second_own = (hat_second * gain_second + shift_second).astype(bf16)
    hidden, second_own, inv_second = hold(hidden, second_own, inv_second)

    with jax.named_scope("mlp"):
        second_all = blank((rows, D), bf16)
        active_all = blank((rows, n_head * ff_rows), bf16)
        d_upper_all = blank((rows, n_head * ff_rows), bf16)
        sec_mine, sec_other = [second_own], []
        terms = {}

        def mlp_chunk(step, second_all, active_all, d_upper_all):
            second_all = fill_pair(second_all, sec_mine[step], sec_other[step], step)
            upper = matmul(chunk_of(second_all, step), up_w) + u_bias
            phi = 0.5 * (1.0 + lax.erf(upper * 0.7071067811865476))
            active = (upper * phi).astype(bf16)
            slope = phi + upper * jnp.exp(-0.5 * upper * upper) * 0.3989422804014327
            d_active = times_transposed(chunk_of(dy_all, step), down_w)
            d_upper = (d_active * slope).astype(bf16)
            terms[step] = [
                times_transposed(d_upper[:tok], up_w).astype(bf16),
                times_transposed(d_upper[tok:], up_w).astype(bf16),
            ]
            return second_all, fill(active_all, active, step), fill(d_upper_all, d_upper, step)

        for step in range(chips):
            if step < chips - 1:
                sec_mine.append(next_chip(sec_mine[step]))
            if step > 0:
                second_all, active_all, d_upper_all = mlp_chunk(
                    step - 1, second_all, active_all, d_upper_all
                )
                if step == chips - 1:
                    ready = sum_of(cross(terms[1]))
            sec_other.append(swap(sec_mine[step], "blk", 1))
            ready, sec_mine, sec_other, terms, second_all, active_all, d_upper_all = hold(
                ready, sec_mine, sec_other, terms, second_all, active_all, d_upper_all
            )
        moving = None
        for step in range(1, chips):
            moving = onward(ready, moving)
            if step == 1:
                second_all, active_all, d_upper_all = mlp_chunk(
                    chips - 1, second_all, active_all, d_upper_all
                )
            ready = sum_of(cross(terms[(step + 1) % chips]))
            if step == 2:
                with jax.named_scope("up_grad"):
                    up_term = cross_rows(second_all, d_upper_all).astype(bf16)
                moving, ready, terms, second_all, active_all, d_upper_all, up_term = hold(
                    moving, ready, terms, second_all, active_all, d_upper_all, up_term
                )
            elif step == 3:
                with jax.named_scope("down_grad"):
                    down_term = cross_rows(active_all, dy_all).astype(bf16)
                moving, ready, terms, down_term = hold(moving, ready, terms, down_term)
            else:
                moving, ready, terms, second_all, active_all, d_upper_all = hold(
                    moving, ready, terms, second_all, active_all, d_upper_all
                )
        d_second = ready + moving.astype(f32)
        upstream = cotangent.astype(f32)
        d_hidden = upstream + norm_back(d_second, hat_second, inv_second, gain_second)
        d_branch_own = d_hidden.astype(bf16)

    def sum_heads(terms):
        return lax.psum_scatter(terms, "head", scatter_dimension=0, tiled=True)

    with jax.named_scope("up_grad"):
        up_sum = sum_heads(up_term)
    d_hidden, d_branch_own, active_all, d_second = hold(
        d_hidden, d_branch_own, active_all, d_second
    )

    with jax.named_scope("d_branch_gather"):
        d_branch = blank((rows, D), bf16)
        mine, other = [d_branch_own], []

        def fill_ordered(buffer, step):
            buffer = lax.dynamic_update_slice_in_dim(buffer, mine[step], place_of(step, 0), 0)
            return lax.dynamic_update_slice_in_dim(buffer, other[step], place_of(step, 1), 0)

        for step in range(chips):
            if step < chips - 1:
                mine.append(next_chip(mine[step]))
            if step > 0:
                d_branch = fill_ordered(d_branch, step - 1)
            other.append(swap(mine[step], "blk", 1))
            if step == 1:
                with jax.named_scope("output"):
                    outs = [
                        [
                            matmul(chunk_of(active_all, k)[:tok], down_w).astype(bf16),
                            matmul(chunk_of(active_all, k)[tok:], down_w).astype(bf16),
                        ]
                        for k in range(chips)
                    ]
                mine, other, d_branch, outs = hold(mine, other, d_branch, outs)
            else:
                mine, other, d_branch = hold(mine, other, d_branch)
        d_branch = fill_ordered(d_branch, chips - 1)
        d_mixed = times_transposed(d_branch, out_w).astype(bf16)
        delta = row_dots(d_mixed, mixed)
    d_mixed, delta, d_branch, up_sum, down_term, mixed = hold(
        d_mixed, delta, d_branch, up_sum, down_term, mixed
    )
    with jax.named_scope("down_grad"):
        down_grad = sum_heads(down_term)

    dq = None

    def kv_grad(m):
        return attend_back(
            spots[2],
            spots[3],
            spots[5][m],
            log_total,
            delta,
            query,
            d_mixed,
            kv_parts[m],
            dq,
        )

    d_kv = {}
    moving = None
    with jax.named_scope("output"):
        ready = sum_of(cross(outs[1]))

    def output_step(step, ready, moving):
        return sum_of(cross(outs[(step + 1) % chips])), onward(ready, moving)

    out_step = 1
    for m in reversed(range(n_head)):
        with jax.named_scope("attention_back"):
            if square and m == 2:
                low = swap(d_kv[3][0], "head", 1)
                high = swap(d_kv[3][1], "head", 2)
            if square and m == 0:
                one = jnp.stack(
                    [d_kv[1][0], (d_kv[1][1].astype(f32) + high.astype(f32)).astype(bf16)]
                )
                two = jnp.stack(
                    [(d_kv[2][0].astype(f32) + low.astype(f32)).astype(bf16), d_kv[2][1]]
                )
                one, two = swap(one, "head", 1), swap(two, "head", 2)
            dq, d_kv[m] = kv_grad(m)
        if m % 2 == 0 and out_step < chips:
            with jax.named_scope("output"):
                ready, moving = output_step(out_step, ready, moving)
                out_step += 1
        if m == 1:
            with jax.named_scope("out_grad"):
                out_term = cross_rows(mixed, d_branch).astype(bf16)
                out_term = out_term.reshape(each, team, w_rows, D).transpose(1, 0, 2, 3)
                out_term = exchange(out_term, "blk", place_in, team)
        if square and m == 1:
            low, high, dq, d_kv, d_mixed, ready, moving, out_term = hold(
                low, high, dq, d_kv, d_mixed, ready, moving, out_term
            )
        elif m > 0:
            dq, d_kv, d_mixed = hold(dq, d_kv, d_mixed)
    with jax.named_scope("up_grad"):
        up_sum = up_sum.reshape(chips, 2, w_rows, n_head * ff_rows)
        up_mine = lax.dynamic_index_in_dim(up_sum, core, 1, keepdims=False)
        up_other = lax.dynamic_index_in_dim(up_sum, 1 - core, 1, keepdims=False)
        up_pieces = pair_up(up_mine, swap(up_other, "blk", 1), chip, core)
    with jax.named_scope("output"):
        while out_step < chips:
            ready, moving = output_step(out_step, ready, moving)
            out_step += 1
    with jax.named_scope("attention_back"):
        if square:
            d_kv = (d_kv[0].astype(f32) + one.astype(f32) + two.astype(f32)).astype(bf16)
        else:
            d_kv = scatter_head(lambda m: d_kv[m].astype(f32)).astype(bf16)
        d_qkv = jnp.concatenate([dq.astype(bf16), d_kv[0], d_kv[1]], axis=1)
    d_qkv, ready, moving, up_pieces, out_term, down_grad = hold(
        d_qkv, ready, moving, up_pieces, out_term, down_grad
    )
    with jax.named_scope("out_grad"):
        out_grad = sum_heads(out_term.reshape(n_head * w_rows, D))

    first_sums = []

    def normed_term(step):
        halves = []
        for other, piece in enumerate((tok_mine[step], tok_other[step])):
            part = lax.dynamic_slice_in_dim(d_qkv, place_of(step, other), tok, 0)
            term = times_transposed(part, qkv_w)
            row_mean, inverse = stats[step, other]
            hat = (piece.astype(f32) - row_mean) * inverse
            first_sums.append((jnp.sum(term * hat, axis=0), jnp.sum(term, axis=0)))
            halves.append(term.astype(bf16))
        return halves

    slab = n_blk * w_rows
    with jax.named_scope("d_normed"):
        term = normed_term(1)
    (term,) = hold(term)
    with jax.named_scope("d_normed"):
        ready_normed = sum_of(cross(term))
    with jax.named_scope("qkv_grad"):
        if square:
            qkv_term = cross_rows(normed, d_qkv).astype(bf16).reshape(n_head, slab, 3 * own_heads)
            far = pick(qkv_term, head ^ 3)
        else:
            far = qkv_term = d_qkv
    with jax.named_scope("output"):
        output = (hidden + (ready + moving.astype(f32) + d_bias)).astype(bf16)
    ready, qkv_term, far, output = hold(ready_normed, qkv_term, far, output)
    with jax.named_scope("d_normed"):
        term = normed_term(2 % chips)
    moving = None
    for step in range(1, chips):
        with jax.named_scope("d_normed"):
            moving = onward(ready, moving)
            ready = sum_of(cross(term))
            if step < chips - 1:
                term = normed_term((step + 2) % chips)
        with jax.named_scope("qkv_grad"):
            if square and step == 1:
                low = swap(far[: slab // 2], "head", 1)
                high = swap(far[slab // 2 :], "head", 2)
                one, two = pick(qkv_term, head ^ 1), pick(qkv_term, head ^ 2)
            if square and step == 2:
                one = jnp.concatenate([one[: slab // 2], one[slab // 2 :] + high])
                two = jnp.concatenate([two[: slab // 2] + low, two[slab // 2 :]])
                one, two = swap(one, "head", 1), swap(two, "head", 2)
        if step == 2:
            with jax.named_scope("down_grad"):
                down_grad = down_grad.astype(f32)
        if square and step == 1:
            ready, term, moving, low, high, one, two, first_sums = hold(
                ready, term, moving, low, high, one, two, first_sums
            )
        elif step == 2:
            ready, term, moving, first_sums, down_grad = hold(
                ready, term, moving, first_sums, down_grad
            )
        else:
            ready, term, moving, first_sums = hold(ready, term, moving, first_sums)
    with jax.named_scope("up_grad"):
        up_pieces = swap_chips(up_pieces)
        (up_grad,) = merge_columns(
            up_pieces, 1, n_head * ff_rows, ff_columns, chip, "merge_up"
        )
    with jax.named_scope("d_normed"):
        d_normed = ready + moving.astype(f32)
        hat_first, inv_first = norm_parts(own)
        tokens_grad = (d_hidden + norm_back(d_normed, hat_first, inv_first, gain_first)).astype(bf16)

    with jax.named_scope("qkv_grad"):
        if square:
            qkv_grad = pick(qkv_term, head).astype(f32) + one.astype(f32) + two.astype(f32)
        else:
            qkv_grad = scatter_head(
                lambda m: cross_rows(
                    lax.dynamic_slice_in_dim(normed, (head ^ m) * slab, slab, 1), d_qkv
                )
            )
        qkv_grad = qkv_grad.astype(bf16).reshape(chips, 2, w_rows, 3 * own_heads)
        qkv_mine = lax.dynamic_index_in_dim(qkv_grad, core, 1, keepdims=False)
        qkv_other = lax.dynamic_index_in_dim(qkv_grad, 1 - core, 1, keepdims=False)
        pieces = swap_chips(pair_up(qkv_mine, swap(qkv_other, "blk", 1), chip, core))
        qkv_grad = merge_columns(pieces, 3, own_heads, head_columns, chip, "merge_heads")

    with jax.named_scope("vector_grads"):
        full = [
            sum(pair[0] for pair in first_sums),
            sum(pair[1] for pair in first_sums),
            jnp.sum(d_branch_own.astype(f32), axis=0),
            jnp.sum(d_second * hat_second, axis=0),
            jnp.sum(d_second, axis=0),
            jnp.sum(upstream, axis=0),
        ]
        parts = [v.reshape(n_head, n_blk, w_rows) for v in full]
        up_row = jnp.sum(d_upper_all.astype(f32), axis=0)
        up_table = jnp.zeros((n_blk, n_head, ff_rows), f32)
        up_table = put(up_table, up_row.reshape(n_head, ff_rows), blk)
        parts.append(up_table.transpose(1, 0, 2))
        for v in (dq.astype(bf16), d_kv[1]):
            bias_sum = jnp.sum(v.astype(f32), axis=0).reshape(each, 1, DH)
            head_table = jnp.zeros((n_head, sets, DH), f32)
            head_table = lax.dynamic_update_slice(
                head_table, bias_sum, (place_in * each, blk // team, 0)
            )
            parts.append(head_table.reshape(n_head, n_blk, w_rows))
        sums = sum_rows(jnp.concatenate(parts, axis=2), head, blk)
        cuts = [sums[i * w_rows : (i + 1) * w_rows] for i in range(6)]
        up_bias_grad = sums[6 * w_rows : 6 * w_rows + ff_rows]
        rest = sums[6 * w_rows + ff_rows :]

    return (
        output,
        tokens_grad,
        cuts[0],
        cuts[1],
        qkv_grad[0],
        qkv_grad[1],
        qkv_grad[2],
        rest[:w_rows],
        rest[w_rows:],
        out_grad.astype(f32),
        cuts[2],
        cuts[3],
        cuts[4],
        up_grad,
        up_bias_grad,
        down_grad.astype(f32),
        cuts[5],
    )


def solution(mesh):
    by_token = P(("blk", "head"), None)
    matrix = P(("head", "blk"), None)
    vector = P(("head", "blk"))
    return jax.shard_map(
        local,
        mesh=mesh,
        in_specs=(
            by_token,
            P(("blk", "head")),
            by_token,
            vector,
            vector,
            matrix,
            matrix,
            matrix,
            vector,
            vector,
            matrix,
            vector,
            vector,
            vector,
            matrix,
            vector,
            matrix,
            vector,
        ),
        out_specs=(
            by_token,
            by_token,
            vector,
            vector,
            matrix,
            matrix,
            matrix,
            vector,
            vector,
            matrix,
            vector,
            vector,
            vector,
            matrix,
            vector,
            matrix,
            vector,
        ),
        check_vma=False,
    )
```

```python
import functools

import jax
import jax.numpy as jnp
from jax import lax
from jax.experimental import pallas as pl
from jax.experimental.pallas import tpu as pltpu
from jax.sharding import PartitionSpec as P

D = 2048
H = 16
DH = 128

norm_epsilon = 1e-05
masked_fill = -1e30
tile = 256
bf16 = jnp.bfloat16
f32 = jnp.float32
log2_e = 1.4426950408889634
vmem_bytes = 48 * 1024 * 1024


def matmul(left, right):
    return jnp.dot(left, right, preferred_element_type=f32)


def cross_rows(left, right):
    return lax.dot_general(left, right, (((0,), (0,)), ((), ())), preferred_element_type=f32)


def times_transposed(left, right):
    return lax.dot_general(left, right, (((1,), (1,)), ((), ())), preferred_element_type=f32)


def norm_parts(values):
    row_mean = jnp.mean(values, axis=-1, keepdims=True)
    centered = values - row_mean
    row_var = jnp.mean(centered * centered, axis=-1, keepdims=True)
    inverse = lax.rsqrt(row_var + norm_epsilon)
    return (centered * inverse, inverse)


def norm_back(grad_out, normal_hat, inverse, gain):
    scaled_grad = grad_out * gain
    return inverse * (
        scaled_grad
        - jnp.mean(scaled_grad, axis=-1, keepdims=True)
        - normal_hat * jnp.mean(scaled_grad * normal_hat, axis=-1, keepdims=True)
    )


def swap(v, axis, mask):
    size = lax.axis_size(axis)
    return lax.ppermute(v, axis, [(i, i ^ mask) for i in range(size)])


def ring_order(chips):
    return list(range(0, chips, 2)) + [k for k in range(chips - 1, 0, -1) if k % 2]


def next_chip(v):
    chips = lax.axis_size("blk") // 2
    order = ring_order(chips)
    moves = [(order[k], order[(k + 1) % chips]) for k in range(chips)]
    return lax.ppermute(v, "blk", [(2 * a + c, 2 * b + c) for a, b in moves for c in range(2)])


def pick(v, index):
    return lax.dynamic_index_in_dim(v, index, 0, keepdims=False)


def put(v, part, index):
    return lax.dynamic_update_index_in_dim(v, part, index, 0)


def bits_of(size):
    return [1 << k for k in range(size.bit_length() - 1)]


def blank(shape, dtype):
    return pl.pallas_call(
        lambda out: None,
        out_shape=jax.ShapeDtypeStruct(shape, dtype),
        out_specs=pl.BlockSpec(memory_space=pl.ANY),
        name="blank",
    )()


def hold(*values):
    return lax.optimization_barrier(values)


def gather_head(v):
    size = lax.axis_size("head")
    if size == 4:
        half = v.shape[0] // 2
        one, two = swap(v, "head", 1), swap(v, "head", 2)
        low = swap(two[:half], "head", 1)
        high = swap(one[half:], "head", 2)
        return [v, one, two, jnp.concatenate([low, high], axis=0)]
    held = [v]
    for bit in bits_of(size):
        held = held + [swap(part, "head", bit) for part in held]
    return held


def scatter_head(chunk):
    size = lax.axis_size("head")
    if size == 4:
        far = chunk(3).astype(bf16)
        half = far.shape[0] // 2
        low = swap(far[:half], "head", 1)
        high = swap(far[half:], "head", 2)
        one, two = chunk(1), chunk(2)
        one = jnp.concatenate([one[:half], one[half:] + high.astype(f32)], axis=0)
        two = jnp.concatenate([two[:half] + low.astype(f32), two[half:]], axis=0)
        one = swap(one.astype(bf16), "head", 1)
        two = swap(two.astype(bf16), "head", 2)
        return chunk(0) + one.astype(f32) + two.astype(f32)
    terms = [chunk(m) for m in range(size)]
    for bit in reversed(bits_of(size)):
        terms = [
            terms[m] + swap(terms[m | bit].astype(bf16), "head", bit).astype(f32) for m in range(bit)
        ]
    return terms[0]


def exchange(pieces, axis, mine, group):
    out = pieces
    for mask in range(1, group):
        out = put(out, swap(pick(pieces, mine ^ mask), axis, mask), mine ^ mask)
    return out


def scalars(*values):
    return jnp.stack([jnp.asarray(v, jnp.int32) for v in values])


def local_call(kernel, out_shapes, scalar, *arrays, name):
    return pl.pallas_call(
        kernel,
        in_specs=[pl.BlockSpec(memory_space=pltpu.SMEM)]
        + [pl.BlockSpec(memory_space=pltpu.VMEM)] * len(arrays),
        out_specs=[pl.BlockSpec(memory_space=pltpu.VMEM)] * len(out_shapes),
        out_shape=[jax.ShapeDtypeStruct(shape, dtype) for shape, dtype in out_shapes],
        compiler_params=pltpu.CompilerParams(vmem_limit_bytes=vmem_bytes),
        name=name,
    )(scalar, *arrays)


def place(blocks, at):
    count = len(blocks)

    def kernel(at_ref, *refs):
        for k in range(count):
            refs[count][at_ref[k]] = refs[k][...]

    shape = ((count,) + blocks[0].shape, blocks[0].dtype)
    return local_call(kernel, [shape], at, *blocks, name="place")[0]


def place_cores(pieces, at):
    count = len(pieces)

    def kernel(at_ref, *refs):
        for k in range(count):
            for c in range(2):
                refs[count + c][at_ref[k]] = refs[k][c]

    shape = ((count,) + pieces[0].shape[1:], pieces[0].dtype)
    return local_call(kernel, [shape, shape], at, *pieces, name="place_cores")


def lanes(start, size):
    return pl.ds(pl.multiple_of(start, DH), size)


def split_columns(arrays, width, columns_of, core, chips, name):
    rows = arrays[0].shape[0]

    def kernel(core_ref, *refs):
        sources, (mine, other) = refs[:-2], refs[-2:]
        me = core_ref[0]
        for chip in range(chips):
            for out, index in ((mine, me), (other, 1 - me)):
                starts, run = columns_of(2 * chip + index)
                for p, source in enumerate(sources):
                    for i, start in enumerate(starts):
                        low = p * width + i * run
                        out[chip, :, low : low + run] = source[:, lanes(start, run)]

    shape = ((chips, rows, len(arrays) * width), arrays[0].dtype)
    return local_call(kernel, [shape, shape], scalars(core), *arrays, name=name)


def pair_up(mine, other, chip, core):
    chips = mine.shape[0]

    def kernel(at, mine_ref, other_ref, *outs):
        for m in range(chips):
            outs[m][at[1]] = mine_ref[at[0] ^ m]
            outs[m][1 - at[1]] = other_ref[at[0] ^ m]

    shape = ((2,) + mine.shape[1:], mine.dtype)
    return local_call(kernel, [shape] * chips, scalars(chip, core), mine, other, name="pair_up")


def swap_chips(pieces):
    return [pieces[0]] + [swap(pieces[m], "blk", 2 * m) for m in range(1, len(pieces))]


def merge_columns(pieces, count, width, columns_of, chip, name, row=None):
    chips = len(pieces)
    rows = pieces[0].shape[1] if row is None else row
    total = 2 * chips * width

    def kernel(at, *refs):
        sources, outs = refs[:chips], refs[chips:]
        sums = None
        for m in range(chips):
            for core in range(2):
                starts, run = columns_of(2 * (at[0] ^ m) + core)
                for p in range(count):
                    for i, start in enumerate(starts):
                        low = p * width + i * run
                        part = sources[m][core, :rows, low : low + run]
                        outs[p][:, lanes(start, run)] = part.astype(f32)
                if row is not None:
                    part = sources[m][core, rows:, :].astype(f32)
                    sums = part if sums is None else sums + part
        if row is not None:
            outs[count][...] = sums

    shapes = [((rows, total), f32)] * count
    if row is not None:
        shapes.append(((pieces[0].shape[1] - row, count * width), f32))
    return local_call(kernel, shapes, scalars(chip), *pieces, name=name)


def attend_tile(t, which, ways, tok, factor, carried, final, refs):
    heads_at, first, query = refs[:3]
    groups = len(which)
    keys = refs[3 : 3 + groups]
    values = refs[3 + groups : 3 + 2 * groups]
    refs = refs[3 + 2 * groups :]
    seen = (t + 1) * tile
    row = t * tile + lax.broadcasted_iota(jnp.int32, (tile, 1), 0)
    column = lax.broadcasted_iota(jnp.int32, (1, seen), 1)
    row = (row // tok * ways + heads_at[0]) * tok + row % tok
    start = jnp.transpose(jnp.broadcast_to(first[...], (DH, tile)))[:, :1]
    if carried:
        acc = refs[0][...]
        high = jnp.transpose(jnp.broadcast_to(refs[1][0, 0:1, :], (DH, tile)))[:, :1]
        total = jnp.transpose(jnp.broadcast_to(refs[1][0, 1:2, :], (DH, tile)))[:, :1]
        refs = refs[2:]
    else:
        high = jnp.full((tile, 1), masked_fill, f32)
        total = jnp.zeros((tile, 1), f32)
        acc = jnp.zeros((tile, DH), f32)
    for k, m in enumerate(which):
        scores = times_transposed(query[...], keys[k][0, :seen, :]) * factor
        pos = (column // tok * ways + heads_at[m]) * tok + column % tok
        keep = pos[:, t * tile :] <= row
        last = jnp.where(keep & (pos[:, t * tile :] >= start), scores[:, t * tile :], masked_fill)
        if t > 0:
            rest = jnp.where(pos[:, : t * tile] >= start, scores[:, : t * tile], masked_fill)
            scores = jnp.concatenate([rest, last], axis=1)
        else:
            scores = last
        new_high = jnp.maximum(high, jnp.max(scores, axis=-1, keepdims=True))
        weights = jnp.exp2(scores - new_high)
        shrink = jnp.exp2(high - new_high)
        total = total * shrink + jnp.sum(weights, axis=-1, keepdims=True)
        acc = acc * shrink + matmul(weights.astype(bf16), values[k][0, :seen, :])
        high = new_high

    def as_row(column):
        return jnp.transpose(jnp.broadcast_to(column, (tile, DH)))[0:1, :]

    if final:
        refs[0][...] = (acc / total).astype(bf16)
        refs[1][0] = as_row(high + jnp.log2(total))
    else:
        refs[0][...] = acc
        refs[1][0, 0:1, :] = as_row(high)
        refs[1][0, 1:2, :] = as_row(total)


def attend_kernel(tiles, which, ways, tok, factor, carried, final, *refs):
    for t in range(tiles):
        pl.when(pl.program_id(1) == t)(
            functools.partial(attend_tile, t, which, ways, tok, factor, carried, final, refs)
        )


def attend(heads_at, which, first, tok, query, keys, values, state, final):
    rows, width = query.shape
    heads = width // DH
    tiles = rows // tile
    line = pl.BlockSpec((1, tile), lambda i, t: (0, t))
    some = pl.BlockSpec((tile, DH), lambda i, t: (t, i))
    pair = pl.BlockSpec((1, 2, tile), lambda i, t: (i, 0, t))
    single = pl.BlockSpec((1, 1, tile), lambda i, t: (i, 0, t))

    def all_rows(index):
        return pl.BlockSpec((1, rows, DH), lambda i, t: (index, 0, i))

    parts = [keys[m] for m in which] + [values[m] for m in which]
    pairs = rows * rows * len(which) * heads // 2
    carried = state is not None
    return pl.pallas_call(
        functools.partial(
            attend_kernel,
            tiles,
            tuple(which),
            heads_at.shape[0],
            tok,
            log2_e * DH**-0.5,
            carried,
            final,
        ),
        grid=(heads, tiles),
        in_specs=[pl.BlockSpec(memory_space=pltpu.SMEM), line, some]
        + [all_rows(index) for _, index in parts]
        + ([some, pair] if carried else []),
        out_specs=[some, single if final else pair],
        out_shape=[
            jax.ShapeDtypeStruct((rows, width), bf16 if final else f32),
            jax.ShapeDtypeStruct((heads, 1 if final else 2, rows), f32),
        ],
        compiler_params=pltpu.CompilerParams(vmem_limit_bytes=vmem_bytes),
        cost_estimate=pl.CostEstimate(
            flops=4 * pairs * DH,
            bytes_accessed=4 * rows * width * len(which),
            transcendentals=pairs,
        ),
        name="attend",
    )(heads_at, first, query, *[array for array, _ in parts], *(state if carried else []))


def attend_back_tile(t, m, ways, tok, factor, scaling, carried, refs):
    heads_at, first, log_total, delta, query, d_out, keys, values = refs[:8]
    dq, dk, dv = refs[-3:]
    rows = query.shape[0]
    ahead = pl.ds(t * tile, rows - t * tile)
    k_tile, v_tile = keys[0], values[0]
    q_part, d_part = query[ahead, :], d_out[ahead, :]
    scores = times_transposed(k_tile, q_part) * factor
    pos = t * tile + lax.broadcasted_iota(jnp.int32, (tile, 1), 0)
    pos = (pos // tok * ways + heads_at[m]) * tok + pos % tok
    row = t * tile + lax.broadcasted_iota(jnp.int32, (1, rows - t * tile), 1)
    row = (row // tok * ways + heads_at[0]) * tok + row % tok
    probs = jnp.exp2(scores - log_total[0, :, ahead])
    start = first[:, ahead]
    keep = (pos >= start[:, :tile]) & (pos <= row[:, :tile])
    near = jnp.where(keep, probs[:, :tile], 0.0)
    if rows > (t + 1) * tile:
        far = jnp.where(pos >= start[:, tile:], probs[:, tile:], 0.0)
        probs = jnp.concatenate([near, far], axis=1)
    else:
        probs = near
    dv[...] = matmul(probs.astype(bf16), d_part).astype(bf16)
    d_probs = times_transposed(v_tile, d_part)
    d_scores = (probs * (d_probs - delta[0, :, ahead])).astype(bf16)
    dk[...] = (scaling * matmul(d_scores, q_part)).astype(bf16)
    term = scaling * cross_rows(d_scores, k_tile)
    if t > 0:
        dq[ahead, :] += term
    elif carried:
        dq[...] = refs[8][...] + term
    else:
        dq[...] = term


def attend_back_kernel(tiles, m, ways, tok, factor, scaling, carried, *refs):
    for t in range(tiles):
        pl.when(pl.program_id(1) == t)(
            functools.partial(attend_back_tile, t, m, ways, tok, factor, scaling, carried, refs)
        )


def attend_back(heads_at, m, first, tok, log_total, delta, query, d_out, key, value, dq_in):
    rows, width = query.shape
    heads = width // DH
    tiles = rows // tile
    line = pl.BlockSpec((1, rows), lambda i, t: (0, 0))
    stat = pl.BlockSpec((1, 1, rows), lambda i, t: (i, 0, 0))
    tile_rows = pl.BlockSpec((tile, DH), lambda i, t: (t, i))
    block = pl.BlockSpec((rows, DH), lambda i, t: (0, i))

    def some(index):
        return pl.BlockSpec((1, tile, DH), lambda i, t: (index, t, i))

    pairs = rows * rows * heads // 2
    carried = dq_in is not None
    return pl.pallas_call(
        functools.partial(
            attend_back_kernel,
            tiles,
            m,
            heads_at.shape[0],
            tok,
            log2_e * DH**-0.5,
            DH**-0.5,
            carried,
        ),
        grid=(heads, tiles),
        in_specs=[pl.BlockSpec(memory_space=pltpu.SMEM), line, stat, stat, block, block]
        + [some(key[1]), some(value[1])]
        + [block] * (1 if carried else 0),
        out_specs=[block, tile_rows, tile_rows],
        out_shape=[
            jax.ShapeDtypeStruct((rows, width), f32),
            jax.ShapeDtypeStruct((rows, width), bf16),
            jax.ShapeDtypeStruct((rows, width), bf16),
        ],
        compiler_params=pltpu.CompilerParams(vmem_limit_bytes=vmem_bytes),
        cost_estimate=pl.CostEstimate(
            flops=10 * pairs * DH, bytes_accessed=20 * rows * width, transcendentals=pairs
        ),
        name="attend_back",
    )(
        heads_at,
        first,
        log_total,
        delta,
        query,
        d_out,
        key[0],
        value[0],
        *([dq_in] if carried else []),
    )


def normalized(values):
    centered = values - jnp.mean(values, axis=-1, keepdims=True)
    return centered * lax.rsqrt(jnp.mean(centered * centered, axis=-1, keepdims=True) + norm_epsilon)


def project_in(at, mine, other, gain, shift, weights, bias):
    chips, count = len(mine), len(weights)
    tok, width = mine[0].shape
    columns = weights[0].shape[2]
    own = columns // 3

    def body(at_ref, *refs):
        mine_refs, other_refs = refs[:chips], refs[chips : 2 * chips]
        gain_ref, shift_ref, bias_ref = refs[2 * chips : 2 * chips + 3]
        weight_refs = refs[2 * chips + 3 : 2 * chips + 3 + count]
        query, key_value, normed, whole = refs[2 * chips + 3 + count :]
        core = at_ref[chips]

        @pl.when(pl.program_id(0) == 0)
        def _():
            for k, part in enumerate(weight_refs):
                for z in range(chips):
                    low = pl.multiple_of(at_ref[chips + 1 + k] + z * 2 * part.shape[1], 16)
                    whole[pl.ds(low, part.shape[1]), :] = part[z]

        for step in range(chips):

            @pl.when(pl.program_id(0) == step)
            def _():
                for part, place in ((mine_refs[step], core), (other_refs[step], 1 - core)):
                    hat = normalized(part[...].astype(f32))
                    low = pl.multiple_of(place * tok, tok)
                    normed[pl.ds(low, tok), :] = (hat * gain_ref[...] + shift_ref[...]).astype(bf16)

        product = matmul(normed[...], whole[...]) + bias_ref[...]
        product = product.astype(bf16)
        query[...] = product[:, :own]
        key_value[0] = product[:, own : 2 * own]
        key_value[1] = product[:, 2 * own :]

    def fixed(shape):
        return pl.BlockSpec(shape, lambda i, at_ref: (0,) * len(shape))

    rows = 2 * tok * chips
    arrays = [*mine, *other, gain, shift, bias, *weights]
    return pl.pallas_call(
        body,
        grid_spec=pltpu.PrefetchScalarGridSpec(
            num_scalar_prefetch=1,
            grid=(chips,),
            in_specs=[fixed(array.shape) for array in arrays],
            out_specs=[
                pl.BlockSpec((2 * tok, own), lambda i, at_ref: (at_ref[i], 0)),
                pl.BlockSpec((2, 2 * tok, own), lambda i, at_ref: (0, at_ref[i], 0)),
                pl.BlockSpec((2 * tok, width), lambda i, at_ref: (at_ref[i], 0)),
                fixed((width, columns)),
            ],
        ),
        out_shape=[
            jax.ShapeDtypeStruct((rows, own), bf16),
            jax.ShapeDtypeStruct((2, rows, own), bf16),
            jax.ShapeDtypeStruct((rows, width), bf16),
            jax.ShapeDtypeStruct((width, columns), bf16),
        ],
        compiler_params=pltpu.CompilerParams(vmem_limit_bytes=vmem_bytes),
        cost_estimate=pl.CostEstimate(
            flops=2 * rows * width * columns, bytes_accessed=8 * rows * width, transcendentals=0
        ),
        name="project_in",
    )(at, *arrays)


def terms_out(at, array, weights, tokens, transposed):
    steps = at.shape[0] // 2
    rows, width = array.shape
    tok = rows // (2 * steps)
    out_width = weights.shape[0] if transposed else weights.shape[1]

    def body(at_ref, *refs):
        parts, whole = refs[:2], refs[2]
        outs = refs[-3:] if tokens else refs[-2:]
        step = pl.program_id(0)
        sums = []
        left = jnp.concatenate([parts[0][...], parts[1][...]], axis=0)
        both = times_transposed(left, whole[...]) if transposed else matmul(left, whole[...])
        for e in (0, 1):
            term = both[e * tok : (e + 1) * tok]
            outs[e][0] = term.astype(bf16)
            if tokens:
                hat = normalized(refs[3 + e][0].astype(f32))
                sums.append(
                    jnp.concatenate(
                        [
                            jnp.sum(term * hat, axis=0, keepdims=True),
                            jnp.sum(term, axis=0, keepdims=True),
                        ],
                        axis=0,
                    )
                )
        if tokens:

            @pl.when(step == 0)
            def _():
                outs[2][...] = sums[0] + sums[1]

            @pl.when(step > 0)
            def _():
                outs[2][...] += sums[0] + sums[1]

    def block(e):
        return pl.BlockSpec((tok, width), lambda i, at_ref: (at_ref[2 * i + e], 0))

    stacked = pl.BlockSpec((1, tok, out_width), lambda i, at_ref: (i, 0, 0))
    shape = jax.ShapeDtypeStruct((steps, tok, out_width), bf16)
    extra = list(tokens) if tokens else []
    return pl.pallas_call(
        body,
        grid_spec=pltpu.PrefetchScalarGridSpec(
            num_scalar_prefetch=1,
            grid=(steps,),
            in_specs=[block(0), block(1), pl.BlockSpec(weights.shape, lambda i, at_ref: (0, 0))]
            + [stacked] * len(extra),
            out_specs=[stacked, stacked]
            + ([pl.BlockSpec((2, out_width), lambda i, at_ref: (0, 0))] if tokens else []),
        ),
        out_shape=[shape, shape]
        + ([jax.ShapeDtypeStruct((2, out_width), f32)] if tokens else []),
        compiler_params=pltpu.CompilerParams(vmem_limit_bytes=vmem_bytes),
        cost_estimate=pl.CostEstimate(
            flops=2 * rows * width * out_width,
            bytes_accessed=4 * rows * out_width,
            transcendentals=0,
        ),
        name="terms_out",
    )(at, array, array, weights, *extra)


def mix_back(at, mine, other, weights, mixed):
    chips = len(mine)
    tok = mine[0].shape[0]
    rows, own = mixed.shape
    heads = own // DH

    def kernel(at_ref, *refs):
        parts = [refs[e * chips + k] for k in range(chips) for e in (0, 1)]
        whole, mixed_ref, d_mixed, delta = refs[2 * chips :]
        for k, part in enumerate(parts):
            here = pl.ds(pl.multiple_of(at_ref[k] * tok, tok), tok)
            d_mixed[here, :] = times_transposed(part[...], whole[...]).astype(bf16)
        products = d_mixed[...].astype(f32) * mixed_ref[...].astype(f32)
        for k in range(heads):
            turned = jnp.transpose(products[:, k * DH : (k + 1) * DH])
            delta[k] = jnp.sum(turned, axis=0, keepdims=True)

    shapes = [((rows, own), bf16), ((heads, 1, rows), f32)]
    return local_call(kernel, shapes, at, *mine, *other, weights, mixed, name="mix_back")


def mix_grad(at, mine, other, mixed, each, team):
    chips = len(mine)
    tok, width = mine[0].shape
    own = mixed.shape[1]
    w_rows = own // (each * team)

    def kernel(at_ref, *refs):
        parts = [refs[e * chips + k] for k in range(chips) for e in (0, 1)]
        mixed_ref, out = refs[2 * chips :]
        total = None
        for k, part in enumerate(parts):
            here = pl.ds(pl.multiple_of(at_ref[k] * tok, tok), tok)
            term = cross_rows(mixed_ref[here, :], part[...])
            total = term if total is None else total + term
        total = total.astype(bf16)
        for i in range(each):
            for j in range(team):
                low = (i * team + j) * w_rows
                out[j, i] = total[low : low + w_rows]

    shape = ((team, each, w_rows, width), bf16)
    return local_call(kernel, [shape], at, *mine, *other, mixed, name="mix_grad")[0]


def reorder(array, at):
    def kernel(at_ref, source, out):
        for k in range(array.shape[0]):
            out[k] = source[at_ref[k]]

    return local_call(kernel, [(array.shape, array.dtype)], at, array, name="reorder")[0]


def local(
    tokens,
    segments,
    cotangent,
    first_gain,
    first_shift,
    query_proj,
    key_proj,
    value_proj,
    query_bias,
    value_bias,
    out_proj,
    out_bias,
    second_gain,
    second_shift,
    up_proj,
    up_bias,
    down_proj,
    down_bias,
):
    n_head, n_blk = lax.axis_size("head"), lax.axis_size("blk")
    head, blk = lax.axis_index("head"), lax.axis_index("blk")
    chips = n_blk // 2
    chip, core = blk // 2, blk % 2
    tok = tokens.shape[0]
    rows = tok * n_blk
    w_rows = query_proj.shape[0]
    ff_rows = down_proj.shape[0]
    team = DH // w_rows
    sets = n_blk // team
    each = n_head // team
    place_in = blk % team
    own_heads = each * DH

    ring = ring_order(chips)
    behind = jnp.array(
        [[ring[(ring.index(z) - k) % chips] for k in range(chips)] for z in range(chips)], jnp.int32
    )
    behind_all = pick(behind, chip)
    behind = [behind_all[k] for k in range(chips)]

    def spot(step, other):
        return (2 * behind[step] + (core ^ other)) * tok

    def fill_pair(buffer, mine, other, step):
        buffer = lax.dynamic_update_slice_in_dim(buffer, mine, spot(step, 0), 0)
        return lax.dynamic_update_slice_in_dim(buffer, other, spot(step, 1), 0)

    square = n_head == 4

    def head_columns(b):
        at = (b % team) * each
        return [((at + i) * sets + b // team) * DH for i in range(each)], DH

    def ff_columns(b):
        return [(h * n_blk + b) * ff_rows for h in range(n_head)], ff_rows

    ways, two_cores = jnp.arange(n_head, dtype=jnp.int32), jnp.arange(2, dtype=jnp.int32)
    heads_at = head ^ ways
    chips_at = chip ^ jnp.arange(chips, dtype=jnp.int32)
    blocks_at = (2 * behind_all[:, None] + (core ^ two_cores)[None, :]).reshape(-1)
    weights_at = (heads_at[:, None] * n_blk + two_cores[None, :]).reshape(-1) * w_rows
    weights_at = jnp.concatenate([behind_all, core[None], weights_at])

    with jax.named_scope("tokens_gather"):
        tok_mine, tok_other = [tokens], []
        tok_mine.append(next_chip(tokens))

    with jax.named_scope("tokens_gather"):
        tok_other.append(swap(tokens, "blk", 1))

    with jax.named_scope("vectors"):
        small = [
            first_gain,
            first_shift,
            query_bias,
            value_bias,
            out_bias,
            second_gain,
            second_shift,
            down_bias,
            up_bias,
            segments.astype(bf16),
        ]
        small = [v.reshape(-1, w_rows).astype(f32) for v in small]
        height = sum(v.shape[0] for v in small)
        above, packed = 0, 0.0
        for v in small:
            packed = packed + lax.pad(
                v, f32(0), ((above, height - above - v.shape[0], 0), (0, 0, 0))
            )
            above += v.shape[0]
        small = packed.astype(bf16)[None]
    with jax.named_scope("qkv_weights"):
        mine, other = split_columns(
            [query_proj, key_proj, value_proj], own_heads, head_columns, core, chips, "split_heads"
        )
        pieces = pair_up(mine, swap(other, "blk", 1), chip, core)

    with jax.named_scope("down_weights"):
        down_w = lax.all_gather(down_proj, "head", axis=0, tiled=True)
    places = (heads_at, chips_at, blocks_at, weights_at)
    pieces, small, up_proj, tok_mine, tok_other, places = hold(
        pieces, small, up_proj, tok_mine, tok_other, places
    )
    heads_at, chips_at, blocks_at, weights_at = places

    with jax.named_scope("qkv_weights"):
        pieces = swap_chips(pieces)
        fused = place_cores(pieces, chips_at)
    with jax.named_scope("vectors"):
        for bit in bits_of(n_head):
            small = jnp.concatenate([small, swap(small, "head", bit)])
        small = jnp.concatenate([small, swap(small, "blk", 1)])
        small_parts = [small]
        small_parts.append(next_chip(small))

    fused, small_parts, tok_mine, tok_other, up_proj = hold(
        fused, small_parts, tok_mine, tok_other, up_proj
    )

    def small_table():
        height, width = small_parts[0].shape[1:]
        source = jnp.concatenate(small_parts).reshape(n_head * n_blk, height * width)
        index = jnp.arange(n_head * n_blk, dtype=jnp.int32)
        from_chip = jnp.repeat(jnp.stack(behind), 2 * n_head)
        from_core = core ^ (index // n_head % 2)
        from_row = (head ^ (index % n_head)) * n_blk + 2 * from_chip + from_core
        select = (from_row[None, :] == index[:, None]).astype(bf16)
        return matmul(select, source).reshape(n_head, n_blk, height * width)

    def vector(index):
        return table[:, :, index * w_rows : (index + 1) * w_rows].reshape(1, D)

    table = None
    for step in range(1, chips - 1):
        with jax.named_scope("tokens_gather"):
            tok_mine.append(next_chip(tok_mine[step]))
        with jax.named_scope("qkv_weights"):
            if step == 1 and square:
                one = [swap(part, "head", 1) for part in fused]
                two = [swap(part, "head", 2) for part in fused]
            if step == 2 and square:
                low, high = swap(two[0], "head", 1), swap(one[1], "head", 2)
            if step == 1 and not square:
                fused_parts = [gather_head(part) for part in fused]
                fused_parts = [part[m] for m in range(n_head) for part in fused_parts]
        with jax.named_scope("vectors"):
            if len(small_parts) < chips:
                small_parts.append(next_chip(small_parts[-1]))
            elif table is None:
                table = small_table()
        if step == 1:
            with jax.named_scope("up_weights"):
                up_mine, up_other = split_columns(
                    [up_proj], n_head * ff_rows, ff_columns, core, chips, "split_up"
                )
        if step == 1:
            tok_mine, tok_other, small_parts, up_mine, up_other = hold(
                tok_mine, tok_other, small_parts, up_mine, up_other
            )
        elif step < chips - 2:
            tok_mine, small_parts = hold(tok_mine, small_parts)
    if square:
        fused_parts = [*fused, *one, *two, low, high]
    if table is None:
        with jax.named_scope("vectors"):
            table = small_table()
    with jax.named_scope("vectors"):

        def own_head_part(full):
            part = full.reshape(n_head, sets, DH)
            part = lax.dynamic_index_in_dim(part, blk // team, 1, keepdims=False)
            return lax.dynamic_slice_in_dim(part, place_in * each, each, 0).reshape(1, own_heads)

        gain_first, shift_first = vector(0), vector(1)
        q_bias, v_bias = own_head_part(vector(2)), own_head_part(vector(3))
        qkv_bias = jnp.concatenate([q_bias, jnp.zeros_like(q_bias), v_bias], axis=1)
    first_vectors = (gain_first, shift_first, qkv_bias)
    fused_parts, tok_mine, cotangent, up_other, out_proj, first_vectors, down_w = hold(
        fused_parts, tok_mine, cotangent, up_other, out_proj, first_vectors, down_w
    )
    gain_first, shift_first, qkv_bias = first_vectors

    with jax.named_scope("tokens_gather"):
        tok_other += [swap(piece, "blk", 1) for piece in tok_mine[1:]]
    with jax.named_scope("qkv"):
        query, kv, normed, qkv_w = project_in(
            weights_at,
            tok_mine,
            tok_other,
            gain_first,
            shift_first,
            fused_parts,
            qkv_bias,
        )
    with jax.named_scope("up_weights"):
        up_pieces = pair_up(up_mine, swap(up_other, "blk", 1), chip, core)
    with jax.named_scope("out_weights"):
        if square:
            out_parts = [out_proj, swap(out_proj, "head", 1), swap(out_proj, "head", 2)]
        else:
            out_parts = gather_head(out_proj)
    query, kv, up_pieces, normed, out_parts, cotangent, qkv_w, table = hold(
        query, kv, up_pieces, normed, out_parts, cotangent, qkv_w, table
    )

    with jax.named_scope("kv_gather"):
        keys, values = [(kv, 0)], [(kv, 1)]
        if square:
            kv_parts = [swap(kv, "head", 1), swap(kv, "head", 2)]
        else:
            kv_parts = gather_head(kv)[1:]
    with jax.named_scope("up_weights"):
        up_pieces = swap_chips(up_pieces)
    with jax.named_scope("vectors"):
        seq = table[:, :, 8 * w_rows + ff_rows :]
        seg_all = seq.transpose(1, 0, 2).reshape(-1)
        seg_rows = pick(seq, head).reshape(rows)
        first_pos = jnp.sum((seg_all[:, None] < seg_rows[None, :]).astype(jnp.int32), axis=0)[None]
    with jax.named_scope("attention"):
        state = attend(heads_at, [0], first_pos, tok, query, keys, values, None, False)
    kv_parts, state, up_pieces, cotangent, out_parts, first_pos = hold(
        kv_parts, state, up_pieces, cotangent, out_parts, first_pos
    )

    with jax.named_scope("dy_gather"):
        dy_all = lax.all_gather(cotangent, "blk", axis=0, tiled=True)
    with jax.named_scope("up_weights"):
        up_part = place(up_pieces, chips_at).reshape(n_blk * w_rows, n_head * ff_rows)
    with jax.named_scope("kv_gather"):
        keys += [(part, 0) for part in kv_parts]
        values += [(part, 1) for part in kv_parts]
        if square:
            low = swap(kv_parts[1][:1], "head", 1)
            high = swap(kv_parts[0][1:], "head", 2)
    with jax.named_scope("out_weights"):
        if square:
            half = w_rows // 2
            out_low = swap(out_parts[2][:half], "head", 1)
            out_high = swap(out_parts[1][half:], "head", 2)
            out_parts = out_parts + [jnp.concatenate([out_low, out_high])]
    if square:
        low, high, out_parts, state, up_part = hold(low, high, out_parts, state, up_part)
        keys.append((low, 0))
        values.append((high, 0))
    else:
        out_parts, state, up_part = hold(out_parts, state, up_part)
    with jax.named_scope("up_weights"):
        up_w = lax.all_gather(up_part, "head", axis=0, tiled=True)

    with jax.named_scope("out_weights"):
        out_w = place(out_parts, heads_at).reshape(team, each, w_rows, D)
        out_w = exchange(out_w, "blk", place_in, team)
        out_w = out_w.transpose(1, 0, 2, 3).reshape(own_heads, D)
    with jax.named_scope("attention"):
        left = list(range(1, n_head))
        mixed, log_total = attend(
            heads_at, left, first_pos, tok, query, keys, values, state, True
        )
    mixed, out_w, table = hold(mixed, out_w, table)

    def cross(term):
        return (term[0], swap(term[1], "blk", 1))

    def onward(pair, moving):
        return next_chip(sum_of(pair, moving).astype(bf16))

    def sum_of(pair, moving):
        total = pair[0].astype(f32) + pair[1].astype(f32)
        return total if moving is None else total + moving.astype(f32)

    def met(own, other):
        crossing = swap(other, "blk", 1)
        return [(own[step], crossing[step]) for step in range(chips)]

    with jax.named_scope("branch"):
        ready = met(*terms_out(blocks_at, mixed, out_w, None, False))
        ready, dy_all = hold(ready, dy_all)
        moving = None
        for step in range(1, chips):
            moving = onward(ready[step], moving)
            with jax.named_scope("vectors"):
                if step == 1:
                    o_bias, gain_second, shift_second, d_bias = [vector(k) for k in range(4, 8)]
                    u_bias = table[:, :, 8 * w_rows : 8 * w_rows + ff_rows]
                    u_bias = lax.dynamic_index_in_dim(u_bias, blk, 1, keepdims=False)
                    vectors = (o_bias, gain_second, shift_second, d_bias, u_bias.reshape(1, -1))
            if step == 1:
                moving, ready, vectors = hold(moving, ready, vectors)
                o_bias, gain_second, shift_second, d_bias, u_bias = vectors
            else:
                moving, ready = hold(moving, ready)
        own = tokens.astype(f32)
        hidden = own + (sum_of(ready[0], moving) + o_bias)
        hat_second, inv_second = norm_parts(hidden)
        second_own = (hat_second * gain_second + shift_second).astype(bf16)
    hidden, second_own, inv_second, up_w = hold(hidden, second_own, inv_second, up_w)

    with jax.named_scope("mlp"):
        second_all = blank((rows, D), bf16)
        active_all = blank((rows, n_head * ff_rows), bf16)
        d_upper_all = blank((rows, n_head * ff_rows), bf16)
        sec_mine, sec_other = [second_own], []
        terms = {}

        def mlp_chunk(step, second_all, active_all, d_upper_all):
            base = 2 * behind[step] * tok

            def chunk_of(array):
                return lax.dynamic_slice_in_dim(array, base, 2 * tok, 0)

            def fill(buffer, chunk):
                return lax.dynamic_update_slice_in_dim(buffer, chunk, base, 0)

            second_all = fill_pair(second_all, sec_mine[step], sec_other[step], step)
            upper = matmul(chunk_of(second_all), up_w) + u_bias
            phi = 0.5 * (1.0 + lax.erf(upper * 0.7071067811865476))
            active = (upper * phi).astype(bf16)
            slope = phi + upper * jnp.exp(-0.5 * upper * upper) * 0.3989422804014327
            d_active = times_transposed(chunk_of(dy_all), down_w)
            d_upper = (d_active * slope).astype(bf16)
            terms[step] = [
                times_transposed(
                    lax.dynamic_slice_in_dim(d_upper, (core ^ other) * tok, tok, 0), up_w
                ).astype(bf16)
                for other in (0, 1)
            ]
            return second_all, fill(active_all, active), fill(d_upper_all, d_upper)

        for step in range(chips):
            if step < chips - 1:
                sec_mine.append(next_chip(sec_mine[step]))
            if step > 0:
                second_all, active_all, d_upper_all = mlp_chunk(
                    step - 1, second_all, active_all, d_upper_all
                )
                if step == chips - 1:
                    ready = cross(terms[1])
            sec_other.append(swap(sec_mine[step], "blk", 1))
            ready, sec_mine, sec_other, terms, second_all, active_all, d_upper_all = hold(
                ready, sec_mine, sec_other, terms, second_all, active_all, d_upper_all
            )
        moving = None
        for step in range(1, chips):
            moving = onward(ready, moving)
            if step == 1:
                second_all, active_all, d_upper_all = mlp_chunk(
                    chips - 1, second_all, active_all, d_upper_all
                )
            ready = cross(terms[(step + 1) % chips])
            if step == 1:
                with jax.named_scope("up_grad"):
                    up_term = cross_rows(second_all, d_upper_all).astype(bf16)
                moving, ready, terms, active_all, d_upper_all, up_term = hold(
                    moving, ready, terms, active_all, d_upper_all, up_term
                )
            elif step == 2:
                with jax.named_scope("down_grad"):
                    down_term = cross_rows(active_all, dy_all).astype(bf16)
                moving, ready, terms, down_term, active_all = hold(
                    moving, ready, terms, down_term, active_all
                )
            elif step == 3:
                with jax.named_scope("output"):
                    out_term = matmul(active_all, down_w).astype(bf16)
                moving, ready, terms, out_term = hold(moving, ready, terms, out_term)
            else:
                moving, ready, terms = hold(moving, ready, terms)
        d_second = sum_of(ready, moving)
        upstream = cotangent.astype(f32)
        d_hidden = upstream + norm_back(d_second, hat_second, inv_second, gain_second)
        d_branch_own = d_hidden.astype(bf16)

    def sum_heads(terms):
        return lax.psum_scatter(terms, "head", scatter_dimension=0, tiled=True)

    with jax.named_scope("up_grad"):
        up_sum = sum_heads(up_term)
    d_hidden, d_branch_own, active_all, d_second = hold(
        d_hidden, d_branch_own, active_all, d_second
    )
    mine, other = [d_branch_own], []

    with jax.named_scope("d_branch_gather"):
        for step in range(chips - 1):
            mine.append(next_chip(mine[step]))
            if step == 1:
                mine, up_sum, down_term = hold(mine, up_sum, down_term)
                with jax.named_scope("down_grad"):
                    down_grad = sum_heads(down_term)
            else:
                (mine,) = hold(mine)
        other = [swap(piece, "blk", 1) for piece in mine]
        d_mixed, delta = mix_back(blocks_at, mine, other, out_w, mixed)
    d_mixed, delta, mine, other, up_sum, out_term = hold(
        d_mixed, delta, mine, other, up_sum, out_term
    )

    dq = None

    def kv_grad(m):
        return attend_back(
            heads_at, m, first_pos, tok, log_total, delta, query, d_mixed, keys[m], values[m], dq
        )

    d_keys, d_values = {}, {}
    for m in reversed(range(n_head)):
        with jax.named_scope("attention_back"):
            if square and m == 2:
                low = swap(d_keys[3], "head", 1)
                high = swap(d_values[3], "head", 2)
            if square and m == 0:
                one = [d_keys[1], (d_values[1].astype(f32) + high.astype(f32)).astype(bf16)]
                two = [(d_keys[2].astype(f32) + low.astype(f32)).astype(bf16), d_values[2]]
                one, two, dq = hold(one, two, dq)
                one[0], two[0] = swap(one[0], "head", 1), swap(two[0], "head", 2)
            dq, d_keys[m], d_values[m] = kv_grad(m)
        if m == n_head - 1:
            with jax.named_scope("up_grad"):
                up_sum = up_sum.reshape(chips, 2, w_rows, n_head * ff_rows)
                up_mine = lax.dynamic_index_in_dim(up_sum, core, 1, keepdims=False)
                up_other = lax.dynamic_index_in_dim(up_sum, 1 - core, 1, keepdims=False)
                up_pieces = pair_up(up_mine, swap(up_other, "blk", 1), chip, core)
            dq, d_keys, d_values, d_mixed, up_pieces = hold(
                dq, d_keys, d_values, d_mixed, up_pieces
            )
        elif m == n_head - 2:
            with jax.named_scope("up_grad"):
                up_pieces = swap_chips(up_pieces)
            dq, d_keys, d_values, d_mixed = hold(dq, d_keys, d_values, d_mixed)
        elif square and m == 1:
            low, high, dq, d_keys, d_values, d_mixed, up_pieces, down_grad, out_term = hold(
                low, high, dq, d_keys, d_values, d_mixed, up_pieces, down_grad, out_term
            )
        elif m > 0:
            dq, d_keys, d_values, d_mixed = hold(dq, d_keys, d_values, d_mixed)
    if square:
        one, two, dq, mine, other, mixed, tok_mine, tok_other = hold(
            one, two, dq, mine, other, mixed, tok_mine, tok_other
        )
        with jax.named_scope("attention_back"):
            one[1], two[1] = swap(one[1], "head", 1), swap(two[1], "head", 2)
    with jax.named_scope("output"):
        out_sum = lax.psum_scatter(out_term, "blk", scatter_dimension=0, tiled=True)
    with jax.named_scope("out_grad"):
        mix_term = mix_grad(blocks_at, mine, other, mixed, each, team)
        mix_term = exchange(mix_term, "blk", place_in, team)
    with jax.named_scope("d_normed"):
        tok_stacks = (jnp.stack(tok_mine), jnp.stack(tok_other))
    with jax.named_scope("attention_back"):
        if square:
            d_keys, d_values = [
                (total[0].astype(f32) + one[k].astype(f32) + two[k].astype(f32)).astype(bf16)
                for k, total in enumerate((d_keys, d_values))
            ]
        else:
            d_keys, d_values = [
                scatter_head(lambda m: total[m].astype(f32)).astype(bf16)
                for total in (d_keys, d_values)
            ]
        d_qkv = jnp.concatenate([dq.astype(bf16), d_keys, d_values], axis=1)
    kept = (d_branch_own, d_second, hat_second, d_upper_all, cotangent, dq, d_values)
    d_qkv, up_pieces, mix_term, tok_stacks = hold(d_qkv, up_pieces, mix_term, tok_stacks)

    slab = n_blk * w_rows
    with jax.named_scope("d_normed"):
        own_terms, other_terms, first_sums = terms_out(
            blocks_at, d_qkv, qkv_w, tok_stacks, True
        )
        ready = met(own_terms, other_terms)
    ready, first_sums, normed, d_qkv, mix_term, out_sum = hold(
        ready, first_sums, normed, d_qkv, mix_term, out_sum
    )
    moving = onward(ready[1], None)
    with jax.named_scope("out_grad"):
        out_grad = sum_heads(mix_term.reshape(n_head * w_rows, D))
    with jax.named_scope("qkv_grad"):
        qkv_term = cross_rows(normed, d_qkv).astype(bf16).reshape(n_head, slab, 3 * own_heads)
    ready, qkv_term, moving, kept, first_sums = hold(ready, qkv_term, moving, kept, first_sums)
    d_branch_own, d_second, hat_second, d_upper_all, cotangent, dq, d_values = kept
    with jax.named_scope("vector_grads"):
        full = [
            first_sums[0],
            first_sums[1],
            jnp.sum(d_branch_own.astype(f32), axis=0),
            jnp.sum(d_second * hat_second, axis=0),
            jnp.sum(d_second, axis=0),
            jnp.sum(cotangent.astype(f32), axis=0),
        ]
        parts = [v.reshape(n_head, n_blk, w_rows) for v in full]
        up_row = jnp.sum(d_upper_all.astype(f32), axis=0)
        up_table = jnp.zeros((n_blk, n_head, ff_rows), f32)
        up_table = put(up_table, up_row.reshape(n_head, ff_rows), blk)
        parts.append(up_table.transpose(1, 0, 2))
        for v in (dq.astype(bf16), d_values):
            bias_sum = jnp.sum(v.astype(f32), axis=0).reshape(each, 1, DH)
            head_table = jnp.zeros((n_head, sets, DH), f32)
            head_table = lax.dynamic_update_slice(
                head_table, bias_sum, (place_in * each, blk // team, 0)
            )
            parts.append(head_table.reshape(n_head, n_blk, w_rows))
        parts = jnp.concatenate(parts, axis=2)
        wide = 3 * own_heads
        deep = -(-parts.shape[2] // wide)
        parts = jnp.pad(parts, ((0, 0), (0, 0), (0, deep * wide - parts.shape[2])))
        parts = parts.reshape(n_head, n_blk * deep, wide).astype(bf16)
    for step in range(2, chips):
        with jax.named_scope("d_normed"):
            moving = onward(ready[step], moving)
        if step == 2 and square:
            with jax.named_scope("qkv_grad"):
                half = slab // 2
                far = pick(qkv_term, head ^ 3)
                low = swap(far[:half], "head", 1)
                high = swap(far[half:], "head", 2)
                one, two = pick(qkv_term, head ^ 1), pick(qkv_term, head ^ 2)
            with jax.named_scope("vector_grads"):
                across = swap(pick(parts, head ^ 3), "head", 1)
            moving, low, high, one, two, parts, across, ready = hold(
                moving, low, high, one, two, parts, across, ready
            )
        elif step == 3 and square:
            with jax.named_scope("qkv_grad"):
                two_parts = pick(parts, head ^ 2) + across
                one = jnp.concatenate([one[:half], one[half:] + high, pick(parts, head ^ 1)])
                two = jnp.concatenate([two[:half] + low, two[half:], two_parts])
                one, two = swap(one, "head", 1), swap(two, "head", 2)
            with jax.named_scope("output"):
                output = (hidden + (out_sum.astype(f32) + d_bias)).astype(bf16)
            with jax.named_scope("up_grad"):
                (up_grad,) = merge_columns(
                    up_pieces, 1, n_head * ff_rows, ff_columns, chip, "merge_up"
                )
            with jax.named_scope("down_grad"):
                down_grad = down_grad.astype(f32)
            moving, one, two, output, up_grad, down_grad, ready = hold(
                moving, one, two, output, up_grad, down_grad, ready
            )
        else:
            moving, ready = hold(moving, ready)
    with jax.named_scope("qkv_grad"):
        whole = jnp.concatenate([qkv_term, parts], axis=1)
        if square:
            qkv_grad = pick(whole, head).astype(f32) + one.astype(f32) + two.astype(f32)
        else:
            qkv_grad = scatter_head(lambda m: pick(whole, head ^ m).astype(f32))
            output = (hidden + (out_sum.astype(f32) + d_bias)).astype(bf16)
            (up_grad,) = merge_columns(up_pieces, 1, n_head * ff_rows, ff_columns, chip, "merge_up")
            down_grad = down_grad.astype(f32)
        qkv_grad = qkv_grad.astype(bf16)
        extra = qkv_grad[slab:].reshape(chips, 2, deep, wide)
        extra = jnp.pad(extra, ((0, 0), (0, 0), (0, -deep % 16), (0, 0)))
        qkv_grad = qkv_grad[:slab].reshape(chips, 2, w_rows, wide)
        qkv_grad = jnp.concatenate([qkv_grad, extra], axis=2)
        qkv_mine = lax.dynamic_index_in_dim(qkv_grad, core, 1, keepdims=False)
        qkv_other = lax.dynamic_index_in_dim(qkv_grad, 1 - core, 1, keepdims=False)
        pieces = pair_up(qkv_mine, swap(qkv_other, "blk", 1), chip, core)
        pieces = swap_chips(pieces)
        *qkv_grad, sums = merge_columns(
            pieces, 3, own_heads, head_columns, chip, "merge_heads", row=w_rows
        )
    with jax.named_scope("vector_grads"):
        sums = sums[:deep].reshape(-1)
        cuts = [sums[i * w_rows : (i + 1) * w_rows] for i in range(6)]
        up_bias_grad = sums[6 * w_rows : 6 * w_rows + ff_rows]
        rest = sums[6 * w_rows + ff_rows : 8 * w_rows + ff_rows]
    with jax.named_scope("d_normed"):
        d_normed = sum_of(ready[0], moving)
        hat_first, inv_first = norm_parts(own)
        tokens_grad = (d_hidden + norm_back(d_normed, hat_first, inv_first, gain_first)).astype(bf16)

    return (
        output,
        tokens_grad,
        cuts[0],
        cuts[1],
        qkv_grad[0],
        qkv_grad[1],
        qkv_grad[2],
        rest[:w_rows],
        rest[w_rows:],
        out_grad.astype(f32),
        cuts[2],
        cuts[3],
        cuts[4],
        up_grad,
        up_bias_grad,
        down_grad,
        cuts[5],
    )


def solution(mesh):
    by_token = P(("blk", "head"), None)
    matrix = P(("head", "blk"), None)
    vector = P(("head", "blk"))
    return jax.shard_map(
        local,
        mesh=mesh,
        in_specs=(
            by_token,
            P(("blk", "head")),
            by_token,
            vector,
            vector,
            matrix,
            matrix,
            matrix,
            vector,
            vector,
            matrix,
            vector,
            vector,
            vector,
            matrix,
            vector,
            matrix,
            vector,
        ),
        out_specs=(
            by_token,
            by_token,
            vector,
            vector,
            matrix,
            matrix,
            matrix,
            vector,
            vector,
            matrix,
            vector,
            vector,
            vector,
            matrix,
            vector,
            matrix,
            vector,
        ),
        check_vma=False,
    )
```

```python
import functools

import jax
import jax.numpy as jnp
from jax import lax
from jax.experimental import pallas as pl
from jax.experimental.pallas import tpu as pltpu
from jax.sharding import PartitionSpec as P

D = 2048
H = 16
DH = 128

norm_epsilon = 1e-05
masked_fill = -1e30
tile = 256
bf16 = jnp.bfloat16
f32 = jnp.float32
log2_e = 1.4426950408889634
vmem_bytes = 58 * 1024 * 1024
vmem_small = 20 * 1024 * 1024


def matmul(left, right):
    return jnp.dot(left, right, preferred_element_type=f32)


def cross_rows(left, right):
    return lax.dot_general(left, right, (((0,), (0,)), ((), ())), preferred_element_type=f32)


def times_transposed(left, right):
    return lax.dot_general(left, right, (((1,), (1,)), ((), ())), preferred_element_type=f32)


def norm_parts(values):
    row_mean = jnp.mean(values, axis=-1, keepdims=True)
    centered = values - row_mean
    row_var = jnp.mean(centered * centered, axis=-1, keepdims=True)
    inverse = lax.rsqrt(row_var + norm_epsilon)
    return (centered * inverse, inverse)


def norm_back(grad_out, normal_hat, inverse, gain):
    scaled_grad = grad_out * gain
    return inverse * (
        scaled_grad
        - jnp.mean(scaled_grad, axis=-1, keepdims=True)
        - normal_hat * jnp.mean(scaled_grad * normal_hat, axis=-1, keepdims=True)
    )


def swap(v, axis, mask):
    size = lax.axis_size(axis)
    return lax.ppermute(v, axis, [(i, i ^ mask) for i in range(size)])


def ring_order(chips):
    return list(range(0, chips, 2)) + [k for k in range(chips - 1, 0, -1) if k % 2]


def next_chip(v):
    chips = lax.axis_size("blk") // 2
    order = ring_order(chips)
    moves = [(order[k], order[(k + 1) % chips]) for k in range(chips)]
    return lax.ppermute(v, "blk", [(2 * a + c, 2 * b + c) for a, b in moves for c in range(2)])


def pick(v, index):
    return lax.dynamic_index_in_dim(v, index, 0, keepdims=False)


def put(v, part, index):
    return lax.dynamic_update_index_in_dim(v, part, index, 0)


def bits_of(size):
    return [1 << k for k in range(size.bit_length() - 1)]


def blank(shape, dtype):
    return pl.pallas_call(
        lambda out: None,
        out_shape=jax.ShapeDtypeStruct(shape, dtype),
        out_specs=pl.BlockSpec(memory_space=pl.ANY),
        name="blank",
    )()


def hold(*values):
    return lax.optimization_barrier(values)


def gather_head(v):
    size = lax.axis_size("head")
    if size == 4:
        half = v.shape[0] // 2
        one, two = swap(v, "head", 1), swap(v, "head", 2)
        low = swap(two[:half], "head", 1)
        high = swap(one[half:], "head", 2)
        return [v, one, two, jnp.concatenate([low, high], axis=0)]
    held = [v]
    for bit in bits_of(size):
        held = held + [swap(part, "head", bit) for part in held]
    return held


def scatter_head(chunk):
    size = lax.axis_size("head")
    if size == 4:
        far = chunk(3).astype(bf16)
        half = far.shape[0] // 2
        low = swap(far[:half], "head", 1)
        high = swap(far[half:], "head", 2)
        one, two = chunk(1), chunk(2)
        one = jnp.concatenate([one[:half], one[half:] + high.astype(f32)], axis=0)
        two = jnp.concatenate([two[:half] + low.astype(f32), two[half:]], axis=0)
        one = swap(one.astype(bf16), "head", 1)
        two = swap(two.astype(bf16), "head", 2)
        return chunk(0) + one.astype(f32) + two.astype(f32)
    terms = [chunk(m) for m in range(size)]
    for bit in reversed(bits_of(size)):
        terms = [
            terms[m] + swap(terms[m | bit].astype(bf16), "head", bit).astype(f32) for m in range(bit)
        ]
    return terms[0]


def exchange(pieces, axis, mine, group):
    out = pieces
    for mask in range(1, group):
        out = put(out, swap(pick(pieces, mine ^ mask), axis, mask), mine ^ mask)
    return out


def scalars(*values):
    return jnp.stack([jnp.asarray(v, jnp.int32) for v in values])


def local_call(kernel, out_shapes, scalar, *arrays, name, vmem=None):
    return pl.pallas_call(
        kernel,
        in_specs=[pl.BlockSpec(memory_space=pltpu.SMEM)]
        + [pl.BlockSpec(memory_space=pltpu.VMEM)] * len(arrays),
        out_specs=[pl.BlockSpec(memory_space=pltpu.VMEM)] * len(out_shapes),
        out_shape=[jax.ShapeDtypeStruct(shape, dtype) for shape, dtype in out_shapes],
        compiler_params=pltpu.CompilerParams(vmem_limit_bytes=vmem or vmem_small),
        name=name,
    )(scalar, *arrays)


def place(blocks, at):
    count = len(blocks)

    def kernel(at_ref, *refs):
        for k in range(count):
            refs[count][at_ref[k]] = refs[k][...]

    shape = ((count,) + blocks[0].shape, blocks[0].dtype)
    return local_call(kernel, [shape], at, *blocks, name="place")[0]


def place_cores(pieces, at):
    count = len(pieces)

    def kernel(at_ref, *refs):
        for k in range(count):
            for c in range(2):
                refs[count + c][at_ref[k]] = refs[k][c]

    shape = ((count,) + pieces[0].shape[1:], pieces[0].dtype)
    return local_call(kernel, [shape, shape], at, *pieces, name="place_cores")


def lanes(start, size):
    return pl.ds(pl.multiple_of(start, DH), size)


def split_columns(arrays, width, columns_of, core, chips, name):
    rows = arrays[0].shape[0]

    def kernel(core_ref, *refs):
        sources, (mine, other) = refs[:-2], refs[-2:]
        me = core_ref[0]
        for chip in range(chips):
            for out, index in ((mine, me), (other, 1 - me)):
                starts, run = columns_of(2 * chip + index)
                for p, source in enumerate(sources):
                    for i, start in enumerate(starts):
                        low = p * width + i * run
                        out[chip, :, low : low + run] = source[:, lanes(start, run)]

    shape = ((chips, rows, len(arrays) * width), arrays[0].dtype)
    return local_call(kernel, [shape, shape], scalars(core), *arrays, name=name)


def pair_up(mine, other, chip, core):
    chips = mine.shape[0]

    def kernel(at, mine_ref, other_ref, *outs):
        for m in range(chips):
            outs[m][at[1]] = mine_ref[at[0] ^ m]
            outs[m][1 - at[1]] = other_ref[at[0] ^ m]

    shape = ((2,) + mine.shape[1:], mine.dtype)
    return local_call(kernel, [shape] * chips, scalars(chip, core), mine, other, name="pair_up")


def swap_chips(pieces):
    return [pieces[0]] + [swap(pieces[m], "blk", 2 * m) for m in range(1, len(pieces))]


def merge_columns(pieces, count, width, columns_of, chip, name, row=None):
    chips = len(pieces)
    rows = pieces[0].shape[1] if row is None else row
    total = 2 * chips * width

    def kernel(at, *refs):
        sources, outs = refs[:chips], refs[chips:]
        sums = None
        for m in range(chips):
            for core in range(2):
                starts, run = columns_of(2 * (at[0] ^ m) + core)
                for p in range(count):
                    for i, start in enumerate(starts):
                        low = p * width + i * run
                        part = sources[m][core, :rows, low : low + run]
                        outs[p][:, lanes(start, run)] = part.astype(f32)
                if row is not None:
                    part = sources[m][core, rows:, :].astype(f32)
                    sums = part if sums is None else sums + part
        if row is not None:
            outs[count][...] = sums

    shapes = [((rows, total), f32)] * count
    if row is not None:
        shapes.append(((pieces[0].shape[1] - row, count * width), f32))
    return local_call(kernel, shapes, scalars(chip), *pieces, name=name)


def each_tile(heads, tiles, whole, body):
    for i in range(heads):
        for t in range(tiles):
            if whole:
                body(i, t)
            else:
                pl.when(pl.program_id(0) == i * tiles + t)(functools.partial(body, i, t))


def fixed_blocks(arrays):
    return [
        pl.BlockSpec(array.shape, lambda i, n=len(array.shape): (0,) * n) for array in arrays
    ]


def attend(heads_at, which, first, tok, query, keys, values, state, final):
    rows, width = query.shape
    heads, tiles, ways = width // DH, rows // tile, heads_at.shape[0]
    factor = log2_e * DH**-0.5
    carried = state is not None
    arrays = []
    for array, _ in [keys[m] for m in which] + [values[m] for m in which]:
        if not any(array is other for other in arrays):
            arrays.append(array)

    def find(entry):
        return [array is entry[0] for array in arrays].index(True), entry[1]

    def kernel(heads_ref, first_ref, query_ref, *refs):
        parts = refs[: len(arrays)]
        outs = refs[-2:]

        def body(i, t):
            lane, here = pl.ds(i * DH, DH), pl.ds(t * tile, tile)
            seen = (t + 1) * tile
            row = t * tile + lax.broadcasted_iota(jnp.int32, (tile, 1), 0)
            column = lax.broadcasted_iota(jnp.int32, (1, seen), 1)
            row = (row // tok * ways + heads_ref[0]) * tok + row % tok
            start = jnp.transpose(jnp.broadcast_to(first_ref[:, here], (DH, tile)))[:, :1]
            if carried:
                stats = refs[len(arrays) + 1]
                high = jnp.transpose(jnp.broadcast_to(stats[i, 0:1, here], (DH, tile)))[:, :1]
                total = jnp.transpose(jnp.broadcast_to(stats[i, 1:2, here], (DH, tile)))[:, :1]
                top = high
            else:
                top = jnp.full((tile, 1), masked_fill, f32)
            scores = []
            for m in which:
                k, index = find(keys[m])
                raw = times_transposed(query_ref[here, lane], parts[k][index, :seen, lane])
                pos = (column // tok * ways + heads_ref[m]) * tok + column % tok
                keep = (pos[:, t * tile :] <= row) & (pos[:, t * tile :] >= start)
                last = jnp.where(keep, raw[:, t * tile :], masked_fill)
                if t > 0:
                    rest = jnp.where(pos[:, : t * tile] >= start, raw[:, : t * tile], masked_fill)
                    last = jnp.concatenate([rest, last], axis=1)
                scores.append(last)
                top = jnp.maximum(top, jnp.max(last, axis=-1, keepdims=True))
            if carried:
                shrink = jnp.exp2((high - top) * factor)
                total, acc = total * shrink, refs[len(arrays)][here, lane] * shrink
            else:
                total, acc = jnp.zeros((tile, 1), f32), jnp.zeros((tile, DH), f32)
            for m, part in zip(which, scores):
                weights = jnp.exp2((part - top) * factor)
                total = total + jnp.sum(weights, axis=-1, keepdims=True)
                k, index = find(values[m])
                acc = acc + matmul(weights.astype(bf16), parts[k][index, :seen, lane])

            def as_row(value):
                return jnp.transpose(jnp.broadcast_to(value, (tile, DH)))[0:1, :]

            if final:
                outs[0][here, lane] = (acc / total).astype(bf16)
                outs[1][i, :, here] = as_row(top * factor + jnp.log2(total))
            else:
                outs[0][here, lane] = acc
                outs[1][i, 0:1, here] = as_row(top)
                outs[1][i, 1:2, here] = as_row(total)

        each_tile(heads, tiles, rows * len(which) <= 4096, body)

    pairs = rows * rows * len(which) * heads // 2
    operands = [first, query, *arrays, *(state if carried else [])]
    shapes = [
        jax.ShapeDtypeStruct((rows, width), bf16 if final else f32),
        jax.ShapeDtypeStruct((heads, 1 if final else 2, rows), f32),
    ]
    return pl.pallas_call(
        kernel,
        grid=(1 if rows * len(which) <= 4096 else heads * tiles,),
        in_specs=[pl.BlockSpec(memory_space=pltpu.SMEM)] + fixed_blocks(operands),
        out_specs=fixed_blocks(shapes),
        out_shape=shapes,
        compiler_params=pltpu.CompilerParams(vmem_limit_bytes=vmem_bytes),
        cost_estimate=pl.CostEstimate(
            flops=4 * pairs * DH,
            bytes_accessed=4 * rows * width * len(which),
            transcendentals=pairs,
        ),
        name="attend",
    )(heads_at, *operands)


def attend_back(heads_at, m, first, tok, log_total, delta, query, d_out, key, value, dq_in):
    rows, width = query.shape
    heads, tiles, ways = width // DH, rows // tile, heads_at.shape[0]
    factor, scaling = log2_e * DH**-0.5, DH**-0.5
    carried = dq_in is not None
    parts = [key[0]] if key[0] is value[0] else [key[0], value[0]]

    def kernel(heads_ref, first_ref, log_ref, delta_ref, query_ref, out_ref, *refs):
        keys, values = refs[0], refs[len(parts) - 1]
        dq, dk, dv = refs[-3:]

        def body(i, t):
            lane, here = pl.ds(i * DH, DH), pl.ds(t * tile, tile)
            ahead = pl.ds(t * tile, rows - t * tile)
            k_tile, v_tile = keys[key[1], here, lane], values[value[1], here, lane]
            q_part, d_part = query_ref[ahead, lane], out_ref[ahead, lane]
            scores = times_transposed(k_tile, q_part) * factor
            pos = t * tile + lax.broadcasted_iota(jnp.int32, (tile, 1), 0)
            pos = (pos // tok * ways + heads_ref[m]) * tok + pos % tok
            row = t * tile + lax.broadcasted_iota(jnp.int32, (1, tile), 1)
            row = (row // tok * ways + heads_ref[0]) * tok + row % tok
            probs = jnp.exp2(scores - log_ref[i, :, ahead])
            start = first_ref[:, ahead]
            keep = (pos >= start[:, :tile]) & (pos <= row)
            near = jnp.where(keep, probs[:, :tile], 0.0)
            if rows > (t + 1) * tile:
                far = jnp.where(pos >= start[:, tile:], probs[:, tile:], 0.0)
                probs = jnp.concatenate([near, far], axis=1)
            else:
                probs = near
            dv[here, lane] = matmul(probs.astype(bf16), d_part).astype(bf16)
            d_probs = times_transposed(v_tile, d_part)
            d_scores = (probs * (d_probs - delta_ref[i, :, ahead])).astype(bf16)
            dk[here, lane] = (scaling * matmul(d_scores, q_part)).astype(bf16)
            term = scaling * cross_rows(d_scores, k_tile)
            if t > 0:
                dq[ahead, lane] += term
            elif carried:
                dq[:, lane] = refs[len(parts)][:, lane] + term
            else:
                dq[:, lane] = term

        each_tile(heads, tiles, rows <= 1024, body)

    pairs = rows * rows * heads // 2
    operands = [first, log_total, delta, query, d_out, *parts] + ([dq_in] if carried else [])
    shapes = [jax.ShapeDtypeStruct((rows, width), kind) for kind in (f32, bf16, bf16)]
    return pl.pallas_call(
        kernel,
        grid=(1 if rows <= 1024 else heads * tiles,),
        in_specs=[pl.BlockSpec(memory_space=pltpu.SMEM)] + fixed_blocks(operands),
        out_specs=fixed_blocks(shapes),
        out_shape=shapes,
        compiler_params=pltpu.CompilerParams(vmem_limit_bytes=vmem_bytes),
        cost_estimate=pl.CostEstimate(
            flops=10 * pairs * DH, bytes_accessed=20 * rows * width, transcendentals=pairs
        ),
        name="attend_back",
    )(heads_at, *operands)


def normalized(values):
    centered = values - jnp.mean(values, axis=-1, keepdims=True)
    return centered * lax.rsqrt(jnp.mean(centered * centered, axis=-1, keepdims=True) + norm_epsilon)


def project_in(at, mine, other, gain, shift, weights, bias):
    chips, count = len(mine), len(weights)
    tok, width = mine[0].shape
    columns = weights[0].shape[2]
    own = columns // 3

    def body(at_ref, *refs):
        mine_refs, other_refs = refs[:chips], refs[chips : 2 * chips]
        gain_ref, shift_ref, bias_ref = refs[2 * chips : 2 * chips + 3]
        weight_refs = refs[2 * chips + 3 : 2 * chips + 3 + count]
        query, key_value, normed, whole = refs[2 * chips + 3 + count :]
        core = at_ref[chips]

        @pl.when(pl.program_id(0) == 0)
        def _():
            for k, part in enumerate(weight_refs):
                for z in range(chips):
                    low = pl.multiple_of(at_ref[chips + 1 + k] + z * 2 * part.shape[1], 16)
                    whole[pl.ds(low, part.shape[1]), :] = part[z]

        for step in range(chips):

            @pl.when(pl.program_id(0) == step)
            def _():
                for part, place in ((mine_refs[step], core), (other_refs[step], 1 - core)):
                    hat = normalized(part[...].astype(f32))
                    low = pl.multiple_of(place * tok, tok)
                    normed[pl.ds(low, tok), :] = (hat * gain_ref[...] + shift_ref[...]).astype(bf16)

        product = matmul(normed[...], whole[...]) + bias_ref[...]
        product = product.astype(bf16)
        query[...] = product[:, :own]
        key_value[0] = product[:, own : 2 * own]
        key_value[1] = product[:, 2 * own :]

    def fixed(shape):
        return pl.BlockSpec(shape, lambda i, at_ref: (0,) * len(shape))

    rows = 2 * tok * chips
    arrays = [*mine, *other, gain, shift, bias, *weights]
    return pl.pallas_call(
        body,
        grid_spec=pltpu.PrefetchScalarGridSpec(
            num_scalar_prefetch=1,
            grid=(chips,),
            in_specs=[fixed(array.shape) for array in arrays],
            out_specs=[
                pl.BlockSpec((2 * tok, own), lambda i, at_ref: (at_ref[i], 0)),
                pl.BlockSpec((2, 2 * tok, own), lambda i, at_ref: (0, at_ref[i], 0)),
                pl.BlockSpec((2 * tok, width), lambda i, at_ref: (at_ref[i], 0)),
                fixed((width, columns)),
            ],
        ),
        out_shape=[
            jax.ShapeDtypeStruct((rows, own), bf16),
            jax.ShapeDtypeStruct((2, rows, own), bf16),
            jax.ShapeDtypeStruct((rows, width), bf16),
            jax.ShapeDtypeStruct((width, columns), bf16),
        ],
        compiler_params=pltpu.CompilerParams(vmem_limit_bytes=vmem_bytes),
        cost_estimate=pl.CostEstimate(
            flops=2 * rows * width * columns, bytes_accessed=8 * rows * width, transcendentals=0
        ),
        name="project_in",
    )(at, *arrays)


def terms_out(at, array, weights, transposed):
    steps = at.shape[0] // 2
    rows, width = array.shape
    tok = rows // (2 * steps)
    out_width = weights.shape[0] if transposed else weights.shape[1]

    def body(at_ref, mine, other, whole, *outs):
        left = jnp.concatenate([mine[...], other[...]], axis=0)
        both = times_transposed(left, whole[...]) if transposed else matmul(left, whole[...])
        for e in (0, 1):
            outs[e][0] = both[e * tok : (e + 1) * tok].astype(bf16)

    def block(e):
        return pl.BlockSpec((tok, width), lambda i, at_ref: (at_ref[2 * i + e], 0))

    stacked = pl.BlockSpec((1, tok, out_width), lambda i, at_ref: (i, 0, 0))
    shape = jax.ShapeDtypeStruct((steps, tok, out_width), bf16)
    return pl.pallas_call(
        body,
        grid_spec=pltpu.PrefetchScalarGridSpec(
            num_scalar_prefetch=1,
            grid=(steps,),
            in_specs=[block(0), block(1), pl.BlockSpec(weights.shape, lambda i, at_ref: (0, 0))],
            out_specs=[stacked, stacked],
        ),
        out_shape=[shape, shape],
        compiler_params=pltpu.CompilerParams(vmem_limit_bytes=vmem_bytes),
        cost_estimate=pl.CostEstimate(
            flops=2 * rows * width * out_width,
            bytes_accessed=4 * rows * out_width,
            transcendentals=0,
        ),
        name="terms_out",
    )(at, array, array, weights)


def norm_sums(own, other, mine, others):
    chips, tok, width = own.shape

    def body(*refs):
        terms, pieces, out = refs[:2], refs[2 : 2 + 2 * chips], refs[-1]
        step = pl.program_id(0)

        @pl.when(step == 0)
        def _():
            out[...] = jnp.zeros_like(out)

        for k in range(chips):

            @pl.when(step == k)
            def _():
                for e in (0, 1):
                    term = terms[e][0].astype(f32)
                    hat = normalized(pieces[e * chips + k][...].astype(f32))
                    out[0:1, :] += jnp.sum(term * hat, axis=0, keepdims=True)
                    out[1:2, :] += jnp.sum(term, axis=0, keepdims=True)

    stacked = pl.BlockSpec((1, tok, width), lambda i: (i, 0, 0))
    return pl.pallas_call(
        body,
        grid=(chips,),
        in_specs=[stacked, stacked] + fixed_blocks([*mine, *others]),
        out_specs=pl.BlockSpec((2, width), lambda i: (0, 0)),
        out_shape=jax.ShapeDtypeStruct((2, width), f32),
        compiler_params=pltpu.CompilerParams(vmem_limit_bytes=vmem_bytes),
        name="norm_sums",
    )(own, other, *mine, *others)


def mix_back(at, parts, weights, mixed, earlier):
    count = len(parts)
    tok = parts[0].shape[0]
    rows, own = mixed.shape
    heads = own // DH

    def kernel(at_ref, *refs):
        whole, outs = refs[count], refs[count + 1 :]
        d_mixed = outs[2] if earlier is not None else outs[0]
        if earlier is not None:
            mixed_ref, before, _, delta = outs
            d_mixed[...] = before[...]
        for k in range(count):
            here = pl.ds(pl.multiple_of(at_ref[k] * tok, tok), tok)
            d_mixed[here, :] = times_transposed(refs[k][...], whole[...]).astype(bf16)
        if earlier is not None:
            products = d_mixed[...].astype(f32) * mixed_ref[...].astype(f32)
            for k in range(heads):
                turned = jnp.transpose(products[:, k * DH : (k + 1) * DH])
                delta[k] = jnp.sum(turned, axis=0, keepdims=True)

    shapes = [((rows, own), bf16)]
    if earlier is None:
        return local_call(kernel, shapes, at, *parts, weights, name="mix_back", vmem=vmem_bytes)[0]
    shapes.append(((heads, 1, rows), f32))
    return local_call(
        kernel, shapes, at, *parts, weights, mixed, earlier, name="mix_back", vmem=vmem_bytes
    )


def mix_grad(at, mine, other, mixed, each, team):
    chips = len(mine)
    tok, width = mine[0].shape
    own = mixed.shape[1]
    w_rows = own // (each * team)

    def kernel(at_ref, *refs):
        parts = [refs[e * chips + k] for k in range(chips) for e in (0, 1)]
        mixed_ref, out = refs[2 * chips :]
        total = None
        for k, part in enumerate(parts):
            here = pl.ds(pl.multiple_of(at_ref[k] * tok, tok), tok)
            term = cross_rows(mixed_ref[here, :], part[...])
            total = term if total is None else total + term
        total = total.astype(bf16)
        for i in range(each):
            for j in range(team):
                low = (i * team + j) * w_rows
                out[j, i] = total[low : low + w_rows]

    shape = ((team, each, w_rows, width), bf16)
    return local_call(kernel, [shape], at, *mine, *other, mixed, name="mix_grad", vmem=vmem_bytes)[0]


def reorder(array, at):
    def kernel(at_ref, source, out):
        for k in range(array.shape[0]):
            out[k] = source[at_ref[k]]

    return local_call(kernel, [(array.shape, array.dtype)], at, array, name="reorder")[0]


def local(
    tokens,
    segments,
    cotangent,
    first_gain,
    first_shift,
    query_proj,
    key_proj,
    value_proj,
    query_bias,
    value_bias,
    out_proj,
    out_bias,
    second_gain,
    second_shift,
    up_proj,
    up_bias,
    down_proj,
    down_bias,
):
    n_head, n_blk = lax.axis_size("head"), lax.axis_size("blk")
    head, blk = lax.axis_index("head"), lax.axis_index("blk")
    chips = n_blk // 2
    chip, core = blk // 2, blk % 2
    tok = tokens.shape[0]
    rows = tok * n_blk
    w_rows = query_proj.shape[0]
    ff_rows = down_proj.shape[0]
    team = DH // w_rows
    sets = n_blk // team
    each = n_head // team
    place_in = blk % team
    own_heads = each * DH

    ring = ring_order(chips)
    behind = jnp.array(
        [[ring[(ring.index(z) - k) % chips] for k in range(chips)] for z in range(chips)], jnp.int32
    )
    behind_all = pick(behind, chip)
    behind = [behind_all[k] for k in range(chips)]

    def spot(step, other):
        return (2 * behind[step] + (core ^ other)) * tok

    def fill_pair(buffer, mine, other, step):
        buffer = lax.dynamic_update_slice_in_dim(buffer, mine, spot(step, 0), 0)
        return lax.dynamic_update_slice_in_dim(buffer, other, spot(step, 1), 0)

    square = n_head == 4

    def head_columns(b):
        at = (b % team) * each
        return [((at + i) * sets + b // team) * DH for i in range(each)], DH

    def ff_columns(b):
        return [(h * n_blk + b) * ff_rows for h in range(n_head)], ff_rows

    ways, two_cores = jnp.arange(n_head, dtype=jnp.int32), jnp.arange(2, dtype=jnp.int32)
    heads_at = head ^ ways
    chips_at = chip ^ jnp.arange(chips, dtype=jnp.int32)
    blocks_at = (2 * behind_all[:, None] + (core ^ two_cores)[None, :]).reshape(-1)
    weights_at = (heads_at[:, None] * n_blk + two_cores[None, :]).reshape(-1) * w_rows
    weights_at = jnp.concatenate([behind_all, core[None], weights_at])

    with jax.named_scope("tokens_gather"):
        tok_mine, tok_other = [tokens], []
        tok_mine.append(next_chip(tokens))

    with jax.named_scope("tokens_gather"):
        tok_other.append(swap(tokens, "blk", 1))

    with jax.named_scope("vectors"):
        small = [
            first_gain,
            first_shift,
            query_bias,
            value_bias,
            out_bias,
            second_gain,
            second_shift,
            down_bias,
            up_bias,
            segments.astype(bf16),
        ]
        small = [v.reshape(-1, w_rows).astype(f32) for v in small]
        height = sum(v.shape[0] for v in small)
        above, packed = 0, 0.0
        for v in small:
            packed = packed + lax.pad(
                v, f32(0), ((above, height - above - v.shape[0], 0), (0, 0, 0))
            )
            above += v.shape[0]
        small = packed.astype(bf16)[None]
    with jax.named_scope("qkv_weights"):
        mine, other = split_columns(
            [query_proj, key_proj, value_proj], own_heads, head_columns, core, chips, "split_heads"
        )
        pieces = pair_up(mine, swap(other, "blk", 1), chip, core)

    places = (heads_at, chips_at, blocks_at, weights_at)
    pieces, small, up_proj, tok_mine, tok_other, places = hold(
        pieces, small, up_proj, tok_mine, tok_other, places
    )
    heads_at, chips_at, blocks_at, weights_at = places

    with jax.named_scope("qkv_weights"):
        pieces = swap_chips(pieces)
        fused = place_cores(pieces, chips_at)
    with jax.named_scope("vectors"):
        for bit in bits_of(n_head):
            small = jnp.concatenate([small, swap(small, "head", bit)])
        small = jnp.concatenate([small, swap(small, "blk", 1)])
        small_parts = [small]
        small_parts.append(next_chip(small))

    fused, small_parts, tok_mine, tok_other, up_proj = hold(
        fused, small_parts, tok_mine, tok_other, up_proj
    )

    def small_table():
        height, width = small_parts[0].shape[1:]
        source = jnp.concatenate(small_parts).reshape(n_head * n_blk, height * width)
        index = jnp.arange(n_head * n_blk, dtype=jnp.int32)
        from_chip = jnp.repeat(jnp.stack(behind), 2 * n_head)
        from_core = core ^ (index // n_head % 2)
        from_row = (head ^ (index % n_head)) * n_blk + 2 * from_chip + from_core
        select = (from_row[None, :] == index[:, None]).astype(bf16)
        return matmul(select, source).reshape(n_head, n_blk, height * width)

    def vector(index):
        return table[:, :, index * w_rows : (index + 1) * w_rows].reshape(1, D)

    table = None
    for step in range(1, chips - 1):
        with jax.named_scope("tokens_gather"):
            tok_mine.append(next_chip(tok_mine[step]))
        with jax.named_scope("qkv_weights"):
            if step == 1 and square:
                one = [swap(part, "head", 1) for part in fused]
                two = [swap(part, "head", 2) for part in fused]
            if step == 2 and square:
                low, high = swap(two[0], "head", 1), swap(one[1], "head", 2)
            if step == 1 and not square:
                fused_parts = [gather_head(part) for part in fused]
                fused_parts = [part[m] for m in range(n_head) for part in fused_parts]
        with jax.named_scope("vectors"):
            if len(small_parts) < chips:
                small_parts.append(next_chip(small_parts[-1]))
            elif table is None:
                table = small_table()
        if step == 1:
            with jax.named_scope("up_weights"):
                up_mine, up_other = split_columns(
                    [up_proj], n_head * ff_rows, ff_columns, core, chips, "split_up"
                )
        if step == 1:
            tok_mine, tok_other, small_parts, up_mine, up_other = hold(
                tok_mine, tok_other, small_parts, up_mine, up_other
            )
        elif step < chips - 2:
            tok_mine, small_parts = hold(tok_mine, small_parts)
    if square:
        fused_parts = [*fused, *one, *two, low, high]
    if table is None:
        with jax.named_scope("vectors"):
            table = small_table()
    with jax.named_scope("vectors"):

        def own_head_part(full):
            part = full.reshape(n_head, sets, DH)
            part = lax.dynamic_index_in_dim(part, blk // team, 1, keepdims=False)
            return lax.dynamic_slice_in_dim(part, place_in * each, each, 0).reshape(1, own_heads)

        gain_first, shift_first = vector(0), vector(1)
        q_bias, v_bias = own_head_part(vector(2)), own_head_part(vector(3))
        qkv_bias = jnp.concatenate([q_bias, jnp.zeros_like(q_bias), v_bias], axis=1)
    first_vectors = (gain_first, shift_first, qkv_bias)
    fused_parts, tok_mine, cotangent, up_other, out_proj, first_vectors = hold(
        fused_parts, tok_mine, cotangent, up_other, out_proj, first_vectors
    )
    gain_first, shift_first, qkv_bias = first_vectors

    with jax.named_scope("tokens_gather"):
        tok_other += [swap(piece, "blk", 1) for piece in tok_mine[1:]]
    with jax.named_scope("qkv"):
        query, kv, normed, qkv_w = project_in(
            weights_at,
            tok_mine,
            tok_other,
            gain_first,
            shift_first,
            fused_parts,
            qkv_bias,
        )
    with jax.named_scope("up_weights"):
        up_pieces = pair_up(up_mine, swap(up_other, "blk", 1), chip, core)
    with jax.named_scope("out_weights"):
        out_parts = [out_proj] + [swap(out_proj, "head", m) for m in range(1, n_head)]
    query, kv, up_pieces, normed, out_parts, cotangent, qkv_w, table = hold(
        query, kv, up_pieces, normed, out_parts, cotangent, qkv_w, table
    )

    with jax.named_scope("kv_gather"):
        keys, values = [(kv, 0)], [(kv, 1)]
        if square:
            kv_parts = [swap(kv, "head", 1), swap(kv, "head", 2)]
        else:
            kv_parts = gather_head(kv)[1:]
    with jax.named_scope("up_weights"):
        up_pieces = swap_chips(up_pieces)
    with jax.named_scope("vectors"):
        seq = table[:, :, 8 * w_rows + ff_rows :]
        seg_all = seq.transpose(1, 0, 2).reshape(-1)
        seg_rows = pick(seq, head).reshape(rows)
        first_pos = jnp.sum((seg_all[:, None] < seg_rows[None, :]).astype(jnp.int32), axis=0)[None]
    with jax.named_scope("attention"):
        state = attend(heads_at, [0], first_pos, tok, query, keys, values, None, False)
    kv_parts, state, up_pieces, cotangent, out_parts, first_pos = hold(
        kv_parts, state, up_pieces, cotangent, out_parts, first_pos
    )

    with jax.named_scope("dy_gather"):
        dy_all = lax.all_gather(cotangent, "blk", axis=0, tiled=True)
    with jax.named_scope("up_weights"):
        up_part = place(up_pieces, chips_at).reshape(n_blk * w_rows, n_head * ff_rows)
    with jax.named_scope("kv_gather"):
        keys += [(part, 0) for part in kv_parts]
        values += [(part, 1) for part in kv_parts]
        if square:
            low = swap(kv_parts[1][:1], "head", 1)
            high = swap(kv_parts[0][1:], "head", 2)
    with jax.named_scope("out_weights"):
        out_w = place(out_parts, heads_at).reshape(team, each, w_rows, D)
        out_w = exchange(out_w, "blk", place_in, team)
        out_w = out_w.transpose(1, 0, 2, 3).reshape(own_heads, D)
    if square:
        low, high, out_w, state, up_part, down_proj = hold(
            low, high, out_w, state, up_part, down_proj
        )
        keys.append((low, 0))
        values.append((high, 0))
    else:
        out_w, state, up_part, down_proj = hold(out_w, state, up_part, down_proj)
    with jax.named_scope("up_weights"):
        up_w = lax.all_gather(up_part, "head", axis=0, tiled=True)

    with jax.named_scope("attention"):
        left = list(range(1, n_head))
        mixed, log_total = attend(
            heads_at, left, first_pos, tok, query, keys, values, state, True
        )
    with jax.named_scope("down_weights"):
        if square:
            downs = [down_proj, swap(down_proj, "head", 1), swap(down_proj, "head", 2)]
        else:
            downs = gather_head(down_proj)
    mixed, out_w, table, downs = hold(mixed, out_w, table, downs)

    def cross(term):
        return (term[0], swap(term[1], "blk", 1))

    def onward(pair, moving):
        return next_chip(sum_of(pair, moving).astype(bf16))

    def sum_of(pair, moving):
        total = pair[0].astype(f32) + pair[1].astype(f32)
        return total if moving is None else total + moving.astype(f32)

    def met(own, other):
        return (own, swap(other, "blk", 1))

    def entry(pair, step):
        return (pair[0][step], pair[1][step])

    with jax.named_scope("branch"):
        ready = met(*terms_out(blocks_at, mixed, out_w, False))
        ready, dy_all = hold(ready, dy_all)
        moving = None
        for step in range(1, chips):
            moving = onward(entry(ready, step), moving)
            with jax.named_scope("vectors"):
                if step == 1:
                    o_bias, gain_second, shift_second, d_bias = [vector(k) for k in range(4, 8)]
                    u_bias = table[:, :, 8 * w_rows : 8 * w_rows + ff_rows]
                    u_bias = lax.dynamic_index_in_dim(u_bias, blk, 1, keepdims=False)
                    vectors = (o_bias, gain_second, shift_second, d_bias, u_bias.reshape(1, -1))
            with jax.named_scope("down_weights"):
                if square and step == 2:
                    half = ff_rows // 2
                    low = swap(downs[2][:half], "head", 1)
                    high = swap(downs[1][half:], "head", 2)
                if not square and step == 1:
                    down_w = place(downs, heads_at).reshape(n_head * ff_rows, D)
            if step == 1:
                moving, ready, vectors = hold(moving, ready, vectors)
                o_bias, gain_second, shift_second, d_bias, u_bias = vectors
            elif step == 2:
                moving, ready, downs = hold(moving, ready, downs)
            elif square and step == 3:
                moving, ready, low, high = hold(moving, ready, low, high)
            else:
                moving, ready = hold(moving, ready)
        own = tokens.astype(f32)
        hidden = own + (sum_of(entry(ready, 0), moving) + o_bias)
        hat_second, inv_second = norm_parts(hidden)
        second_own = (hat_second * gain_second + shift_second).astype(bf16)
    hidden, second_own, inv_second = hold(hidden, second_own, inv_second)

    with jax.named_scope("down_weights"):
        if square:
            blocks = [part.reshape(2, half, D)[k] for part in downs for k in (0, 1)]
            at = (2 * heads_at[:, None] + two_cores[None, :]).reshape(-1)
            down_w = place(blocks + [low, high], at).reshape(n_head * ff_rows, D)

    with jax.named_scope("mlp"):
        second_all = blank((rows, D), bf16)
        active_all = blank((rows, n_head * ff_rows), bf16)
        d_upper_all = blank((rows, n_head * ff_rows), bf16)
        sec_mine, sec_other = [second_own], []
        terms = {}

        def mlp_chunk(step, second_all, active_all, d_upper_all):
            base = 2 * behind[step] * tok

            def chunk_of(array):
                return lax.dynamic_slice_in_dim(array, base, 2 * tok, 0)

            def fill(buffer, chunk):
                return lax.dynamic_update_slice_in_dim(buffer, chunk, base, 0)

            second_all = fill_pair(second_all, sec_mine[step], sec_other[step], step)
            upper = matmul(chunk_of(second_all), up_w) + u_bias
            phi = 0.5 * (1.0 + lax.erf(upper * 0.7071067811865476))
            active = (upper * phi).astype(bf16)
            slope = phi + upper * jnp.exp(-0.5 * upper * upper) * 0.3989422804014327
            d_active = times_transposed(chunk_of(dy_all), down_w)
            d_upper = (d_active * slope).astype(bf16)
            terms[step] = [
                times_transposed(
                    lax.dynamic_slice_in_dim(d_upper, (core ^ other) * tok, tok, 0), up_w
                ).astype(bf16)
                for other in (0, 1)
            ]
            return second_all, fill(active_all, active), fill(d_upper_all, d_upper)

        for step in range(chips):
            if step < chips - 1:
                sec_mine.append(next_chip(sec_mine[step]))
            if step > 0:
                second_all, active_all, d_upper_all = mlp_chunk(
                    step - 1, second_all, active_all, d_upper_all
                )
                if step == chips - 1:
                    ready = cross(terms[1])
            sec_other.append(swap(sec_mine[step], "blk", 1))
            ready, sec_mine, sec_other, terms, second_all, active_all, d_upper_all = hold(
                ready, sec_mine, sec_other, terms, second_all, active_all, d_upper_all
            )
        moving = None
        for step in range(1, chips):
            moving = onward(ready, moving)
            if step == 1:
                second_all, active_all, d_upper_all = mlp_chunk(
                    chips - 1, second_all, active_all, d_upper_all
                )
            ready = cross(terms[(step + 1) % chips])
            if step == 2:
                with jax.named_scope("up_grad"):
                    up_term = cross_rows(second_all, d_upper_all).astype(bf16)
                moving, ready, terms, active_all, d_upper_all, up_term = hold(
                    moving, ready, terms, active_all, d_upper_all, up_term
                )
            elif step == 3:
                with jax.named_scope("down_grad"):
                    down_term = cross_rows(active_all, dy_all).astype(bf16)
                moving, ready, terms, down_term, active_all = hold(
                    moving, ready, terms, down_term, active_all
                )
            else:
                moving, ready, terms, second_all, active_all, d_upper_all = hold(
                    moving, ready, terms, second_all, active_all, d_upper_all
                )
        d_second = sum_of(ready, moving)
        upstream = cotangent.astype(f32)
        d_hidden = upstream + norm_back(d_second, hat_second, inv_second, gain_second)
        d_branch_own = d_hidden.astype(bf16)

    def sum_heads(terms):
        return lax.psum_scatter(terms, "head", scatter_dimension=0, tiled=True)

    with jax.named_scope("up_grad"):
        up_sum = sum_heads(up_term)
    d_hidden, d_branch_own, active_all, d_second = hold(
        d_hidden, d_branch_own, active_all, d_second
    )
    mine, other = [d_branch_own], []

    with jax.named_scope("d_branch_gather"):
        half = tok // 2
        halves = [[d_branch_own[:half]], [d_branch_own[half:]]]
        with jax.named_scope("output"):
            out_term = matmul(active_all, down_w).astype(bf16)
        for step in range(chips - 1):
            for chain in halves:
                if step > 0:
                    (held,) = hold(chain[step])
                    chain[step] = held
                chain.append(next_chip(chain[step]))
            if step > 0:
                mine.append(jnp.concatenate([chain[step] for chain in halves], axis=0))
        mine.append(jnp.concatenate([chain[-1] for chain in halves], axis=0))
        mine, up_sum, out_term = hold(mine, up_sum, out_term)
        with jax.named_scope("output"):
            out_sum = lax.psum_scatter(out_term, "blk", scatter_dimension=0, tiled=True)
        other = [swap(piece, "blk", 1) for piece in mine]
        by_core = blocks_at.reshape(chips, 2)
        d_mixed = mix_back(by_core[:, 0], mine, out_w, mixed, None)
        d_mixed, delta = mix_back(by_core[:, 1], other, out_w, mixed, d_mixed)
    with jax.named_scope("up_grad"):
        up_sum = up_sum.reshape(chips, 2, w_rows, n_head * ff_rows)
        up_mine = lax.dynamic_index_in_dim(up_sum, core, 1, keepdims=False)
        up_other = lax.dynamic_index_in_dim(up_sum, 1 - core, 1, keepdims=False)
        up_pieces = pair_up(up_mine, swap(up_other, "blk", 1), chip, core)
    d_mixed, delta, mine, other = hold(d_mixed, delta, mine, other)

    dq = None

    def kv_grad(m):
        return attend_back(
            heads_at, m, first_pos, tok, log_total, delta, query, d_mixed, keys[m], values[m], dq
        )

    d_keys, d_values = {}, {}
    for m in reversed(range(n_head)):
        with jax.named_scope("attention_back"):
            if square and m == 2:
                low = swap(d_keys[3], "head", 1)
                high = swap(d_values[3], "head", 2)
            if square and m == 0:
                one = [d_keys[1], (d_values[1].astype(f32) + high.astype(f32)).astype(bf16)]
                two = [(d_keys[2].astype(f32) + low.astype(f32)).astype(bf16), d_values[2]]
                one, two, dq, up_pieces = hold(one, two, dq, up_pieces)
                one[0], two[0] = swap(one[0], "head", 1), swap(two[0], "head", 2)
            dq, d_keys[m], d_values[m] = kv_grad(m)
        if square and m == 1:
            low, high, dq, d_keys, d_values, d_mixed = hold(
                low, high, dq, d_keys, d_values, d_mixed
            )
        elif m > 0:
            dq, d_keys, d_values, d_mixed = hold(dq, d_keys, d_values, d_mixed)
    with jax.named_scope("up_grad"):
        up_pieces = swap_chips(up_pieces)
    if square:
        one, two, dq, mine, other, mixed, out_sum, down_term = hold(
            one, two, dq, mine, other, mixed, out_sum, down_term
        )
        with jax.named_scope("attention_back"):
            one[1], two[1] = swap(one[1], "head", 1), swap(two[1], "head", 2)
    with jax.named_scope("out_grad"):
        mix_term = mix_grad(blocks_at, mine, other, mixed, each, team)
    with jax.named_scope("down_grad"):
        down_grad = sum_heads(down_term)
    with jax.named_scope("attention_back"):
        if square:
            d_keys, d_values = [
                (total[0].astype(f32) + one[k].astype(f32) + two[k].astype(f32)).astype(bf16)
                for k, total in enumerate((d_keys, d_values))
            ]
        else:
            d_keys, d_values = [
                scatter_head(lambda m: total[m].astype(f32)).astype(bf16)
                for total in (d_keys, d_values)
            ]
        d_qkv = jnp.concatenate([dq.astype(bf16), d_keys, d_values], axis=1)
    kept = (d_branch_own, d_second, hat_second, d_upper_all, cotangent, dq, d_values)
    d_qkv, up_pieces, mix_term = hold(d_qkv, up_pieces, mix_term)

    slab, wide = n_blk * w_rows, 3 * own_heads
    with jax.named_scope("d_normed"):
        own_terms, other_terms = terms_out(blocks_at, d_qkv, qkv_w, True)
        ready = met(own_terms, other_terms)
    with jax.named_scope("qkv_grad"):
        qkv_term = cross_rows(normed, d_qkv).astype(bf16).reshape(n_head, slab, wide)
    ready, qkv_term, mix_term, up_pieces, kept = hold(ready, qkv_term, mix_term, up_pieces, kept)
    d_branch_own, d_second, hat_second, d_upper_all, cotangent, dq, d_values = kept
    moving = None
    for step in range(1, chips):
        with jax.named_scope("d_normed"):
            moving = onward(entry(ready, step), moving)
        if step == 1:
            with jax.named_scope("qkv_grad"):
                if square:
                    half = slab // 2
                    far = pick(qkv_term, head ^ 3)
                    low, high = swap(far[:half], "head", 1), swap(far[half:], "head", 2)
                else:
                    low = high = qkv_term
            with jax.named_scope("vector_grads"):
                full = [
                    jnp.sum(d_branch_own.astype(f32), axis=0),
                    jnp.sum(d_second * hat_second, axis=0),
                    jnp.sum(d_second, axis=0),
                    jnp.sum(cotangent.astype(f32), axis=0),
                ]
                parts = [v.reshape(n_head, n_blk, w_rows) for v in full]
                up_row = jnp.sum(d_upper_all.astype(f32), axis=0)
                up_table = jnp.zeros((n_blk, n_head, ff_rows), f32)
                up_table = put(up_table, up_row.reshape(n_head, ff_rows), blk)
                parts.append(up_table.transpose(1, 0, 2))
                for v in (dq.astype(bf16), d_values):
                    bias_sum = jnp.sum(v.astype(f32), axis=0).reshape(each, 1, DH)
                    head_table = jnp.zeros((n_head, sets, DH), f32)
                    head_table = lax.dynamic_update_slice(
                        head_table, bias_sum, (place_in * each, blk // team, 0)
                    )
                    parts.append(head_table.reshape(n_head, n_blk, w_rows))
            moving, ready, low, high, parts, own_terms, mix_term, tok_mine, tok_other = hold(
                moving, ready, low, high, parts, own_terms, mix_term, tok_mine, tok_other
            )
        elif step == 2:
            with jax.named_scope("qkv_grad"):
                if square:
                    one, two = pick(qkv_term, head ^ 1), pick(qkv_term, head ^ 2)
                    one = jnp.concatenate([one[:half], one[half:] + high])
                    two = jnp.concatenate([two[:half] + low, two[half:]])
                    one, two = swap(one, "head", 1), swap(two, "head", 2)
            with jax.named_scope("vector_grads"):
                first_sums = norm_sums(own_terms, other_terms, tok_mine, tok_other)
            moving, ready, first_sums, down_grad, mix_term = hold(
                moving, ready, first_sums, down_grad, mix_term
            )
        elif step == 3:
            with jax.named_scope("out_grad"):
                mix_term = exchange(mix_term, "blk", place_in, team)
            with jax.named_scope("vector_grads"):
                parts = [v.reshape(n_head, n_blk, w_rows) for v in first_sums] + parts
                parts = jnp.concatenate(parts, axis=2)
                deep = -(-parts.shape[2] // wide)
                parts = jnp.pad(parts, ((0, 0), (0, 0), (0, deep * wide - parts.shape[2])))
                parts = parts.reshape(n_head, n_blk * deep, wide)
            moving, ready, parts, mix_term = hold(moving, ready, parts, mix_term)
        else:
            moving, ready = hold(moving, ready)
    with jax.named_scope("out_grad"):
        out_grad = sum_heads(mix_term.reshape(n_head * w_rows, D))
    with jax.named_scope("vector_grads"):
        sums = scatter_head(lambda m: pick(parts, head ^ m))
        sums = sums.astype(bf16)
    with jax.named_scope("qkv_grad"):
        if square:
            qkv_grad = pick(qkv_term, head).astype(f32) + one.astype(f32) + two.astype(f32)
        else:
            qkv_grad = scatter_head(lambda m: pick(qkv_term, head ^ m).astype(f32))
        qkv_grad = qkv_grad.astype(bf16).reshape(chips, 2, w_rows, wide)
        extra = sums.reshape(chips, 2, deep, wide)
        extra = jnp.pad(extra, ((0, 0), (0, 0), (0, -deep % 16), (0, 0)))
        qkv_grad = jnp.concatenate([qkv_grad, extra], axis=2)
        qkv_mine = lax.dynamic_index_in_dim(qkv_grad, core, 1, keepdims=False)
        qkv_other = lax.dynamic_index_in_dim(qkv_grad, 1 - core, 1, keepdims=False)
        pieces = pair_up(qkv_mine, swap(qkv_other, "blk", 1), chip, core)
    pieces, up_pieces, down_grad, out_sum, moving = hold(
        pieces, up_pieces, down_grad, out_sum, moving
    )
    with jax.named_scope("qkv_grad"):
        pieces = swap_chips(pieces)
    with jax.named_scope("d_normed"):
        d_normed = sum_of(entry(ready, 0), moving)
        hat_first, inv_first = norm_parts(own)
        tokens_grad = (d_hidden + norm_back(d_normed, hat_first, inv_first, gain_first)).astype(bf16)
    with jax.named_scope("output"):
        output = (hidden + (out_sum.astype(f32) + d_bias)).astype(bf16)
    with jax.named_scope("up_grad"):
        (up_grad,) = merge_columns(up_pieces, 1, n_head * ff_rows, ff_columns, chip, "merge_up")
    with jax.named_scope("down_grad"):
        down_grad = down_grad.astype(f32)
    with jax.named_scope("qkv_grad"):
        *qkv_grad, sums = merge_columns(
            pieces, 3, own_heads, head_columns, chip, "merge_heads", row=w_rows
        )
    with jax.named_scope("vector_grads"):
        sums = sums[:deep].reshape(-1)
        cuts = [sums[i * w_rows : (i + 1) * w_rows] for i in range(6)]
        up_bias_grad = sums[6 * w_rows : 6 * w_rows + ff_rows]
        rest = sums[6 * w_rows + ff_rows : 8 * w_rows + ff_rows]

    return (
        output,
        tokens_grad,
        cuts[0],
        cuts[1],
        qkv_grad[0],
        qkv_grad[1],
        qkv_grad[2],
        rest[:w_rows],
        rest[w_rows:],
        out_grad.astype(f32),
        cuts[2],
        cuts[3],
        cuts[4],
        up_grad,
        up_bias_grad,
        down_grad,
        cuts[5],
    )


def solution(mesh):
    by_token = P(("blk", "head"), None)
    matrix = P(("head", "blk"), None)
    vector = P(("head", "blk"))
    return jax.shard_map(
        local,
        mesh=mesh,
        in_specs=(
            by_token,
            P(("blk", "head")),
            by_token,
            vector,
            vector,
            matrix,
            matrix,
            matrix,
            vector,
            vector,
            matrix,
            vector,
            vector,
            vector,
            matrix,
            vector,
            matrix,
            vector,
        ),
        out_specs=(
            by_token,
            by_token,
            vector,
            vector,
            matrix,
            matrix,
            matrix,
            vector,
            vector,
            matrix,
            vector,
            vector,
            vector,
            matrix,
            vector,
            matrix,
            vector,
        ),
        check_vma=False,
    )
```

```python
import functools

import jax
import jax.numpy as jnp
from jax import lax
from jax.experimental import pallas as pl
from jax.experimental.pallas import tpu as pltpu
from jax.sharding import PartitionSpec as P

D = 2048
H = 16
DH = 128

norm_epsilon = 1e-05
masked_fill = -1e30
tile = 256
bf16 = jnp.bfloat16
f32 = jnp.float32
log2_e = 1.4426950408889634
vmem_bytes = 58 * 1024 * 1024
vmem_small = 20 * 1024 * 1024


def matmul(left, right):
    return jnp.dot(left, right, preferred_element_type=f32)


def cross_rows(left, right):
    return lax.dot_general(left, right, (((0,), (0,)), ((), ())), preferred_element_type=f32)


def times_transposed(left, right):
    return lax.dot_general(left, right, (((1,), (1,)), ((), ())), preferred_element_type=f32)


def norm_parts(values):
    row_mean = jnp.mean(values, axis=-1, keepdims=True)
    centered = values - row_mean
    row_var = jnp.mean(centered * centered, axis=-1, keepdims=True)
    inverse = lax.rsqrt(row_var + norm_epsilon)
    return (centered * inverse, inverse)


def norm_back(grad_out, normal_hat, inverse, gain):
    scaled_grad = grad_out * gain
    return inverse * (
        scaled_grad
        - jnp.mean(scaled_grad, axis=-1, keepdims=True)
        - normal_hat * jnp.mean(scaled_grad * normal_hat, axis=-1, keepdims=True)
    )


def swap(v, axis, mask):
    size = lax.axis_size(axis)
    return lax.ppermute(v, axis, [(i, i ^ mask) for i in range(size)])


def ring_order(chips):
    return list(range(0, chips, 2)) + [k for k in range(chips - 1, 0, -1) if k % 2]


def next_chip(v):
    chips = lax.axis_size("blk") // 2
    order = ring_order(chips)
    moves = [(order[k], order[(k + 1) % chips]) for k in range(chips)]
    return lax.ppermute(v, "blk", [(2 * a + c, 2 * b + c) for a, b in moves for c in range(2)])


def pick(v, index):
    return lax.dynamic_index_in_dim(v, index, 0, keepdims=False)


def put(v, part, index):
    return lax.dynamic_update_index_in_dim(v, part, index, 0)


def bits_of(size):
    return [1 << k for k in range(size.bit_length() - 1)]


def blank(shape, dtype):
    return pl.pallas_call(
        lambda out: None,
        out_shape=jax.ShapeDtypeStruct(shape, dtype),
        out_specs=pl.BlockSpec(memory_space=pl.ANY),
        name="blank",
    )()


def hold(*values):
    return lax.optimization_barrier(values)


def gather_head(v):
    size = lax.axis_size("head")
    if size == 4:
        half = v.shape[0] // 2
        one, two = swap(v, "head", 1), swap(v, "head", 2)
        low = swap(two[:half], "head", 1)
        high = swap(one[half:], "head", 2)
        return [v, one, two, jnp.concatenate([low, high], axis=0)]
    held = [v]
    for bit in bits_of(size):
        held = held + [swap(part, "head", bit) for part in held]
    return held


def scatter_head(chunk):
    size = lax.axis_size("head")
    if size == 4:
        far = chunk(3).astype(bf16)
        half = far.shape[0] // 2
        low = swap(far[:half], "head", 1)
        high = swap(far[half:], "head", 2)
        one, two = chunk(1), chunk(2)
        one = jnp.concatenate([one[:half], one[half:] + high.astype(f32)], axis=0)
        two = jnp.concatenate([two[:half] + low.astype(f32), two[half:]], axis=0)
        one = swap(one.astype(bf16), "head", 1)
        two = swap(two.astype(bf16), "head", 2)
        return chunk(0) + one.astype(f32) + two.astype(f32)
    terms = [chunk(m) for m in range(size)]
    for bit in reversed(bits_of(size)):
        terms = [
            terms[m] + swap(terms[m | bit].astype(bf16), "head", bit).astype(f32) for m in range(bit)
        ]
    return terms[0]


def exchange(pieces, axis, mine, group):
    out = pieces
    for mask in range(1, group):
        out = put(out, swap(pick(pieces, mine ^ mask), axis, mask), mine ^ mask)
    return out


def scalars(*values):
    return jnp.stack([jnp.asarray(v, jnp.int32) for v in values])


def local_call(kernel, out_shapes, scalar, *arrays, name, vmem=None):
    return pl.pallas_call(
        kernel,
        in_specs=[pl.BlockSpec(memory_space=pltpu.SMEM)]
        + [pl.BlockSpec(memory_space=pltpu.VMEM)] * len(arrays),
        out_specs=[pl.BlockSpec(memory_space=pltpu.VMEM)] * len(out_shapes),
        out_shape=[jax.ShapeDtypeStruct(shape, dtype) for shape, dtype in out_shapes],
        compiler_params=pltpu.CompilerParams(vmem_limit_bytes=vmem or vmem_small),
        name=name,
    )(scalar, *arrays)


def place(blocks, at):
    count = len(blocks)

    def kernel(at_ref, *refs):
        for k in range(count):
            refs[count][at_ref[k]] = refs[k][...]

    shape = ((count,) + blocks[0].shape, blocks[0].dtype)
    return local_call(kernel, [shape], at, *blocks, name="place")[0]


def place_halves(first, parts, low, high, at):
    count, rows, width = first.shape

    def kernel(at_ref, first_ref, *refs):
        out = refs[-1]
        for k in range(count):
            out[k, 0] = first_ref[k]
        for m in range(count - 1):
            out[at_ref[m], 1] = refs[m][...]
        out[at_ref[count - 1], 1, : rows // 2] = refs[count - 1][...]
        out[at_ref[count - 1], 1, rows // 2 :] = refs[count][...]

    shape = ((count, 2, rows, width), first.dtype)
    return local_call(kernel, [shape], at, first, *parts, low, high, name="place_halves")[0]


def pack_sums(at, first, early, up_row, d_query, d_values, n_head, n_blk, wide, w_rows):
    ff = up_row.shape[1] // n_head
    own = d_query.shape[1]
    each = own // DH

    team = DH // w_rows

    def kernel(at_ref, first_ref, *refs):
        earlies, up_ref, query_ref, value_ref, out = refs[:-4], *refs[-4:]
        vectors = [first_ref[0:1, :], first_ref[1:2, :]] + [ref[...] for ref in earlies]
        totals = [
            jnp.sum(ref[...].astype(bf16).astype(f32), axis=0, keepdims=True)
            for ref in (query_ref, value_ref)
        ]
        for h in range(n_head):
            for b in range(n_blk):
                low = (h * n_blk + b) * w_rows
                row = [v[:, low : low + w_rows] for v in vectors]
                mine = jnp.where(at_ref[0] == b, 1.0, 0.0)
                row.append(up_ref[:, h * ff : (h + 1) * ff] * mine)
                for total in totals:
                    part = jnp.zeros((1, w_rows), f32)
                    for i in range(each):
                        for k in range(team):
                            here = (at_ref[1] + i == h) & (at_ref[2] + k == b)
                            low = i * DH + k * w_rows
                            part += total[:, low : low + w_rows] * jnp.where(here, 1.0, 0.0)
                    row.append(part)
                used = sum(part.shape[1] for part in row)
                if used < wide:
                    row.append(jnp.zeros((1, wide - used), f32))
                out[h, b : b + 1, :] = jnp.concatenate(row, axis=1)

    shape = ((n_head, n_blk, wide), f32)
    return local_call(
        kernel, [shape], at, first, *early, up_row, d_query, d_values, name="pack_sums"
    )[0]


def place_cores(pieces, at):
    count = len(pieces)

    def kernel(at_ref, *refs):
        for k in range(count):
            for c in range(2):
                refs[count + c][at_ref[k]] = refs[k][c]

    shape = ((count,) + pieces[0].shape[1:], pieces[0].dtype)
    return local_call(kernel, [shape, shape], at, *pieces, name="place_cores")


def lanes(start, size):
    return pl.ds(pl.multiple_of(start, DH), size)


def split_columns(arrays, width, columns_of, core, chips, name):
    rows = arrays[0].shape[0]

    def kernel(core_ref, *refs):
        sources, (mine, other) = refs[:-2], refs[-2:]
        me = core_ref[0]
        for chip in range(chips):
            for out, index in ((mine, me), (other, 1 - me)):
                starts, run = columns_of(2 * chip + index)
                for p, source in enumerate(sources):
                    for i, start in enumerate(starts):
                        low = p * width + i * run
                        out[chip, :, low : low + run] = source[:, lanes(start, run)]

    shape = ((chips, rows, len(arrays) * width), arrays[0].dtype)
    return local_call(kernel, [shape, shape], scalars(core), *arrays, name=name)


def pair_up(mine, other, chip, core):
    chips = mine.shape[0]

    def kernel(at, mine_ref, other_ref, *outs):
        for m in range(chips):
            outs[m][at[1]] = mine_ref[at[0] ^ m]
            outs[m][1 - at[1]] = other_ref[at[0] ^ m]

    shape = ((2,) + mine.shape[1:], mine.dtype)
    return local_call(kernel, [shape] * chips, scalars(chip, core), mine, other, name="pair_up")


def swap_chips(pieces):
    return [pieces[0]] + [swap(pieces[m], "blk", 2 * m) for m in range(1, len(pieces))]


def merge_columns(pieces, count, width, columns_of, chip, name, row=None):
    chips = len(pieces)
    rows = pieces[0].shape[1] if row is None else row
    total = 2 * chips * width

    def kernel(at, *refs):
        sources, outs = refs[:chips], refs[chips:]
        sums = None
        for m in range(chips):
            for core in range(2):
                starts, run = columns_of(2 * (at[0] ^ m) + core)
                for p in range(count):
                    for i, start in enumerate(starts):
                        low = p * width + i * run
                        part = sources[m][core, :rows, low : low + run]
                        outs[p][:, lanes(start, run)] = part.astype(f32)
                if row is not None:
                    part = sources[m][core, rows:, :].astype(f32)
                    sums = part if sums is None else sums + part
        if row is not None:
            outs[count][...] = sums

    shapes = [((rows, total), f32)] * count
    if row is not None:
        shapes.append(((pieces[0].shape[1] - row, count * width), f32))
    return local_call(kernel, shapes, scalars(chip), *pieces, name=name)


def each_tile(heads, tiles, whole, body):
    for i in range(heads):
        for t in range(tiles):
            if whole:
                body(i, t)
            else:
                pl.when(pl.program_id(0) == i * tiles + t)(functools.partial(body, i, t))


def fixed_blocks(arrays):
    return [
        pl.BlockSpec(array.shape, lambda i, n=len(array.shape): (0,) * n) for array in arrays
    ]


def attend(heads_at, which, first, tok, query, keys, values, state, final):
    rows, width = query.shape
    heads, tiles, ways = width // DH, rows // tile, heads_at.shape[0]
    factor = log2_e * DH**-0.5
    carried = state is not None
    arrays = []
    for array, _ in [keys[m] for m in which] + [values[m] for m in which]:
        if not any(array is other for other in arrays):
            arrays.append(array)

    def find(entry):
        return [array is entry[0] for array in arrays].index(True), entry[1]

    def kernel(heads_ref, first_ref, query_ref, *refs):
        parts = refs[: len(arrays)]
        outs = refs[-2:]

        def body(i, t):
            lane, here = pl.ds(i * DH, DH), pl.ds(t * tile, tile)
            seen = (t + 1) * tile
            row = t * tile + lax.broadcasted_iota(jnp.int32, (tile, 1), 0)
            column = lax.broadcasted_iota(jnp.int32, (1, seen), 1)
            row = (row // tok * ways + heads_ref[0]) * tok + row % tok
            start = jnp.transpose(jnp.broadcast_to(first_ref[:, here], (DH, tile)))[:, :1]
            if carried:
                stats = refs[len(arrays) + 1]
                high = jnp.transpose(jnp.broadcast_to(stats[i, 0:1, here], (DH, tile)))[:, :1]
                total = jnp.transpose(jnp.broadcast_to(stats[i, 1:2, here], (DH, tile)))[:, :1]
                top = high
            else:
                top = jnp.full((tile, 1), masked_fill, f32)
            scores = []
            for m in which:
                k, index = find(keys[m])
                raw = times_transposed(query_ref[here, lane], parts[k][index, :seen, lane])
                pos = (column // tok * ways + heads_ref[m]) * tok + column % tok
                keep = (pos[:, t * tile :] <= row) & (pos[:, t * tile :] >= start)
                last = jnp.where(keep, raw[:, t * tile :], masked_fill)
                if t > 0:
                    rest = jnp.where(pos[:, : t * tile] >= start, raw[:, : t * tile], masked_fill)
                    last = jnp.concatenate([rest, last], axis=1)
                scores.append(last)
                top = jnp.maximum(top, jnp.max(last, axis=-1, keepdims=True))
            if carried:
                shrink = jnp.exp2((high - top) * factor)
                total, acc = total * shrink, refs[len(arrays)][here, lane] * shrink
            else:
                total, acc = jnp.zeros((tile, 1), f32), jnp.zeros((tile, DH), f32)
            for m, part in zip(which, scores):
                weights = jnp.exp2((part - top) * factor)
                total = total + jnp.sum(weights, axis=-1, keepdims=True)
                k, index = find(values[m])
                acc = acc + matmul(weights.astype(bf16), parts[k][index, :seen, lane])

            def as_row(value):
                return jnp.transpose(jnp.broadcast_to(value, (tile, DH)))[0:1, :]

            if final:
                outs[0][here, lane] = (acc / total).astype(bf16)
                outs[1][i, :, here] = as_row(top * factor + jnp.log2(total))
            else:
                outs[0][here, lane] = acc
                outs[1][i, 0:1, here] = as_row(top)
                outs[1][i, 1:2, here] = as_row(total)

        each_tile(heads, tiles, rows * len(which) <= 4096, body)

    pairs = rows * rows * len(which) * heads // 2
    operands = [first, query, *arrays, *(state if carried else [])]
    shapes = [
        jax.ShapeDtypeStruct((rows, width), bf16 if final else f32),
        jax.ShapeDtypeStruct((heads, 1 if final else 2, rows), f32),
    ]
    return pl.pallas_call(
        kernel,
        grid=(1 if rows * len(which) <= 4096 else heads * tiles,),
        in_specs=[pl.BlockSpec(memory_space=pltpu.SMEM)] + fixed_blocks(operands),
        out_specs=fixed_blocks(shapes),
        out_shape=shapes,
        compiler_params=pltpu.CompilerParams(vmem_limit_bytes=vmem_bytes),
        cost_estimate=pl.CostEstimate(
            flops=4 * pairs * DH,
            bytes_accessed=4 * rows * width * len(which),
            transcendentals=pairs,
        ),
        name="attend",
    )(heads_at, *operands)


def attend_back(heads_at, m, first, tok, log_total, delta, query, d_out, key, value, dq_in):
    rows, width = query.shape
    heads, tiles, ways = width // DH, rows // tile, heads_at.shape[0]
    factor, scaling = log2_e * DH**-0.5, DH**-0.5
    carried = dq_in is not None
    parts = [key[0]] if key[0] is value[0] else [key[0], value[0]]

    def kernel(heads_ref, first_ref, log_ref, delta_ref, query_ref, out_ref, *refs):
        keys, values = refs[0], refs[len(parts) - 1]
        dq, dk, dv = refs[-3:]

        def body(i, t):
            lane, here = pl.ds(i * DH, DH), pl.ds(t * tile, tile)
            ahead = pl.ds(t * tile, rows - t * tile)
            k_tile, v_tile = keys[key[1], here, lane], values[value[1], here, lane]
            q_part, d_part = query_ref[ahead, lane], out_ref[ahead, lane]
            scores = times_transposed(k_tile, q_part) * factor
            pos = t * tile + lax.broadcasted_iota(jnp.int32, (tile, 1), 0)
            pos = (pos // tok * ways + heads_ref[m]) * tok + pos % tok
            row = t * tile + lax.broadcasted_iota(jnp.int32, (1, tile), 1)
            row = (row // tok * ways + heads_ref[0]) * tok + row % tok
            probs = jnp.exp2(scores - log_ref[i, :, ahead])
            start = first_ref[:, ahead]
            keep = (pos >= start[:, :tile]) & (pos <= row)
            near = jnp.where(keep, probs[:, :tile], 0.0)
            if rows > (t + 1) * tile:
                far = jnp.where(pos >= start[:, tile:], probs[:, tile:], 0.0)
                probs = jnp.concatenate([near, far], axis=1)
            else:
                probs = near
            dv[here, lane] = matmul(probs.astype(bf16), d_part).astype(bf16)
            d_probs = times_transposed(v_tile, d_part)
            d_scores = (probs * (d_probs - delta_ref[i, :, ahead])).astype(bf16)
            dk[here, lane] = (scaling * matmul(d_scores, q_part)).astype(bf16)
            term = scaling * cross_rows(d_scores, k_tile)
            if t > 0:
                dq[ahead, lane] += term
            elif carried:
                dq[:, lane] = refs[len(parts)][:, lane] + term
            else:
                dq[:, lane] = term

        each_tile(heads, tiles, rows <= 1024, body)

    pairs = rows * rows * heads // 2
    operands = [first, log_total, delta, query, d_out, *parts] + ([dq_in] if carried else [])
    shapes = [jax.ShapeDtypeStruct((rows, width), kind) for kind in (f32, bf16, bf16)]
    return pl.pallas_call(
        kernel,
        grid=(1 if rows <= 1024 else heads * tiles,),
        in_specs=[pl.BlockSpec(memory_space=pltpu.SMEM)] + fixed_blocks(operands),
        out_specs=fixed_blocks(shapes),
        out_shape=shapes,
        compiler_params=pltpu.CompilerParams(vmem_limit_bytes=vmem_bytes),
        cost_estimate=pl.CostEstimate(
            flops=10 * pairs * DH, bytes_accessed=20 * rows * width, transcendentals=pairs
        ),
        name="attend_back",
    )(heads_at, *operands)


def normalized(values):
    centered = values - jnp.mean(values, axis=-1, keepdims=True)
    return centered * lax.rsqrt(jnp.mean(centered * centered, axis=-1, keepdims=True) + norm_epsilon)


def project_in(at, mine, other, gain, shift, weights, bias):
    chips, count = len(mine), len(weights)
    tok, width = mine[0].shape
    columns = weights[0].shape[2]
    own = columns // 3

    def body(at_ref, *refs):
        mine_refs, other_refs = refs[:chips], refs[chips : 2 * chips]
        gain_ref, shift_ref, bias_ref = refs[2 * chips : 2 * chips + 3]
        weight_refs = refs[2 * chips + 3 : 2 * chips + 3 + count]
        query, key_value, normed, whole = refs[2 * chips + 3 + count :]
        core = at_ref[chips]

        @pl.when(pl.program_id(0) == 0)
        def _():
            for k, part in enumerate(weight_refs):
                for z in range(chips):
                    low = pl.multiple_of(at_ref[chips + 1 + k] + z * 2 * part.shape[1], 16)
                    whole[pl.ds(low, part.shape[1]), :] = part[z]

        for step in range(chips):

            @pl.when(pl.program_id(0) == step)
            def _():
                for part, place in ((mine_refs[step], core), (other_refs[step], 1 - core)):
                    hat = normalized(part[...].astype(f32))
                    low = pl.multiple_of(place * tok, tok)
                    normed[pl.ds(low, tok), :] = (hat * gain_ref[...] + shift_ref[...]).astype(bf16)

        product = matmul(normed[...], whole[...]) + bias_ref[...]
        product = product.astype(bf16)
        query[...] = product[:, :own]
        key_value[0] = product[:, own : 2 * own]
        key_value[1] = product[:, 2 * own :]

    def fixed(shape):
        return pl.BlockSpec(shape, lambda i, at_ref: (0,) * len(shape))

    rows = 2 * tok * chips
    arrays = [*mine, *other, gain, shift, bias, *weights]
    return pl.pallas_call(
        body,
        grid_spec=pltpu.PrefetchScalarGridSpec(
            num_scalar_prefetch=1,
            grid=(chips,),
            in_specs=[fixed(array.shape) for array in arrays],
            out_specs=[
                pl.BlockSpec((2 * tok, own), lambda i, at_ref: (at_ref[i], 0)),
                pl.BlockSpec((2, 2 * tok, own), lambda i, at_ref: (0, at_ref[i], 0)),
                pl.BlockSpec((2 * tok, width), lambda i, at_ref: (at_ref[i], 0)),
                fixed((width, columns)),
            ],
        ),
        out_shape=[
            jax.ShapeDtypeStruct((rows, own), bf16),
            jax.ShapeDtypeStruct((2, rows, own), bf16),
            jax.ShapeDtypeStruct((rows, width), bf16),
            jax.ShapeDtypeStruct((width, columns), bf16),
        ],
        compiler_params=pltpu.CompilerParams(vmem_limit_bytes=vmem_bytes),
        cost_estimate=pl.CostEstimate(
            flops=2 * rows * width * columns, bytes_accessed=8 * rows * width, transcendentals=0
        ),
        name="project_in",
    )(at, *arrays)


def terms_out(at, array, weights, transposed):
    steps = at.shape[0] // 2
    rows, width = array.shape
    tok = rows // (2 * steps)
    out_width = weights.shape[0] if transposed else weights.shape[1]

    def body(at_ref, mine, other, whole, *outs):
        left = jnp.concatenate([mine[...], other[...]], axis=0)
        both = times_transposed(left, whole[...]) if transposed else matmul(left, whole[...])
        for e in (0, 1):
            outs[e][0] = both[e * tok : (e + 1) * tok].astype(bf16)

    def block(e):
        return pl.BlockSpec((tok, width), lambda i, at_ref: (at_ref[2 * i + e], 0))

    stacked = pl.BlockSpec((1, tok, out_width), lambda i, at_ref: (i, 0, 0))
    shape = jax.ShapeDtypeStruct((steps, tok, out_width), bf16)
    return pl.pallas_call(
        body,
        grid_spec=pltpu.PrefetchScalarGridSpec(
            num_scalar_prefetch=1,
            grid=(steps,),
            in_specs=[block(0), block(1), pl.BlockSpec(weights.shape, lambda i, at_ref: (0, 0))],
            out_specs=[stacked, stacked],
        ),
        out_shape=[shape, shape],
        compiler_params=pltpu.CompilerParams(vmem_limit_bytes=vmem_bytes),
        cost_estimate=pl.CostEstimate(
            flops=2 * rows * width * out_width,
            bytes_accessed=4 * rows * out_width,
            transcendentals=0,
        ),
        name="terms_out",
    )(at, array, array, weights)


def norm_sums(own, other, mine, others):
    chips, tok, width = own.shape

    def body(*refs):
        terms, pieces, out = refs[:2], refs[2 : 2 + 2 * chips], refs[-1]
        step = pl.program_id(0)

        @pl.when(step == 0)
        def _():
            out[...] = jnp.zeros_like(out)

        for k in range(chips):

            @pl.when(step == k)
            def _():
                for e in (0, 1):
                    term = terms[e][0].astype(f32)
                    hat = normalized(pieces[e * chips + k][...].astype(f32))
                    out[0:1, :] += jnp.sum(term * hat, axis=0, keepdims=True)
                    out[1:2, :] += jnp.sum(term, axis=0, keepdims=True)

    stacked = pl.BlockSpec((1, tok, width), lambda i: (i, 0, 0))
    return pl.pallas_call(
        body,
        grid=(chips,),
        in_specs=[stacked, stacked] + fixed_blocks([*mine, *others]),
        out_specs=pl.BlockSpec((2, width), lambda i: (0, 0)),
        out_shape=jax.ShapeDtypeStruct((2, width), f32),
        compiler_params=pltpu.CompilerParams(vmem_limit_bytes=vmem_bytes),
        name="norm_sums",
    )(own, other, *mine, *others)


def mix_back(at, parts, weights, mixed, earlier):
    count = len(parts)
    tok = parts[0].shape[0]
    rows, own = mixed.shape
    heads = own // DH

    def kernel(at_ref, *refs):
        whole, outs = refs[count], refs[count + 1 :]
        d_mixed = outs[2] if earlier is not None else outs[0]
        if earlier is not None:
            mixed_ref, before, _, delta = outs
            d_mixed[...] = before[...]
        for k in range(count):
            here = pl.ds(pl.multiple_of(at_ref[k] * tok, tok), tok)
            d_mixed[here, :] = times_transposed(refs[k][...], whole[...]).astype(bf16)
        if earlier is not None:
            products = d_mixed[...].astype(f32) * mixed_ref[...].astype(f32)
            for k in range(heads):
                turned = jnp.transpose(products[:, k * DH : (k + 1) * DH])
                delta[k] = jnp.sum(turned, axis=0, keepdims=True)

    shapes = [((rows, own), bf16)]
    if earlier is None:
        return local_call(kernel, shapes, at, *parts, weights, name="mix_back", vmem=vmem_bytes)[0]
    shapes.append(((heads, 1, rows), f32))
    return local_call(
        kernel, shapes, at, *parts, weights, mixed, earlier, name="mix_back", vmem=vmem_bytes
    )


def mix_grad(at, mine, other, mixed, each, team):
    chips = len(mine)
    tok, width = mine[0].shape
    own = mixed.shape[1]
    w_rows = own // (each * team)

    def kernel(at_ref, *refs):
        parts = [refs[e * chips + k] for k in range(chips) for e in (0, 1)]
        mixed_ref, out = refs[2 * chips :]
        total = None
        for k, part in enumerate(parts):
            here = pl.ds(pl.multiple_of(at_ref[k] * tok, tok), tok)
            term = cross_rows(mixed_ref[here, :], part[...])
            total = term if total is None else total + term
        total = total.astype(bf16)
        for i in range(each):
            for j in range(team):
                low = (i * team + j) * w_rows
                out[j, i] = total[low : low + w_rows]

    shape = ((team, each, w_rows, width), bf16)
    return local_call(kernel, [shape], at, *mine, *other, mixed, name="mix_grad", vmem=vmem_bytes)[0]


def reorder(array, at):
    def kernel(at_ref, source, out):
        for k in range(array.shape[0]):
            out[k] = source[at_ref[k]]

    return local_call(kernel, [(array.shape, array.dtype)], at, array, name="reorder")[0]


def local(
    tokens,
    segments,
    cotangent,
    first_gain,
    first_shift,
    query_proj,
    key_proj,
    value_proj,
    query_bias,
    value_bias,
    out_proj,
    out_bias,
    second_gain,
    second_shift,
    up_proj,
    up_bias,
    down_proj,
    down_bias,
):
    n_head, n_blk = lax.axis_size("head"), lax.axis_size("blk")
    head, blk = lax.axis_index("head"), lax.axis_index("blk")
    chips = n_blk // 2
    chip, core = blk // 2, blk % 2
    tok = tokens.shape[0]
    rows = tok * n_blk
    w_rows = query_proj.shape[0]
    ff_rows = down_proj.shape[0]
    team = DH // w_rows
    sets = n_blk // team
    each = n_head // team
    place_in = blk % team
    own_heads = each * DH

    ring = ring_order(chips)
    behind = jnp.array(
        [[ring[(ring.index(z) - k) % chips] for k in range(chips)] for z in range(chips)], jnp.int32
    )
    behind_all = pick(behind, chip)
    behind = [behind_all[k] for k in range(chips)]

    def spot(step, other):
        return (2 * behind[step] + (core ^ other)) * tok

    def fill_pair(buffer, mine, other, step):
        buffer = lax.dynamic_update_slice_in_dim(buffer, mine, spot(step, 0), 0)
        return lax.dynamic_update_slice_in_dim(buffer, other, spot(step, 1), 0)

    square = n_head == 4

    def head_columns(b):
        at = (b % team) * each
        return [((at + i) * sets + b // team) * DH for i in range(each)], DH

    def ff_columns(b):
        return [(h * n_blk + b) * ff_rows for h in range(n_head)], ff_rows

    ways, two_cores = jnp.arange(n_head, dtype=jnp.int32), jnp.arange(2, dtype=jnp.int32)
    heads_at = head ^ ways
    chips_at = chip ^ jnp.arange(chips, dtype=jnp.int32)
    blocks_at = (2 * behind_all[:, None] + (core ^ two_cores)[None, :]).reshape(-1)
    weights_at = (heads_at[:, None] * n_blk + two_cores[None, :]).reshape(-1) * w_rows
    weights_at = jnp.concatenate([behind_all, core[None], weights_at])

    with jax.named_scope("tokens_gather"):
        tok_mine, tok_other = [tokens], []
        tok_mine.append(next_chip(tokens))

    with jax.named_scope("tokens_gather"):
        tok_other.append(swap(tokens, "blk", 1))

    with jax.named_scope("vectors"):
        small = [
            first_gain,
            first_shift,
            query_bias,
            value_bias,
            out_bias,
            second_gain,
            second_shift,
            down_bias,
            up_bias,
            segments.astype(bf16),
        ]
        small = [v.reshape(-1, w_rows).astype(f32) for v in small]
        height = sum(v.shape[0] for v in small)
        above, packed = 0, 0.0
        for v in small:
            packed = packed + lax.pad(
                v, f32(0), ((above, height - above - v.shape[0], 0), (0, 0, 0))
            )
            above += v.shape[0]
        small = packed.astype(bf16)[None]
    with jax.named_scope("qkv_weights"):
        mine, other = split_columns(
            [query_proj, key_proj, value_proj], own_heads, head_columns, core, chips, "split_heads"
        )
    other, down_late = hold(other, down_proj)
    with jax.named_scope("down_weights"):
        half = ff_rows // 2
        if square:
            down_first = lax.all_gather(down_late[:half], "head", axis=0, tiled=False)
        else:
            down_first = down_proj
    with jax.named_scope("qkv_weights"):
        pieces = pair_up(mine, swap(other, "blk", 1), chip, core)

    places = (heads_at, chips_at, blocks_at, weights_at)
    pieces, small, up_proj, tok_mine, tok_other, places = hold(
        pieces, small, up_proj, tok_mine, tok_other, places
    )
    heads_at, chips_at, blocks_at, weights_at = places

    with jax.named_scope("qkv_weights"):
        pieces = swap_chips(pieces)
        fused = place_cores(pieces, chips_at)
    with jax.named_scope("vectors"):
        for bit in bits_of(n_head):
            small = jnp.concatenate([small, swap(small, "head", bit)])
        small = jnp.concatenate([small, swap(small, "blk", 1)])
        small_parts = [small]
        small_parts.append(next_chip(small))

    fused, small_parts, tok_mine, tok_other, up_proj, down_first = hold(
        fused, small_parts, tok_mine, tok_other, up_proj, down_first
    )

    def small_table():
        height, width = small_parts[0].shape[1:]
        source = jnp.concatenate(small_parts).reshape(n_head * n_blk, height * width)
        index = jnp.arange(n_head * n_blk, dtype=jnp.int32)
        from_chip = jnp.repeat(jnp.stack(behind), 2 * n_head)
        from_core = core ^ (index // n_head % 2)
        from_row = (head ^ (index % n_head)) * n_blk + 2 * from_chip + from_core
        select = (from_row[None, :] == index[:, None]).astype(bf16)
        return matmul(select, source).reshape(n_head, n_blk, height * width)

    def vector(index):
        return table[:, :, index * w_rows : (index + 1) * w_rows].reshape(1, D)

    table = None
    for step in range(1, chips - 1):
        with jax.named_scope("tokens_gather"):
            tok_mine.append(next_chip(tok_mine[step]))
        with jax.named_scope("qkv_weights"):
            if step == 1 and square:
                one = [swap(part, "head", 1) for part in fused]
                two = [swap(part, "head", 2) for part in fused]
            if step == 2 and square:
                low, high = swap(two[0], "head", 1), swap(one[1], "head", 2)
            if step == 1 and not square:
                fused_parts = [gather_head(part) for part in fused]
                fused_parts = [part[m] for m in range(n_head) for part in fused_parts]
        with jax.named_scope("vectors"):
            if len(small_parts) < chips:
                small_parts.append(next_chip(small_parts[-1]))
            elif table is None:
                table = small_table()
        if step == 1:
            with jax.named_scope("up_weights"):
                up_mine, up_other = split_columns(
                    [up_proj], n_head * ff_rows, ff_columns, core, chips, "split_up"
                )
        if step == 1:
            tok_mine, tok_other, small_parts, up_mine, up_other = hold(
                tok_mine, tok_other, small_parts, up_mine, up_other
            )
        elif step < chips - 2:
            tok_mine, small_parts = hold(tok_mine, small_parts)
    if square:
        fused_parts = [*fused, *one, *two, low, high]
    if table is None:
        with jax.named_scope("vectors"):
            table = small_table()
    with jax.named_scope("vectors"):

        def own_head_part(full):
            part = full.reshape(n_head, sets, DH)
            part = lax.dynamic_index_in_dim(part, blk // team, 1, keepdims=False)
            return lax.dynamic_slice_in_dim(part, place_in * each, each, 0).reshape(1, own_heads)

        gain_first, shift_first = vector(0), vector(1)
        q_bias, v_bias = own_head_part(vector(2)), own_head_part(vector(3))
        qkv_bias = jnp.concatenate([q_bias, jnp.zeros_like(q_bias), v_bias], axis=1)
    first_vectors = (gain_first, shift_first, qkv_bias)
    fused_parts, tok_mine, cotangent, up_other, out_proj, first_vectors = hold(
        fused_parts, tok_mine, cotangent, up_other, out_proj, first_vectors
    )
    gain_first, shift_first, qkv_bias = first_vectors

    with jax.named_scope("tokens_gather"):
        tok_other += [swap(piece, "blk", 1) for piece in tok_mine[1:]]
    with jax.named_scope("qkv"):
        query, kv, normed, qkv_w = project_in(
            weights_at,
            tok_mine,
            tok_other,
            gain_first,
            shift_first,
            fused_parts,
            qkv_bias,
        )
    with jax.named_scope("up_weights"):
        up_pieces = pair_up(up_mine, swap(up_other, "blk", 1), chip, core)
    with jax.named_scope("out_weights"):
        out_parts = [out_proj] + [swap(out_proj, "head", m) for m in range(1, n_head)]
    query, kv, up_pieces, normed, out_parts, cotangent, qkv_w, table = hold(
        query, kv, up_pieces, normed, out_parts, cotangent, qkv_w, table
    )

    with jax.named_scope("kv_gather"):
        keys, values = [(kv, 0)], [(kv, 1)]
        if square:
            kv_parts = [swap(kv, "head", 1), swap(kv, "head", 2)]
        else:
            kv_parts = gather_head(kv)[1:]
    with jax.named_scope("up_weights"):
        up_pieces = swap_chips(up_pieces)
    with jax.named_scope("vectors"):
        seq = table[:, :, 8 * w_rows + ff_rows :]
        seg_all = seq.transpose(1, 0, 2).reshape(-1)
        seg_rows = pick(seq, head).reshape(rows)
        first_pos = jnp.sum((seg_all[:, None] < seg_rows[None, :]).astype(jnp.int32), axis=0)[None]
    with jax.named_scope("attention"):
        state = attend(heads_at, [0], first_pos, tok, query, keys, values, None, False)
    kv_parts, state, up_pieces, cotangent, out_parts, first_pos = hold(
        kv_parts, state, up_pieces, cotangent, out_parts, first_pos
    )

    with jax.named_scope("dy_gather"):
        dy_all = lax.all_gather(cotangent, "blk", axis=0, tiled=True)
    with jax.named_scope("up_weights"):
        up_part = place(up_pieces, chips_at).reshape(n_blk * w_rows, n_head * ff_rows)
    with jax.named_scope("kv_gather"):
        keys += [(part, 0) for part in kv_parts]
        values += [(part, 1) for part in kv_parts]
        if square:
            low = swap(kv_parts[1][:1], "head", 1)
            high = swap(kv_parts[0][1:], "head", 2)
    with jax.named_scope("out_weights"):
        out_w = place(out_parts, heads_at).reshape(team, each, w_rows, D)
        out_w = exchange(out_w, "blk", place_in, team)
        out_w = out_w.transpose(1, 0, 2, 3).reshape(own_heads, D)
    if square:
        low, high, out_w, state, up_part, down_proj = hold(
            low, high, out_w, state, up_part, down_proj
        )
        keys.append((low, 0))
        values.append((high, 0))
    else:
        out_w, state, up_part, down_proj = hold(out_w, state, up_part, down_proj)
    with jax.named_scope("up_weights"):
        up_w = lax.all_gather(up_part, "head", axis=0, tiled=True)

    with jax.named_scope("attention"):
        left = list(range(1, n_head))
        mixed, log_total = attend(
            heads_at, left, first_pos, tok, query, keys, values, state, True
        )
    with jax.named_scope("down_weights"):
        if square:
            downs = down_proj[half:]
            downs = [downs, swap(downs, "head", 1), swap(downs, "head", 2)]
        else:
            downs = gather_head(down_proj)
    mixed, out_w, table, downs = hold(mixed, out_w, table, downs)

    def cross(term):
        return (term[0], swap(term[1], "blk", 1))

    def onward(pair, moving):
        return next_chip(sum_of(pair, moving).astype(bf16))

    def sum_of(pair, moving):
        total = pair[0].astype(f32) + pair[1].astype(f32)
        return total if moving is None else total + moving.astype(f32)

    def met(own, other):
        return (own, swap(other, "blk", 1))

    def entry(pair, step):
        return (pair[0][step], pair[1][step])

    with jax.named_scope("branch"):
        ready = met(*terms_out(blocks_at, mixed, out_w, False))
        ready, dy_all = hold(ready, dy_all)
        moving = None
        for step in range(1, chips):
            moving = onward(entry(ready, step), moving)
            with jax.named_scope("vectors"):
                if step == 1:
                    o_bias, gain_second, shift_second, d_bias = [vector(k) for k in range(4, 8)]
                    u_bias = table[:, :, 8 * w_rows : 8 * w_rows + ff_rows]
                    u_bias = lax.dynamic_index_in_dim(u_bias, blk, 1, keepdims=False)
                    vectors = (o_bias, gain_second, shift_second, d_bias, u_bias.reshape(1, -1))
            with jax.named_scope("down_weights"):
                if square and step == 2:
                    low = swap(downs[2][: half // 2], "head", 1)
                    high = swap(downs[1][half // 2 :], "head", 2)
                if not square and step == 1:
                    down_w = place(downs, heads_at).reshape(n_head * ff_rows, D)
            if step == 1:
                moving, ready, vectors = hold(moving, ready, vectors)
                o_bias, gain_second, shift_second, d_bias, u_bias = vectors
            elif square and step == 2:
                moving, ready, low, high = hold(moving, ready, low, high)
            else:
                moving, ready = hold(moving, ready)
        own = tokens.astype(f32)
        hidden = own + (sum_of(entry(ready, 0), moving) + o_bias)
        hat_second, inv_second = norm_parts(hidden)
        second_own = (hat_second * gain_second + shift_second).astype(bf16)
    hidden, second_own, inv_second = hold(hidden, second_own, inv_second)

    with jax.named_scope("down_weights"):
        if square:
            down_w = place_halves(down_first, downs, low, high, heads_at)
            down_w = down_w.reshape(n_head * ff_rows, D)

    with jax.named_scope("mlp"):
        second_all = blank((rows, D), bf16)
        active_all = blank((rows, n_head * ff_rows), bf16)
        d_upper_all = blank((rows, n_head * ff_rows), bf16)
        sec_mine, sec_other = [second_own], []
        terms = {}

        def mlp_chunk(step, second_all, active_all, d_upper_all):
            base = 2 * behind[step] * tok

            def chunk_of(array):
                return lax.dynamic_slice_in_dim(array, base, 2 * tok, 0)

            def fill(buffer, chunk):
                return lax.dynamic_update_slice_in_dim(buffer, chunk, base, 0)

            second_all = fill_pair(second_all, sec_mine[step], sec_other[step], step)
            upper = matmul(chunk_of(second_all), up_w) + u_bias
            phi = 0.5 * (1.0 + lax.erf(upper * 0.7071067811865476))
            active = (upper * phi).astype(bf16)
            slope = phi + upper * jnp.exp(-0.5 * upper * upper) * 0.3989422804014327
            d_active = times_transposed(chunk_of(dy_all), down_w)
            d_upper = (d_active * slope).astype(bf16)
            terms[step] = [
                times_transposed(
                    lax.dynamic_slice_in_dim(d_upper, (core ^ other) * tok, tok, 0), up_w
                ).astype(bf16)
                for other in (0, 1)
            ]
            return second_all, fill(active_all, active), fill(d_upper_all, d_upper)

        for step in range(chips):
            if step < chips - 1:
                sec_mine.append(next_chip(sec_mine[step]))
            if step > 0:
                second_all, active_all, d_upper_all = mlp_chunk(
                    step - 1, second_all, active_all, d_upper_all
                )
                if step == chips - 1:
                    ready = cross(terms[1])
            sec_other.append(swap(sec_mine[step], "blk", 1))
            ready, sec_mine, sec_other, terms, second_all, active_all, d_upper_all = hold(
                ready, sec_mine, sec_other, terms, second_all, active_all, d_upper_all
            )
        moving = None
        for step in range(1, chips):
            moving = onward(ready, moving)
            if step == 1:
                second_all, active_all, d_upper_all = mlp_chunk(
                    chips - 1, second_all, active_all, d_upper_all
                )
            ready = cross(terms[(step + 1) % chips])
            if step == 2:
                with jax.named_scope("up_grad"):
                    up_term = cross_rows(second_all, d_upper_all).astype(bf16)
                moving, ready, terms, active_all, d_upper_all, up_term = hold(
                    moving, ready, terms, active_all, d_upper_all, up_term
                )
            elif step == 3:
                with jax.named_scope("down_grad"):
                    down_term = cross_rows(active_all, dy_all).astype(bf16)
                moving, ready, terms, down_term, active_all = hold(
                    moving, ready, terms, down_term, active_all
                )
            else:
                moving, ready, terms, second_all, active_all, d_upper_all = hold(
                    moving, ready, terms, second_all, active_all, d_upper_all
                )
        d_second = sum_of(ready, moving)
        upstream = cotangent.astype(f32)
        d_hidden = upstream + norm_back(d_second, hat_second, inv_second, gain_second)
        d_branch_own = d_hidden.astype(bf16)

    def sum_heads(terms):
        return lax.psum_scatter(terms, "head", scatter_dimension=0, tiled=True)

    with jax.named_scope("up_grad"):
        up_sum = sum_heads(up_term)
    d_hidden, d_branch_own, active_all, d_second, d_upper_all, hat_second, cotangent = hold(
        d_hidden, d_branch_own, active_all, d_second, d_upper_all, hat_second, cotangent
    )
    mine, other = [d_branch_own], []

    with jax.named_scope("d_branch_gather"):
        half = tok // 2
        halves = [[d_branch_own[:half]], [d_branch_own[half:]]]
        with jax.named_scope("output"):
            out_term = matmul(active_all, down_w).astype(bf16)
        for step in range(chips - 1):
            for chain in halves:
                if step > 0:
                    (held,) = hold(chain[step])
                    chain[step] = held
                chain.append(next_chip(chain[step]))
            if step > 0:
                mine.append(jnp.concatenate([chain[step] for chain in halves], axis=0))
        mine.append(jnp.concatenate([chain[-1] for chain in halves], axis=0))
        with jax.named_scope("vector_grads"):
            early = [
                jnp.sum(d_branch_own.astype(f32), axis=0, keepdims=True),
                jnp.sum(d_second * hat_second, axis=0, keepdims=True),
                jnp.sum(d_second, axis=0, keepdims=True),
                jnp.sum(cotangent.astype(f32), axis=0, keepdims=True),
                jnp.sum(d_upper_all.astype(f32), axis=0, keepdims=True),
            ]
        mine, up_sum, out_term, early = hold(mine, up_sum, out_term, early)
        with jax.named_scope("output"):
            out_sum = lax.psum_scatter(out_term, "blk", scatter_dimension=0, tiled=True)
        other = [swap(piece, "blk", 1) for piece in mine]
        by_core = blocks_at.reshape(chips, 2)
        d_mixed = mix_back(by_core[:, 0], mine, out_w, mixed, None)
        d_mixed, delta = mix_back(by_core[:, 1], other, out_w, mixed, d_mixed)
    with jax.named_scope("up_grad"):
        up_sum = up_sum.reshape(chips, 2, w_rows, n_head * ff_rows)
        up_mine = lax.dynamic_index_in_dim(up_sum, core, 1, keepdims=False)
        up_other = lax.dynamic_index_in_dim(up_sum, 1 - core, 1, keepdims=False)
        up_pieces = pair_up(up_mine, swap(up_other, "blk", 1), chip, core)
    d_mixed, delta, mine, other = hold(d_mixed, delta, mine, other)

    dq = None

    def kv_grad(m):
        return attend_back(
            heads_at, m, first_pos, tok, log_total, delta, query, d_mixed, keys[m], values[m], dq
        )

    d_keys, d_values = {}, {}
    for m in reversed(range(n_head)):
        with jax.named_scope("attention_back"):
            if square and m == 2:
                low = swap(d_keys[3], "head", 1)
                high = swap(d_values[3], "head", 2)
            if square and m == 0:
                one = [d_keys[1], (d_values[1].astype(f32) + high.astype(f32)).astype(bf16)]
                two = [(d_keys[2].astype(f32) + low.astype(f32)).astype(bf16), d_values[2]]
                one, two, dq, up_pieces = hold(one, two, dq, up_pieces)
                one[0], two[0] = swap(one[0], "head", 1), swap(two[0], "head", 2)
            dq, d_keys[m], d_values[m] = kv_grad(m)
        if square and m == 1:
            low, high, dq, d_keys, d_values, d_mixed = hold(
                low, high, dq, d_keys, d_values, d_mixed
            )
        elif m > 0:
            dq, d_keys, d_values, d_mixed = hold(dq, d_keys, d_values, d_mixed)
    with jax.named_scope("up_grad"):
        up_pieces = swap_chips(up_pieces)
    if square:
        one, two, dq, mine, other, mixed, out_sum, down_term = hold(
            one, two, dq, mine, other, mixed, out_sum, down_term
        )
        with jax.named_scope("attention_back"):
            one[1], two[1] = swap(one[1], "head", 1), swap(two[1], "head", 2)
    with jax.named_scope("out_grad"):
        mix_term = mix_grad(blocks_at, mine, other, mixed, each, team)
    with jax.named_scope("down_grad"):
        down_grad = sum_heads(down_term)
    with jax.named_scope("attention_back"):
        if square:
            d_keys, d_values = [
                (total[0].astype(f32) + one[k].astype(f32) + two[k].astype(f32)).astype(bf16)
                for k, total in enumerate((d_keys, d_values))
            ]
        else:
            d_keys, d_values = [
                scatter_head(lambda m: total[m].astype(f32)).astype(bf16)
                for total in (d_keys, d_values)
            ]
        d_qkv = jnp.concatenate([dq.astype(bf16), d_keys, d_values], axis=1)
    d_qkv, up_pieces, mix_term = hold(d_qkv, up_pieces, mix_term)

    slab, wide = n_blk * w_rows, 3 * own_heads
    with jax.named_scope("d_normed"):
        own_terms, other_terms = terms_out(blocks_at, d_qkv, qkv_w, True)
        ready = met(own_terms, other_terms)
    ready, normed, d_qkv, mix_term, up_pieces = hold(ready, normed, d_qkv, mix_term, up_pieces)
    moving = None
    for step in range(1, chips):
        with jax.named_scope("d_normed"):
            moving = onward(entry(ready, step), moving)
        if step == 1:
            with jax.named_scope("qkv_grad"):
                qkv_term = cross_rows(normed, d_qkv).astype(bf16).reshape(n_head, slab, wide)
            late = (other_terms, mix_term, tok_mine, tok_other, dq, d_values)
            moving, ready, qkv_term, late = hold(moving, ready, qkv_term, late)
            other_terms, mix_term, tok_mine, tok_other, dq, d_values = late
        elif step == 2:
            with jax.named_scope("qkv_grad"):
                if square:
                    half = slab // 2
                    far = pick(qkv_term, head ^ 3)
                    low, high = swap(far[:half], "head", 1), swap(far[half:], "head", 2)
                else:
                    low = high = qkv_term
            with jax.named_scope("out_grad"):
                mix_term = exchange(mix_term, "blk", place_in, team)
            moving, ready, low, high, mix_term = hold(moving, ready, low, high, mix_term)
        elif step == 3:
            with jax.named_scope("qkv_grad"):
                if square:
                    one, two = pick(qkv_term, head ^ 1), pick(qkv_term, head ^ 2)
                    one = jnp.concatenate([one[:half], one[half:] + high])
                    two = jnp.concatenate([two[:half] + low, two[half:]])
                    one, two = swap(one, "head", 1), swap(two, "head", 2)
            with jax.named_scope("vector_grads"):
                first_sums = norm_sums(ready[0], other_terms, tok_mine, tok_other)
                parts = pack_sums(
                    scalars(blk, place_in * each, blk - place_in),
                    first_sums,
                    early[:4],
                    early[4],
                    dq,
                    d_values,
                    n_head,
                    n_blk,
                    wide,
                    w_rows,
                )
            moving, ready, parts, mix_term, down_grad = hold(
                moving, ready, parts, mix_term, down_grad
            )
        else:
            moving, ready = hold(moving, ready)
    deep = 1
    with jax.named_scope("out_grad"):
        out_grad = sum_heads(mix_term.reshape(n_head * w_rows, D))
    with jax.named_scope("vector_grads"):
        sums = scatter_head(lambda m: pick(parts, head ^ m))
        sums = sums.astype(bf16)
    with jax.named_scope("qkv_grad"):
        if square:
            qkv_grad = pick(qkv_term, head).astype(f32) + one.astype(f32) + two.astype(f32)
        else:
            qkv_grad = scatter_head(lambda m: pick(qkv_term, head ^ m).astype(f32))
        qkv_grad = qkv_grad.astype(bf16).reshape(chips, 2, w_rows, wide)
        extra = sums.reshape(chips, 2, deep, wide)
        extra = jnp.pad(extra, ((0, 0), (0, 0), (0, -deep % 16), (0, 0)))
        qkv_grad = jnp.concatenate([qkv_grad, extra], axis=2)
        qkv_mine = lax.dynamic_index_in_dim(qkv_grad, core, 1, keepdims=False)
        qkv_other = lax.dynamic_index_in_dim(qkv_grad, 1 - core, 1, keepdims=False)
        pieces = pair_up(qkv_mine, swap(qkv_other, "blk", 1), chip, core)
    pieces, up_pieces, down_grad, out_sum, moving = hold(
        pieces, up_pieces, down_grad, out_sum, moving
    )
    with jax.named_scope("qkv_grad"):
        pieces = swap_chips(pieces)
    with jax.named_scope("d_normed"):
        d_normed = sum_of(entry(ready, 0), moving)
        hat_first, inv_first = norm_parts(own)
        tokens_grad = (d_hidden + norm_back(d_normed, hat_first, inv_first, gain_first)).astype(bf16)
    with jax.named_scope("output"):
        output = (hidden + (out_sum.astype(f32) + d_bias)).astype(bf16)
    with jax.named_scope("up_grad"):
        (up_grad,) = merge_columns(up_pieces, 1, n_head * ff_rows, ff_columns, chip, "merge_up")
    with jax.named_scope("down_grad"):
        down_grad = down_grad.astype(f32)
    with jax.named_scope("qkv_grad"):
        *qkv_grad, sums = merge_columns(
            pieces, 3, own_heads, head_columns, chip, "merge_heads", row=w_rows
        )
    with jax.named_scope("vector_grads"):
        sums = sums[:deep].reshape(-1)
        cuts = [sums[i * w_rows : (i + 1) * w_rows] for i in range(6)]
        up_bias_grad = sums[6 * w_rows : 6 * w_rows + ff_rows]
        rest = sums[6 * w_rows + ff_rows : 8 * w_rows + ff_rows]

    return (
        output,
        tokens_grad,
        cuts[0],
        cuts[1],
        qkv_grad[0],
        qkv_grad[1],
        qkv_grad[2],
        rest[:w_rows],
        rest[w_rows:],
        out_grad.astype(f32),
        cuts[2],
        cuts[3],
        cuts[4],
        up_grad,
        up_bias_grad,
        down_grad,
        cuts[5],
    )


def solution(mesh):
    by_token = P(("blk", "head"), None)
    matrix = P(("head", "blk"), None)
    vector = P(("head", "blk"))
    return jax.shard_map(
        local,
        mesh=mesh,
        in_specs=(
            by_token,
            P(("blk", "head")),
            by_token,
            vector,
            vector,
            matrix,
            matrix,
            matrix,
            vector,
            vector,
            matrix,
            vector,
            vector,
            vector,
            matrix,
            vector,
            matrix,
            vector,
        ),
        out_specs=(
            by_token,
            by_token,
            vector,
            vector,
            matrix,
            matrix,
            matrix,
            vector,
            vector,
            matrix,
            vector,
            vector,
            vector,
            matrix,
            vector,
            matrix,
            vector,
        ),
        check_vma=False,
    )
```

```python
import functools

import jax
import jax.numpy as jnp
from jax import lax
from jax.experimental import pallas as pl
from jax.experimental.pallas import tpu as pltpu
from jax.sharding import PartitionSpec as P

D = 2048
H = 16
DH = 128

norm_epsilon = 1e-05
masked_fill = -1e30
tile = 256
bf16 = jnp.bfloat16
f32 = jnp.float32
log2_e = 1.4426950408889634
vmem_bytes = 58 * 1024 * 1024
vmem_small = 20 * 1024 * 1024


def matmul(left, right):
    return jnp.dot(left, right, preferred_element_type=f32)


def cross_rows(left, right):
    return lax.dot_general(left, right, (((0,), (0,)), ((), ())), preferred_element_type=f32)


def times_transposed(left, right):
    return lax.dot_general(left, right, (((1,), (1,)), ((), ())), preferred_element_type=f32)


def norm_parts(values):
    row_mean = jnp.mean(values, axis=-1, keepdims=True)
    centered = values - row_mean
    row_var = jnp.mean(centered * centered, axis=-1, keepdims=True)
    inverse = lax.rsqrt(row_var + norm_epsilon)
    return (centered * inverse, inverse)


def norm_back(grad_out, normal_hat, inverse, gain):
    scaled_grad = grad_out * gain
    return inverse * (
        scaled_grad
        - jnp.mean(scaled_grad, axis=-1, keepdims=True)
        - normal_hat * jnp.mean(scaled_grad * normal_hat, axis=-1, keepdims=True)
    )


def swap(v, axis, mask):
    size = lax.axis_size(axis)
    return lax.ppermute(v, axis, [(i, i ^ mask) for i in range(size)])


def ring_order(chips):
    return list(range(0, chips, 2)) + [k for k in range(chips - 1, 0, -1) if k % 2]


def next_chip(v):
    chips = lax.axis_size("blk") // 2
    order = ring_order(chips)
    moves = [(order[k], order[(k + 1) % chips]) for k in range(chips)]
    return lax.ppermute(v, "blk", [(2 * a + c, 2 * b + c) for a, b in moves for c in range(2)])


def pick(v, index):
    return lax.dynamic_index_in_dim(v, index, 0, keepdims=False)


def put(v, part, index):
    return lax.dynamic_update_index_in_dim(v, part, index, 0)


def bits_of(size):
    return [1 << k for k in range(size.bit_length() - 1)]


def blank(shape, dtype):
    return pl.pallas_call(
        lambda out: None,
        out_shape=jax.ShapeDtypeStruct(shape, dtype),
        out_specs=pl.BlockSpec(memory_space=pl.ANY),
        name="blank",
    )()


def hold(*values):
    return lax.optimization_barrier(values)


def gather_head(v):
    size = lax.axis_size("head")
    if size == 4:
        half = v.shape[0] // 2
        one, two = swap(v, "head", 1), swap(v, "head", 2)
        low = swap(two[:half], "head", 1)
        high = swap(one[half:], "head", 2)
        return [v, one, two, jnp.concatenate([low, high], axis=0)]
    held = [v]
    for bit in bits_of(size):
        held = held + [swap(part, "head", bit) for part in held]
    return held


def scatter_head(chunk):
    size = lax.axis_size("head")
    if size == 4:
        far = chunk(3).astype(bf16)
        half = far.shape[0] // 2
        low = swap(far[:half], "head", 1)
        high = swap(far[half:], "head", 2)
        one, two = chunk(1), chunk(2)
        one = jnp.concatenate([one[:half], one[half:] + high.astype(f32)], axis=0)
        two = jnp.concatenate([two[:half] + low.astype(f32), two[half:]], axis=0)
        one = swap(one.astype(bf16), "head", 1)
        two = swap(two.astype(bf16), "head", 2)
        return chunk(0) + one.astype(f32) + two.astype(f32)
    terms = [chunk(m) for m in range(size)]
    for bit in reversed(bits_of(size)):
        terms = [
            terms[m] + swap(terms[m | bit].astype(bf16), "head", bit).astype(f32) for m in range(bit)
        ]
    return terms[0]


def exchange(pieces, axis, mine, group):
    out = pieces
    for mask in range(1, group):
        out = put(out, swap(pick(pieces, mine ^ mask), axis, mask), mine ^ mask)
    return out


def scalars(*values):
    return jnp.stack([jnp.asarray(v, jnp.int32) for v in values])


def local_call(kernel, out_shapes, scalar, *arrays, name, vmem=None):
    return pl.pallas_call(
        kernel,
        in_specs=[pl.BlockSpec(memory_space=pltpu.SMEM)]
        + [pl.BlockSpec(memory_space=pltpu.VMEM)] * len(arrays),
        out_specs=[pl.BlockSpec(memory_space=pltpu.VMEM)] * len(out_shapes),
        out_shape=[jax.ShapeDtypeStruct(shape, dtype) for shape, dtype in out_shapes],
        compiler_params=pltpu.CompilerParams(vmem_limit_bytes=vmem or vmem_small),
        name=name,
    )(scalar, *arrays)


def place(blocks, at):
    count = len(blocks)

    def kernel(at_ref, *refs):
        for k in range(count):
            refs[count][at_ref[k]] = refs[k][...]

    shape = ((count,) + blocks[0].shape, blocks[0].dtype)
    return local_call(kernel, [shape], at, *blocks, name="place")[0]


def place_halves(first, parts, low, high, at):
    count, rows, width = first.shape

    def kernel(at_ref, first_ref, *refs):
        out = refs[-1]
        for k in range(count):
            out[k, 0] = first_ref[k]
        for m in range(count - 1):
            out[at_ref[m], 1] = refs[m][...]
        out[at_ref[count - 1], 1, : rows // 2] = refs[count - 1][...]
        out[at_ref[count - 1], 1, rows // 2 :] = refs[count][...]

    shape = ((count, 2, rows, width), first.dtype)
    return local_call(kernel, [shape], at, first, *parts, low, high, name="place_halves")[0]


def pack_sums(at, first, early, up_row, d_query, d_values, n_head, n_blk, wide, w_rows):
    ff = up_row.shape[1] // n_head
    own = d_query.shape[1]
    each = own // DH

    team = DH // w_rows

    def kernel(at_ref, first_ref, *refs):
        earlies, up_ref, query_ref, value_ref, out = refs[:-4], *refs[-4:]
        vectors = [first_ref[0:1, :], first_ref[1:2, :]] + [ref[...] for ref in earlies]
        totals = [
            jnp.sum(ref[...].astype(bf16).astype(f32), axis=0, keepdims=True)
            for ref in (query_ref, value_ref)
        ]
        for h in range(n_head):
            for b in range(n_blk):
                low = (h * n_blk + b) * w_rows
                row = [v[:, low : low + w_rows] for v in vectors]
                mine = jnp.where(at_ref[0] == b, 1.0, 0.0)
                row.append(up_ref[:, h * ff : (h + 1) * ff] * mine)
                for total in totals:
                    part = jnp.zeros((1, w_rows), f32)
                    for i in range(each):
                        for k in range(team):
                            here = (at_ref[1] + i == h) & (at_ref[2] + k == b)
                            low = i * DH + k * w_rows
                            part += total[:, low : low + w_rows] * jnp.where(here, 1.0, 0.0)
                    row.append(part)
                used = sum(part.shape[1] for part in row)
                if used < wide:
                    row.append(jnp.zeros((1, wide - used), f32))
                out[h, b : b + 1, :] = jnp.concatenate(row, axis=1)

    shape = ((n_head, n_blk, wide), f32)
    return local_call(
        kernel, [shape], at, first, *early, up_row, d_query, d_values, name="pack_sums"
    )[0]


def place_cores(pieces, at):
    count = len(pieces)

    def kernel(at_ref, *refs):
        for k in range(count):
            for c in range(2):
                refs[count + c][at_ref[k]] = refs[k][c]

    shape = ((count,) + pieces[0].shape[1:], pieces[0].dtype)
    return local_call(kernel, [shape, shape], at, *pieces, name="place_cores")


def lanes(start, size):
    return pl.ds(pl.multiple_of(start, DH), size)


def split_columns(arrays, width, columns_of, core, chips, name):
    rows = arrays[0].shape[0]

    def kernel(core_ref, *refs):
        sources, (mine, other) = refs[:-2], refs[-2:]
        me = core_ref[0]
        for chip in range(chips):
            for out, index in ((mine, me), (other, 1 - me)):
                starts, run = columns_of(2 * chip + index)
                for p, source in enumerate(sources):
                    for i, start in enumerate(starts):
                        low = p * width + i * run
                        out[chip, :, low : low + run] = source[:, lanes(start, run)]

    shape = ((chips, rows, len(arrays) * width), arrays[0].dtype)
    return local_call(kernel, [shape, shape], scalars(core), *arrays, name=name)


def pair_up(mine, other, chip, core):
    chips = mine.shape[0]

    def kernel(at, mine_ref, other_ref, *outs):
        for m in range(chips):
            outs[m][at[1]] = mine_ref[at[0] ^ m]
            outs[m][1 - at[1]] = other_ref[at[0] ^ m]

    shape = ((2,) + mine.shape[1:], mine.dtype)
    return local_call(kernel, [shape] * chips, scalars(chip, core), mine, other, name="pair_up")


def swap_chips(pieces):
    return [pieces[0]] + [swap(pieces[m], "blk", 2 * m) for m in range(1, len(pieces))]


def merge_columns(pieces, count, width, columns_of, chip, name, row=None):
    chips = len(pieces)
    rows = pieces[0].shape[1] if row is None else row
    total = 2 * chips * width

    def kernel(at, *refs):
        sources, outs = refs[:chips], refs[chips:]
        sums = None
        for m in range(chips):
            for core in range(2):
                starts, run = columns_of(2 * (at[0] ^ m) + core)
                for p in range(count):
                    for i, start in enumerate(starts):
                        low = p * width + i * run
                        part = sources[m][core, :rows, low : low + run]
                        outs[p][:, lanes(start, run)] = part.astype(f32)
                if row is not None:
                    part = sources[m][core, rows:, :].astype(f32)
                    sums = part if sums is None else sums + part
        if row is not None:
            outs[count][...] = sums

    shapes = [((rows, total), f32)] * count
    if row is not None:
        shapes.append(((pieces[0].shape[1] - row, count * width), f32))
    return local_call(kernel, shapes, scalars(chip), *pieces, name=name)


def each_tile(heads, tiles, whole, body):
    for i in range(heads):
        for t in range(tiles):
            if whole:
                body(i, t)
            else:
                pl.when(pl.program_id(0) == i * tiles + t)(functools.partial(body, i, t))


def fixed_blocks(arrays):
    return [
        pl.BlockSpec(array.shape, lambda i, n=len(array.shape): (0,) * n) for array in arrays
    ]


def attend(heads_at, which, first, tok, query, keys, values, state, final):
    rows, width = query.shape
    heads, tiles, ways = width // DH, rows // tile, heads_at.shape[0]
    factor = log2_e * DH**-0.5
    carried = state is not None
    arrays = []
    for array, _ in [keys[m] for m in which] + [values[m] for m in which]:
        if not any(array is other for other in arrays):
            arrays.append(array)

    def find(entry):
        return [array is entry[0] for array in arrays].index(True), entry[1]

    def kernel(heads_ref, first_ref, query_ref, *refs):
        parts = refs[: len(arrays)]
        outs = refs[-2:]

        def body(i, t):
            lane, here = pl.ds(i * DH, DH), pl.ds(t * tile, tile)
            seen = (t + 1) * tile
            row = t * tile + lax.broadcasted_iota(jnp.int32, (tile, 1), 0)
            column = lax.broadcasted_iota(jnp.int32, (1, seen), 1)
            row = (row // tok * ways + heads_ref[0]) * tok + row % tok
            start = jnp.transpose(jnp.broadcast_to(first_ref[:, here], (DH, tile)))[:, :1]
            if carried:
                stats = refs[len(arrays) + 1]
                high = jnp.transpose(jnp.broadcast_to(stats[i, 0:1, here], (DH, tile)))[:, :1]
                total = jnp.transpose(jnp.broadcast_to(stats[i, 1:2, here], (DH, tile)))[:, :1]
                top = high
            else:
                top = jnp.full((tile, 1), masked_fill, f32)
            scores = []
            for m in which:
                k, index = find(keys[m])
                raw = times_transposed(query_ref[here, lane], parts[k][index, :seen, lane])
                pos = (column // tok * ways + heads_ref[m]) * tok + column % tok
                keep = (pos[:, t * tile :] <= row) & (pos[:, t * tile :] >= start)
                last = jnp.where(keep, raw[:, t * tile :], masked_fill)
                if t > 0:
                    rest = jnp.where(pos[:, : t * tile] >= start, raw[:, : t * tile], masked_fill)
                    last = jnp.concatenate([rest, last], axis=1)
                scores.append(last)
                top = jnp.maximum(top, jnp.max(last, axis=-1, keepdims=True))
            if carried:
                shrink = jnp.exp2((high - top) * factor)
                total, acc = total * shrink, refs[len(arrays)][here, lane] * shrink
            else:
                total, acc = jnp.zeros((tile, 1), f32), jnp.zeros((tile, DH), f32)
            for m, part in zip(which, scores):
                weights = jnp.exp2((part - top) * factor)
                total = total + jnp.sum(weights, axis=-1, keepdims=True)
                k, index = find(values[m])
                acc = acc + matmul(weights.astype(bf16), parts[k][index, :seen, lane])

            def as_row(value):
                return jnp.transpose(jnp.broadcast_to(value, (tile, DH)))[0:1, :]

            if final:
                outs[0][here, lane] = (acc / total).astype(bf16)
                outs[1][i, :, here] = as_row(top * factor + jnp.log2(total))
            else:
                outs[0][here, lane] = acc
                outs[1][i, 0:1, here] = as_row(top)
                outs[1][i, 1:2, here] = as_row(total)

        each_tile(heads, tiles, rows * len(which) <= 4096, body)

    pairs = rows * rows * len(which) * heads // 2
    operands = [first, query, *arrays, *(state if carried else [])]
    shapes = [
        jax.ShapeDtypeStruct((rows, width), bf16 if final else f32),
        jax.ShapeDtypeStruct((heads, 1 if final else 2, rows), f32),
    ]
    return pl.pallas_call(
        kernel,
        grid=(1 if rows * len(which) <= 4096 else heads * tiles,),
        in_specs=[pl.BlockSpec(memory_space=pltpu.SMEM)] + fixed_blocks(operands),
        out_specs=fixed_blocks(shapes),
        out_shape=shapes,
        compiler_params=pltpu.CompilerParams(vmem_limit_bytes=vmem_bytes),
        cost_estimate=pl.CostEstimate(
            flops=4 * pairs * DH,
            bytes_accessed=4 * rows * width * len(which),
            transcendentals=pairs,
        ),
        name="attend",
    )(heads_at, *operands)


def attend_back(heads_at, m, first, tok, log_total, delta, query, d_out, key, value, dq_in):
    rows, width = query.shape
    heads, tiles, ways = width // DH, rows // tile, heads_at.shape[0]
    factor, scaling = log2_e * DH**-0.5, DH**-0.5
    carried = dq_in is not None
    parts = [key[0]] if key[0] is value[0] else [key[0], value[0]]

    def kernel(heads_ref, first_ref, log_ref, delta_ref, query_ref, out_ref, *refs):
        keys, values = refs[0], refs[len(parts) - 1]
        dq, dk, dv = refs[-3:]

        def body(i, t):
            lane, here = pl.ds(i * DH, DH), pl.ds(t * tile, tile)
            ahead = pl.ds(t * tile, rows - t * tile)
            k_tile, v_tile = keys[key[1], here, lane], values[value[1], here, lane]
            q_part, d_part = query_ref[ahead, lane], out_ref[ahead, lane]
            scores = times_transposed(k_tile, q_part) * factor
            pos = t * tile + lax.broadcasted_iota(jnp.int32, (tile, 1), 0)
            pos = (pos // tok * ways + heads_ref[m]) * tok + pos % tok
            row = t * tile + lax.broadcasted_iota(jnp.int32, (1, tile), 1)
            row = (row // tok * ways + heads_ref[0]) * tok + row % tok
            probs = jnp.exp2(scores - log_ref[i, :, ahead])
            start = first_ref[:, ahead]
            keep = (pos >= start[:, :tile]) & (pos <= row)
            near = jnp.where(keep, probs[:, :tile], 0.0)
            if rows > (t + 1) * tile:
                far = jnp.where(pos >= start[:, tile:], probs[:, tile:], 0.0)
                probs = jnp.concatenate([near, far], axis=1)
            else:
                probs = near
            dv[here, lane] = matmul(probs.astype(bf16), d_part).astype(bf16)
            d_probs = times_transposed(v_tile, d_part)
            d_scores = (probs * (d_probs - delta_ref[i, :, ahead])).astype(bf16)
            dk[here, lane] = (scaling * matmul(d_scores, q_part)).astype(bf16)
            term = scaling * cross_rows(d_scores, k_tile)
            if t > 0:
                dq[ahead, lane] += term
            elif carried:
                dq[:, lane] = refs[len(parts)][:, lane] + term
            else:
                dq[:, lane] = term

        each_tile(heads, tiles, rows <= 1024, body)

    pairs = rows * rows * heads // 2
    operands = [first, log_total, delta, query, d_out, *parts] + ([dq_in] if carried else [])
    shapes = [jax.ShapeDtypeStruct((rows, width), kind) for kind in (f32, bf16, bf16)]
    return pl.pallas_call(
        kernel,
        grid=(1 if rows <= 1024 else heads * tiles,),
        in_specs=[pl.BlockSpec(memory_space=pltpu.SMEM)] + fixed_blocks(operands),
        out_specs=fixed_blocks(shapes),
        out_shape=shapes,
        compiler_params=pltpu.CompilerParams(vmem_limit_bytes=vmem_bytes),
        cost_estimate=pl.CostEstimate(
            flops=10 * pairs * DH, bytes_accessed=20 * rows * width, transcendentals=pairs
        ),
        name="attend_back",
    )(heads_at, *operands)


def normalized(values):
    centered = values - jnp.mean(values, axis=-1, keepdims=True)
    return centered * lax.rsqrt(jnp.mean(centered * centered, axis=-1, keepdims=True) + norm_epsilon)


def project_in(at, mine, other, gain, shift, weights, bias):
    chips, count = len(mine), len(weights)
    tok, width = mine[0].shape
    columns = weights[0].shape[2]
    own = columns // 3

    def body(at_ref, *refs):
        mine_refs, other_refs = refs[:chips], refs[chips : 2 * chips]
        gain_ref, shift_ref, bias_ref = refs[2 * chips : 2 * chips + 3]
        weight_refs = refs[2 * chips + 3 : 2 * chips + 3 + count]
        query, key_value, normed, whole = refs[2 * chips + 3 + count :]
        core = at_ref[chips]

        @pl.when(pl.program_id(0) == 0)
        def _():
            for k, part in enumerate(weight_refs):
                for z in range(chips):
                    low = pl.multiple_of(at_ref[chips + 1 + k] + z * 2 * part.shape[1], 16)
                    whole[pl.ds(low, part.shape[1]), :] = part[z]

        for step in range(chips):

            @pl.when(pl.program_id(0) == step)
            def _():
                for part, place in ((mine_refs[step], core), (other_refs[step], 1 - core)):
                    hat = normalized(part[...].astype(f32))
                    low = pl.multiple_of(place * tok, tok)
                    normed[pl.ds(low, tok), :] = (hat * gain_ref[...] + shift_ref[...]).astype(bf16)

        product = matmul(normed[...], whole[...]) + bias_ref[...]
        product = product.astype(bf16)
        query[...] = product[:, :own]
        key_value[0] = product[:, own : 2 * own]
        key_value[1] = product[:, 2 * own :]

    def fixed(shape):
        return pl.BlockSpec(shape, lambda i, at_ref: (0,) * len(shape))

    rows = 2 * tok * chips
    arrays = [*mine, *other, gain, shift, bias, *weights]
    return pl.pallas_call(
        body,
        grid_spec=pltpu.PrefetchScalarGridSpec(
            num_scalar_prefetch=1,
            grid=(chips,),
            in_specs=[fixed(array.shape) for array in arrays],
            out_specs=[
                pl.BlockSpec((2 * tok, own), lambda i, at_ref: (at_ref[i], 0)),
                pl.BlockSpec((2, 2 * tok, own), lambda i, at_ref: (0, at_ref[i], 0)),
                pl.BlockSpec((2 * tok, width), lambda i, at_ref: (at_ref[i], 0)),
                fixed((width, columns)),
            ],
        ),
        out_shape=[
            jax.ShapeDtypeStruct((rows, own), bf16),
            jax.ShapeDtypeStruct((2, rows, own), bf16),
            jax.ShapeDtypeStruct((rows, width), bf16),
            jax.ShapeDtypeStruct((width, columns), bf16),
        ],
        compiler_params=pltpu.CompilerParams(vmem_limit_bytes=vmem_bytes),
        cost_estimate=pl.CostEstimate(
            flops=2 * rows * width * columns, bytes_accessed=8 * rows * width, transcendentals=0
        ),
        name="project_in",
    )(at, *arrays)


def terms_out(at, array, weights, transposed):
    steps = at.shape[0] // 2
    rows, width = array.shape
    tok = rows // (2 * steps)
    out_width = weights.shape[0] if transposed else weights.shape[1]
    run = out_width // 4

    def body(at_ref, source, part, mine, other, held):
        @pl.when(pl.program_id(0) == 0)
        def _():
            for k in range(2 * steps):
                low = pl.multiple_of(at_ref[k] * tok, tok)
                row = (k % 2) * (rows // 2) + (k // 2) * tok
                held[row : row + tok, :] = source[pl.ds(low, tok), :]

        for e, out in ((1, other), (0, mine)):
            left = held[e * (rows // 2) : (e + 1) * (rows // 2), :]
            term = (times_transposed if transposed else matmul)(left, part[...])
            out[...] = term.astype(bf16).reshape(steps, tok, run)

    stacked = pl.BlockSpec((steps, tok, run), lambda i, at_ref: (0, 0, i))
    shape = jax.ShapeDtypeStruct((steps, tok, out_width), bf16)
    if transposed:
        part = pl.BlockSpec((run, width), lambda i, at_ref: (i, 0))
    else:
        part = pl.BlockSpec((width, run), lambda i, at_ref: (0, i))
    return pl.pallas_call(
        body,
        grid_spec=pltpu.PrefetchScalarGridSpec(
            num_scalar_prefetch=1,
            grid=(4,),
            in_specs=[pl.BlockSpec((rows, width), lambda i, at_ref: (0, 0)), part],
            out_specs=[stacked, stacked],
            scratch_shapes=[pltpu.VMEM((rows, width), bf16)],
        ),
        out_shape=[shape, shape],
        compiler_params=pltpu.CompilerParams(vmem_limit_bytes=vmem_bytes),
        cost_estimate=pl.CostEstimate(
            flops=2 * rows * width * out_width,
            bytes_accessed=4 * rows * out_width,
            transcendentals=0,
        ),
        name="terms_out",
    )(at, array, weights)


def norm_sums(own, other, mine, others):
    chips, tok, width = own.shape

    def body(*refs):
        terms, pieces, out = refs[:2], refs[2 : 2 + 2 * chips], refs[-1]
        step = pl.program_id(0)

        @pl.when(step == 0)
        def _():
            out[...] = jnp.zeros_like(out)

        for k in range(chips):

            @pl.when(step == k)
            def _():
                for e in (0, 1):
                    term = terms[e][0].astype(f32)
                    hat = normalized(pieces[e * chips + k][...].astype(f32))
                    out[0:1, :] += jnp.sum(term * hat, axis=0, keepdims=True)
                    out[1:2, :] += jnp.sum(term, axis=0, keepdims=True)

    stacked = pl.BlockSpec((1, tok, width), lambda i: (i, 0, 0))
    return pl.pallas_call(
        body,
        grid=(chips,),
        in_specs=[stacked, stacked] + fixed_blocks([*mine, *others]),
        out_specs=pl.BlockSpec((2, width), lambda i: (0, 0)),
        out_shape=jax.ShapeDtypeStruct((2, width), f32),
        compiler_params=pltpu.CompilerParams(vmem_limit_bytes=vmem_bytes),
        name="norm_sums",
    )(own, other, *mine, *others)


def mix_back(at, parts, weights, mixed, earlier):
    count = len(parts)
    tok = parts[0].shape[0]
    rows, own = mixed.shape
    heads = own // DH

    def kernel(at_ref, *refs):
        whole, outs = refs[count], refs[count + 1 :]
        d_mixed = outs[2] if earlier is not None else outs[0]
        if earlier is not None:
            mixed_ref, before, _, delta = outs
            d_mixed[...] = before[...]
        for k in range(count):
            here = pl.ds(pl.multiple_of(at_ref[k] * tok, tok), tok)
            d_mixed[here, :] = times_transposed(refs[k][...], whole[...]).astype(bf16)
        if earlier is not None:
            products = d_mixed[...].astype(f32) * mixed_ref[...].astype(f32)
            for k in range(heads):
                turned = jnp.transpose(products[:, k * DH : (k + 1) * DH])
                delta[k] = jnp.sum(turned, axis=0, keepdims=True)

    shapes = [((rows, own), bf16)]
    if earlier is None:
        return local_call(kernel, shapes, at, *parts, weights, name="mix_back", vmem=vmem_bytes)[0]
    shapes.append(((heads, 1, rows), f32))
    return local_call(
        kernel, shapes, at, *parts, weights, mixed, earlier, name="mix_back", vmem=vmem_bytes
    )


def mix_grad(at, mine, other, mixed, each, team):
    chips = len(mine)
    tok, width = mine[0].shape
    own = mixed.shape[1]
    w_rows = own // (each * team)

    def kernel(at_ref, *refs):
        parts = [refs[e * chips + k] for k in range(chips) for e in (0, 1)]
        mixed_ref, out = refs[2 * chips :]
        total = None
        for k, part in enumerate(parts):
            here = pl.ds(pl.multiple_of(at_ref[k] * tok, tok), tok)
            term = cross_rows(mixed_ref[here, :], part[...])
            total = term if total is None else total + term
        total = total.astype(bf16)
        for i in range(each):
            for j in range(team):
                low = (i * team + j) * w_rows
                out[j, i] = total[low : low + w_rows]

    shape = ((team, each, w_rows, width), bf16)
    return local_call(kernel, [shape], at, *mine, *other, mixed, name="mix_grad", vmem=vmem_bytes)[0]


def reorder(array, at):
    def kernel(at_ref, source, out):
        for k in range(array.shape[0]):
            out[k] = source[at_ref[k]]

    return local_call(kernel, [(array.shape, array.dtype)], at, array, name="reorder")[0]


def local(
    tokens,
    segments,
    cotangent,
    first_gain,
    first_shift,
    query_proj,
    key_proj,
    value_proj,
    query_bias,
    value_bias,
    out_proj,
    out_bias,
    second_gain,
    second_shift,
    up_proj,
    up_bias,
    down_proj,
    down_bias,
):
    n_head, n_blk = lax.axis_size("head"), lax.axis_size("blk")
    head, blk = lax.axis_index("head"), lax.axis_index("blk")
    chips = n_blk // 2
    chip, core = blk // 2, blk % 2
    tok = tokens.shape[0]
    rows = tok * n_blk
    w_rows = query_proj.shape[0]
    ff_rows = down_proj.shape[0]
    team = DH // w_rows
    sets = n_blk // team
    each = n_head // team
    place_in = blk % team
    own_heads = each * DH

    ring = ring_order(chips)
    behind = jnp.array(
        [[ring[(ring.index(z) - k) % chips] for k in range(chips)] for z in range(chips)], jnp.int32
    )
    behind_all = pick(behind, chip)
    behind = [behind_all[k] for k in range(chips)]

    def spot(step, other):
        return (2 * behind[step] + (core ^ other)) * tok

    def fill_pair(buffer, mine, other, step):
        buffer = lax.dynamic_update_slice_in_dim(buffer, mine, spot(step, 0), 0)
        return lax.dynamic_update_slice_in_dim(buffer, other, spot(step, 1), 0)

    square = n_head == 4

    def head_columns(b):
        at = (b % team) * each
        return [((at + i) * sets + b // team) * DH for i in range(each)], DH

    def ff_columns(b):
        return [(h * n_blk + b) * ff_rows for h in range(n_head)], ff_rows

    ways, two_cores = jnp.arange(n_head, dtype=jnp.int32), jnp.arange(2, dtype=jnp.int32)
    heads_at = head ^ ways
    chips_at = chip ^ jnp.arange(chips, dtype=jnp.int32)
    blocks_at = (2 * behind_all[:, None] + (core ^ two_cores)[None, :]).reshape(-1)
    weights_at = (heads_at[:, None] * n_blk + two_cores[None, :]).reshape(-1) * w_rows
    weights_at = jnp.concatenate([behind_all, core[None], weights_at])

    with jax.named_scope("tokens_gather"):
        tok_mine, tok_other = [tokens], []
        tok_mine.append(next_chip(tokens))

    with jax.named_scope("tokens_gather"):
        tok_other.append(swap(tokens, "blk", 1))

    with jax.named_scope("vectors"):
        small = [
            first_gain,
            first_shift,
            query_bias,
            value_bias,
            out_bias,
            second_gain,
            second_shift,
            down_bias,
            up_bias,
            segments.astype(bf16),
        ]
        small = [v.reshape(-1, w_rows).astype(f32) for v in small]
        height = sum(v.shape[0] for v in small)
        above, packed = 0, 0.0
        for v in small:
            packed = packed + lax.pad(
                v, f32(0), ((above, height - above - v.shape[0], 0), (0, 0, 0))
            )
            above += v.shape[0]
        small = packed.astype(bf16)[None]
    with jax.named_scope("qkv_weights"):
        mine, other = split_columns(
            [query_proj, key_proj, value_proj], own_heads, head_columns, core, chips, "split_heads"
        )
    other, down_late = hold(other, down_proj)
    with jax.named_scope("down_weights"):
        half = ff_rows // 2
        if square:
            down_first = lax.all_gather(down_late[:half], "head", axis=0, tiled=False)
        else:
            down_first = down_proj
    with jax.named_scope("qkv_weights"):
        pieces = pair_up(mine, swap(other, "blk", 1), chip, core)

    places = (heads_at, chips_at, blocks_at, weights_at)
    pieces, small, up_proj, tok_mine, tok_other, places = hold(
        pieces, small, up_proj, tok_mine, tok_other, places
    )
    heads_at, chips_at, blocks_at, weights_at = places

    with jax.named_scope("qkv_weights"):
        pieces = swap_chips(pieces)
        fused = place_cores(pieces, chips_at)
    with jax.named_scope("vectors"):
        for bit in bits_of(n_head):
            small = jnp.concatenate([small, swap(small, "head", bit)])
        small = jnp.concatenate([small, swap(small, "blk", 1)])
        for bit in bits_of(chips)[:1]:
            small = jnp.concatenate([small, swap(small, "blk", 2 * bit)])

    fused, small, tok_mine, tok_other, up_proj, down_first = hold(
        fused, small, tok_mine, tok_other, up_proj, down_first
    )

    def small_table():
        height, width = small.shape[1:]
        source = small.reshape(n_head * n_blk, height * width)
        index = jnp.arange(n_head * n_blk, dtype=jnp.int32)
        from_chip = chip ^ (index // (2 * n_head))
        from_core = core ^ (index // n_head % 2)
        from_row = (head ^ (index % n_head)) * n_blk + 2 * from_chip + from_core
        select = (from_row[None, :] == index[:, None]).astype(bf16)
        return matmul(select, source).reshape(n_head, n_blk, height * width)

    def vector(index):
        return table[:, :, index * w_rows : (index + 1) * w_rows].reshape(1, D)

    for step in range(1, chips - 1):
        with jax.named_scope("tokens_gather"):
            tok_mine.append(next_chip(tok_mine[step]))
            tok_other.append(swap(tok_mine[step], "blk", 1))
        with jax.named_scope("qkv_weights"):
            if step == 1 and square:
                one = [swap(part, "head", 1) for part in fused]
                two = [swap(part, "head", 2) for part in fused]
            if step == 2 and square:
                low, high = swap(two[0], "head", 1), swap(one[1], "head", 2)
            if step == 1 and not square:
                fused_parts = [gather_head(part) for part in fused]
                fused_parts = [part[m] for m in range(n_head) for part in fused_parts]
        if step == chips - 2:
            with jax.named_scope("vectors"):
                for bit in bits_of(chips)[1:]:
                    small = jnp.concatenate([small, swap(small, "blk", 2 * bit)])
        if step == 1:
            with jax.named_scope("up_weights"):
                up_mine, up_other = split_columns(
                    [up_proj], n_head * ff_rows, ff_columns, core, chips, "split_up"
                )
        if step == 1:
            tok_mine, tok_other, up_mine, up_other, small = hold(
                tok_mine, tok_other, up_mine, up_other, small
            )
        elif step < chips - 2:
            tok_mine, small = hold(tok_mine, small)
    if square:
        fused_parts = [*fused, *one, *two, low, high]
    with jax.named_scope("vectors"):
        table = small_table()
    with jax.named_scope("vectors"):

        def own_head_part(full):
            part = full.reshape(n_head, sets, DH)
            part = lax.dynamic_index_in_dim(part, blk // team, 1, keepdims=False)
            return lax.dynamic_slice_in_dim(part, place_in * each, each, 0).reshape(1, own_heads)

        gain_first, shift_first = vector(0), vector(1)
        q_bias, v_bias = own_head_part(vector(2)), own_head_part(vector(3))
        qkv_bias = jnp.concatenate([q_bias, jnp.zeros_like(q_bias), v_bias], axis=1)
    first_vectors = (gain_first, shift_first, qkv_bias)
    fused_parts, tok_mine, tok_other, cotangent, up_other, out_proj, first_vectors = hold(
        fused_parts, tok_mine, tok_other, cotangent, up_other, out_proj, first_vectors
    )
    gain_first, shift_first, qkv_bias = first_vectors

    with jax.named_scope("tokens_gather"):
        tok_other.append(swap(tok_mine[chips - 1], "blk", 1))
    with jax.named_scope("qkv"):
        query, kv, normed, qkv_w = project_in(
            weights_at,
            tok_mine,
            tok_other,
            gain_first,
            shift_first,
            fused_parts,
            qkv_bias,
        )
    with jax.named_scope("up_weights"):
        up_pieces = pair_up(up_mine, swap(up_other, "blk", 1), chip, core)
    with jax.named_scope("out_weights"):
        out_parts = [out_proj] + [swap(out_proj, "head", m) for m in range(1, n_head)]
    query, kv, up_pieces, normed, out_parts, cotangent, qkv_w, table = hold(
        query, kv, up_pieces, normed, out_parts, cotangent, qkv_w, table
    )

    with jax.named_scope("kv_gather"):
        keys, values = [(kv, 0)], [(kv, 1)]
        if square:
            kv_parts = [swap(kv, "head", 1), swap(kv, "head", 2)]
        else:
            kv_parts = gather_head(kv)[1:]
    with jax.named_scope("up_weights"):
        up_pieces = swap_chips(up_pieces)
    with jax.named_scope("vectors"):
        seq = table[:, :, 8 * w_rows + ff_rows :]
        seg_all = seq.transpose(1, 0, 2).reshape(-1)
        seg_rows = pick(seq, head).reshape(rows)
        first_pos = jnp.sum((seg_all[:, None] < seg_rows[None, :]).astype(jnp.int32), axis=0)[None]
    with jax.named_scope("attention"):
        state = attend(heads_at, [0], first_pos, tok, query, keys, values, None, False)
    if square:
        down_second = down_proj[half:]
    else:
        down_second = down_proj
    kv_parts, state, up_pieces, cotangent, out_parts, first_pos, down_second = hold(
        kv_parts, state, up_pieces, cotangent, out_parts, first_pos, down_second
    )

    with jax.named_scope("dy_gather"):
        dy_all = lax.all_gather(cotangent, "blk", axis=0, tiled=True)
    with jax.named_scope("up_weights"):
        up_part = place(up_pieces, chips_at).reshape(n_blk * w_rows, n_head * ff_rows)
    with jax.named_scope("kv_gather"):
        keys += [(part, 0) for part in kv_parts]
        values += [(part, 1) for part in kv_parts]
        if square:
            low = swap(kv_parts[1][:1], "head", 1)
            high = swap(kv_parts[0][1:], "head", 2)
    with jax.named_scope("out_weights"):
        out_w = place(out_parts, heads_at).reshape(team, each, w_rows, D)
        out_w = exchange(out_w, "blk", place_in, team)
        out_w = out_w.transpose(1, 0, 2, 3).reshape(own_heads, D)
    if square:
        low, high, out_w, state, up_part, down_second = hold(
            low, high, out_w, state, up_part, down_second
        )
        keys.append((low, 0))
        values.append((high, 0))
    else:
        out_w, state, up_part, down_second = hold(out_w, state, up_part, down_second)
    with jax.named_scope("up_weights"):
        up_w = lax.all_gather(up_part, "head", axis=0, tiled=True)

    with jax.named_scope("attention"):
        left = list(range(1, n_head))
        mixed, log_total = attend(
            heads_at, left, first_pos, tok, query, keys, values, state, True
        )
    with jax.named_scope("down_weights"):
        if square:
            downs = [down_second, swap(down_second, "head", 1), swap(down_second, "head", 2)]
        else:
            downs = gather_head(down_second)
    mixed, out_w, table, downs = hold(mixed, out_w, table, downs)

    def cross(term):
        return (term[0], swap(term[1], "blk", 1))

    def onward(pair, moving):
        return next_chip(sum_of(pair, moving).astype(bf16))

    def sum_of(pair, moving):
        total = pair[0].astype(f32) + pair[1].astype(f32)
        return total if moving is None else total + moving.astype(f32)

    def met(own, other):
        return (own, swap(other, "blk", 1))

    def entry(pair, step):
        return (pair[0][step], pair[1][step])

    with jax.named_scope("branch"):
        ready = met(*terms_out(blocks_at, mixed, out_w, False))
        (ready,) = hold(ready)
        moving = None
        for step in range(1, chips):
            moving = onward(entry(ready, step), moving)
            with jax.named_scope("vectors"):
                if step == 1:
                    o_bias, gain_second, shift_second, d_bias = [vector(k) for k in range(4, 8)]
                    u_bias = table[:, :, 8 * w_rows : 8 * w_rows + ff_rows]
                    u_bias = lax.dynamic_index_in_dim(u_bias, blk, 1, keepdims=False)
                    vectors = (o_bias, gain_second, shift_second, d_bias, u_bias.reshape(1, -1))
            with jax.named_scope("down_weights"):
                if square and step == 2:
                    low = swap(downs[2][: half // 2], "head", 1)
                    high = swap(downs[1][half // 2 :], "head", 2)
                if not square and step == 1:
                    down_w = place(downs, heads_at).reshape(n_head * ff_rows, D)
            if step == 1:
                moving, ready, vectors, dy_all = hold(moving, ready, vectors, dy_all)
                o_bias, gain_second, shift_second, d_bias, u_bias = vectors
            elif square and step == 2:
                moving, ready, low, high = hold(moving, ready, low, high)
            else:
                moving, ready = hold(moving, ready)
        own = tokens.astype(f32)
        hidden = own + (sum_of(entry(ready, 0), moving) + o_bias)
        hat_second, inv_second = norm_parts(hidden)
        second_own = (hat_second * gain_second + shift_second).astype(bf16)
    hidden, second_own, inv_second = hold(hidden, second_own, inv_second)

    with jax.named_scope("down_weights"):
        if square:
            down_w = place_halves(down_first, downs, low, high, heads_at)
            down_w = down_w.reshape(n_head * ff_rows, D)

    with jax.named_scope("mlp"):
        second_all = blank((rows, D), bf16)
        active_all = blank((rows, n_head * ff_rows), bf16)
        d_upper_all = blank((rows, n_head * ff_rows), bf16)
        sec_mine, sec_other = [second_own], []
        terms = {}

        def mlp_chunk(step, second_all, active_all, d_upper_all):
            base = 2 * behind[step] * tok

            def chunk_of(array):
                return lax.dynamic_slice_in_dim(array, base, 2 * tok, 0)

            def fill(buffer, chunk):
                return lax.dynamic_update_slice_in_dim(buffer, chunk, base, 0)

            second_all = fill_pair(second_all, sec_mine[step], sec_other[step], step)
            upper = matmul(chunk_of(second_all), up_w) + u_bias
            phi = 0.5 * (1.0 + lax.erf(upper * 0.7071067811865476))
            active = (upper * phi).astype(bf16)
            slope = phi + upper * jnp.exp(-0.5 * upper * upper) * 0.3989422804014327
            d_active = times_transposed(chunk_of(dy_all), down_w)
            d_upper = (d_active * slope).astype(bf16)
            terms[step] = [
                times_transposed(
                    lax.dynamic_slice_in_dim(d_upper, (core ^ other) * tok, tok, 0), up_w
                ).astype(bf16)
                for other in (0, 1)
            ]
            return second_all, fill(active_all, active), fill(d_upper_all, d_upper)

        for step in range(chips):
            if step < chips - 1:
                sec_mine.append(next_chip(sec_mine[step]))
            if step > 0:
                second_all, active_all, d_upper_all = mlp_chunk(
                    step - 1, second_all, active_all, d_upper_all
                )
                if step == chips - 1:
                    ready = cross(terms[1])
            sec_other.append(swap(sec_mine[step], "blk", 1))
            ready, sec_mine, sec_other, terms, second_all, active_all, d_upper_all = hold(
                ready, sec_mine, sec_other, terms, second_all, active_all, d_upper_all
            )
        moving = None
        for step in range(1, chips):
            moving = onward(ready, moving)
            if step == 1:
                second_all, active_all, d_upper_all = mlp_chunk(
                    chips - 1, second_all, active_all, d_upper_all
                )
            ready = cross(terms[(step + 1) % chips])
            if step == 2:
                with jax.named_scope("up_grad"):
                    up_term = cross_rows(second_all, d_upper_all).astype(bf16)
                moving, ready, terms, active_all, d_upper_all, up_term = hold(
                    moving, ready, terms, active_all, d_upper_all, up_term
                )
            elif step == 3:
                with jax.named_scope("down_grad"):
                    down_term = cross_rows(active_all, dy_all).astype(bf16)
                moving, ready, terms, down_term, active_all = hold(
                    moving, ready, terms, down_term, active_all
                )
            else:
                moving, ready, terms, second_all, active_all, d_upper_all = hold(
                    moving, ready, terms, second_all, active_all, d_upper_all
                )
        d_second = sum_of(ready, moving)
        upstream = cotangent.astype(f32)
        d_hidden = upstream + norm_back(d_second, hat_second, inv_second, gain_second)
        d_branch_own = d_hidden.astype(bf16)

    def sum_heads(terms):
        return lax.psum_scatter(terms, "head", scatter_dimension=0, tiled=True)

    with jax.named_scope("up_grad"):
        up_sum = sum_heads(up_term)
    d_hidden, d_branch_own, active_all, d_second, d_upper_all, hat_second, cotangent = hold(
        d_hidden, d_branch_own, active_all, d_second, d_upper_all, hat_second, cotangent
    )
    mine, other = [d_branch_own], []

    with jax.named_scope("d_branch_gather"):
        half = tok // 2
        halves = [[d_branch_own[:half]], [d_branch_own[half:]]]
        with jax.named_scope("output"):
            out_term = matmul(active_all, down_w).astype(bf16)
        for step in range(chips - 1):
            for chain in halves:
                if step > 0:
                    (held,) = hold(chain[step])
                    chain[step] = held
                chain.append(next_chip(chain[step]))
            if step > 0:
                mine.append(jnp.concatenate([chain[step] for chain in halves], axis=0))
        mine.append(jnp.concatenate([chain[-1] for chain in halves], axis=0))
        with jax.named_scope("vector_grads"):
            early = [
                jnp.sum(d_branch_own.astype(f32), axis=0, keepdims=True),
                jnp.sum(d_second * hat_second, axis=0, keepdims=True),
                jnp.sum(d_second, axis=0, keepdims=True),
                jnp.sum(cotangent.astype(f32), axis=0, keepdims=True),
                jnp.sum(d_upper_all.astype(f32), axis=0, keepdims=True),
            ]
        mine, up_sum, out_term, early = hold(mine, up_sum, out_term, early)
        with jax.named_scope("output"):
            out_sum = lax.psum_scatter(out_term, "blk", scatter_dimension=0, tiled=True)
        other = [swap(piece, "blk", 1) for piece in mine]
        by_core = blocks_at.reshape(chips, 2)
        d_mixed = mix_back(by_core[:, 0], mine, out_w, mixed, None)
        d_mixed, delta = mix_back(by_core[:, 1], other, out_w, mixed, d_mixed)
    d_mixed, delta, mine, other = hold(d_mixed, delta, mine, other)

    dq = None

    def kv_grad(m):
        return attend_back(
            heads_at, m, first_pos, tok, log_total, delta, query, d_mixed, keys[m], values[m], dq
        )

    d_keys, d_values = {}, {}
    for m in reversed(range(n_head)):
        with jax.named_scope("attention_back"):
            if square and m == 2:
                low = swap(d_keys[3], "head", 1)
                high = swap(d_values[3], "head", 2)
            if square and m == 0:
                one = [d_keys[1], (d_values[1].astype(f32) + high.astype(f32)).astype(bf16)]
                two = [(d_keys[2].astype(f32) + low.astype(f32)).astype(bf16), d_values[2]]
                one, two, dq, up_sum = hold(one, two, dq, up_sum)
                one[0], two[0] = swap(one[0], "head", 1), swap(two[0], "head", 2)
            dq, d_keys[m], d_values[m] = kv_grad(m)
        if square and m == 1:
            low, high, dq, d_keys, d_values, d_mixed = hold(
                low, high, dq, d_keys, d_values, d_mixed
            )
        elif m > 0:
            dq, d_keys, d_values, d_mixed = hold(dq, d_keys, d_values, d_mixed)
    with jax.named_scope("up_grad"):
        up_sum = up_sum.reshape(chips, 2, w_rows, n_head * ff_rows)
        up_mine = lax.dynamic_index_in_dim(up_sum, core, 1, keepdims=False)
        up_other = lax.dynamic_index_in_dim(up_sum, 1 - core, 1, keepdims=False)
        up_pieces = pair_up(up_mine, swap(up_other, "blk", 1), chip, core)
    if square:
        one, two, dq, mine, other, mixed, out_sum, down_term, up_pieces = hold(
            one, two, dq, mine, other, mixed, out_sum, down_term, up_pieces
        )
    with jax.named_scope("up_grad"):
        up_pieces = swap_chips(up_pieces)
    if square:
        with jax.named_scope("attention_back"):
            one[1], two[1] = swap(one[1], "head", 1), swap(two[1], "head", 2)
    with jax.named_scope("out_grad"):
        mix_term = mix_grad(blocks_at, mine, other, mixed, each, team)
    with jax.named_scope("down_grad"):
        down_grad = sum_heads(down_term)
    with jax.named_scope("attention_back"):
        if square:
            d_keys, d_values = [
                (total[0].astype(f32) + one[k].astype(f32) + two[k].astype(f32)).astype(bf16)
                for k, total in enumerate((d_keys, d_values))
            ]
        else:
            d_keys, d_values = [
                scatter_head(lambda m: total[m].astype(f32)).astype(bf16)
                for total in (d_keys, d_values)
            ]
        d_qkv = jnp.concatenate([dq.astype(bf16), d_keys, d_values], axis=1)
    d_qkv, up_pieces, mix_term = hold(d_qkv, up_pieces, mix_term)

    slab, wide = n_blk * w_rows, 3 * own_heads
    with jax.named_scope("d_normed"):
        own_terms, other_terms = terms_out(blocks_at, d_qkv, qkv_w, True)
        ready = met(own_terms, other_terms)
    ready, normed, d_qkv, mix_term, up_pieces = hold(ready, normed, d_qkv, mix_term, up_pieces)
    moving = None
    for step in range(1, chips):
        with jax.named_scope("d_normed"):
            moving = onward(entry(ready, step), moving)
        if step == 1:
            with jax.named_scope("qkv_grad"):
                qkv_term = cross_rows(normed, d_qkv).astype(bf16).reshape(n_head, slab, wide)
            late = (other_terms, mix_term, tok_mine, tok_other, dq, d_values)
            moving, ready, qkv_term, late = hold(moving, ready, qkv_term, late)
            other_terms, mix_term, tok_mine, tok_other, dq, d_values = late
        elif step == 2:
            with jax.named_scope("qkv_grad"):
                if square:
                    half = slab // 2
                    far = pick(qkv_term, head ^ 3)
                    low, high = swap(far[:half], "head", 1), swap(far[half:], "head", 2)
                else:
                    low = high = qkv_term
            with jax.named_scope("out_grad"):
                mix_term = exchange(mix_term, "blk", place_in, team)
            moving, ready, low, high, mix_term = hold(moving, ready, low, high, mix_term)
        elif step == 3:
            with jax.named_scope("qkv_grad"):
                if square:
                    one, two = pick(qkv_term, head ^ 1), pick(qkv_term, head ^ 2)
                    one = jnp.concatenate([one[:half], one[half:] + high])
                    two = jnp.concatenate([two[:half] + low, two[half:]])
                    one, two = swap(one, "head", 1), swap(two, "head", 2)
            with jax.named_scope("vector_grads"):
                first_sums = norm_sums(ready[0], other_terms, tok_mine, tok_other)
                parts = pack_sums(
                    scalars(blk, place_in * each, blk - place_in),
                    first_sums,
                    early[:4],
                    early[4],
                    dq,
                    d_values,
                    n_head,
                    n_blk,
                    wide,
                    w_rows,
                )
            moving, ready, parts, mix_term, down_grad = hold(
                moving, ready, parts, mix_term, down_grad
            )
        else:
            moving, ready = hold(moving, ready)
    deep = 1
    with jax.named_scope("out_grad"):
        out_grad = sum_heads(mix_term.reshape(n_head * w_rows, D))
    with jax.named_scope("vector_grads"):
        sums = scatter_head(lambda m: pick(parts, head ^ m))
        sums = sums.astype(bf16)
    with jax.named_scope("qkv_grad"):
        if square:
            qkv_grad = pick(qkv_term, head).astype(f32) + one.astype(f32) + two.astype(f32)
        else:
            qkv_grad = scatter_head(lambda m: pick(qkv_term, head ^ m).astype(f32))
        qkv_grad = qkv_grad.astype(bf16).reshape(chips, 2, w_rows, wide)
        extra = sums.reshape(chips, 2, deep, wide)
        extra = jnp.pad(extra, ((0, 0), (0, 0), (0, -deep % 16), (0, 0)))
        qkv_grad = jnp.concatenate([qkv_grad, extra], axis=2)
        qkv_mine = lax.dynamic_index_in_dim(qkv_grad, core, 1, keepdims=False)
        qkv_other = lax.dynamic_index_in_dim(qkv_grad, 1 - core, 1, keepdims=False)
        pieces = pair_up(qkv_mine, swap(qkv_other, "blk", 1), chip, core)
    pieces, up_pieces, down_grad, out_sum, moving = hold(
        pieces, up_pieces, down_grad, out_sum, moving
    )
    with jax.named_scope("qkv_grad"):
        pieces = swap_chips(pieces)
    with jax.named_scope("d_normed"):
        d_normed = sum_of(entry(ready, 0), moving)
        hat_first, inv_first = norm_parts(own)
        tokens_grad = (d_hidden + norm_back(d_normed, hat_first, inv_first, gain_first)).astype(bf16)
    with jax.named_scope("output"):
        output = (hidden + (out_sum.astype(f32) + d_bias)).astype(bf16)
    with jax.named_scope("up_grad"):
        (up_grad,) = merge_columns(up_pieces, 1, n_head * ff_rows, ff_columns, chip, "merge_up")
    with jax.named_scope("down_grad"):
        down_grad = down_grad.astype(f32)
    with jax.named_scope("qkv_grad"):
        *qkv_grad, sums = merge_columns(
            pieces, 3, own_heads, head_columns, chip, "merge_heads", row=w_rows
        )
    with jax.named_scope("vector_grads"):
        sums = sums[:deep].reshape(-1)
        cuts = [sums[i * w_rows : (i + 1) * w_rows] for i in range(6)]
        up_bias_grad = sums[6 * w_rows : 6 * w_rows + ff_rows]
        rest = sums[6 * w_rows + ff_rows : 8 * w_rows + ff_rows]

    return (
        output,
        tokens_grad,
        cuts[0],
        cuts[1],
        qkv_grad[0],
        qkv_grad[1],
        qkv_grad[2],
        rest[:w_rows],
        rest[w_rows:],
        out_grad.astype(f32),
        cuts[2],
        cuts[3],
        cuts[4],
        up_grad,
        up_bias_grad,
        down_grad,
        cuts[5],
    )


def solution(mesh):
    by_token = P(("blk", "head"), None)
    matrix = P(("head", "blk"), None)
    vector = P(("head", "blk"))
    return jax.shard_map(
        local,
        mesh=mesh,
        in_specs=(
            by_token,
            P(("blk", "head")),
            by_token,
            vector,
            vector,
            matrix,
            matrix,
            matrix,
            vector,
            vector,
            matrix,
            vector,
            vector,
            vector,
            matrix,
            vector,
            matrix,
            vector,
        ),
        out_specs=(
            by_token,
            by_token,
            vector,
            vector,
            matrix,
            matrix,
            matrix,
            vector,
            vector,
            matrix,
            vector,
            vector,
            vector,
            matrix,
            vector,
            matrix,
            vector,
        ),
        check_vma=False,
    )
```

```python
import functools

import jax
import jax.numpy as jnp
from jax import lax
from jax.experimental import pallas as pl
from jax.experimental.pallas import tpu as pltpu
from jax.sharding import PartitionSpec as P

D = 2048
H = 16
DH = 128

norm_epsilon = 1e-05
masked_fill = -1e30
tile = 256
bf16 = jnp.bfloat16
f32 = jnp.float32
log2_e = 1.4426950408889634
vmem_bytes = 58 * 1024 * 1024
vmem_small = 20 * 1024 * 1024


def matmul(left, right):
    return jnp.dot(left, right, preferred_element_type=f32)


def cross_rows(left, right):
    return lax.dot_general(left, right, (((0,), (0,)), ((), ())), preferred_element_type=f32)


def times_transposed(left, right):
    return lax.dot_general(left, right, (((1,), (1,)), ((), ())), preferred_element_type=f32)


def norm_parts(values):
    row_mean = jnp.mean(values, axis=-1, keepdims=True)
    centered = values - row_mean
    row_var = jnp.mean(centered * centered, axis=-1, keepdims=True)
    inverse = lax.rsqrt(row_var + norm_epsilon)
    return (centered * inverse, inverse)


def norm_back(grad_out, normal_hat, inverse, gain):
    scaled_grad = grad_out * gain
    return inverse * (
        scaled_grad
        - jnp.mean(scaled_grad, axis=-1, keepdims=True)
        - normal_hat * jnp.mean(scaled_grad * normal_hat, axis=-1, keepdims=True)
    )


def swap(v, axis, mask):
    size = lax.axis_size(axis)
    return lax.ppermute(v, axis, [(i, i ^ mask) for i in range(size)])


def ring_order(chips):
    return list(range(0, chips, 2)) + [k for k in range(chips - 1, 0, -1) if k % 2]


def next_chip(v):
    chips = lax.axis_size("blk") // 2
    order = ring_order(chips)
    moves = [(order[k], order[(k + 1) % chips]) for k in range(chips)]
    return lax.ppermute(v, "blk", [(2 * a + c, 2 * b + c) for a, b in moves for c in range(2)])


def pick(v, index):
    return lax.dynamic_index_in_dim(v, index, 0, keepdims=False)


def put(v, part, index):
    return lax.dynamic_update_index_in_dim(v, part, index, 0)


def bits_of(size):
    return [1 << k for k in range(size.bit_length() - 1)]


def blank(shape, dtype):
    return pl.pallas_call(
        lambda out: None,
        out_shape=jax.ShapeDtypeStruct(shape, dtype),
        out_specs=pl.BlockSpec(memory_space=pl.ANY),
        name="blank",
    )()


def hold(*values):
    return lax.optimization_barrier(values)


def gather_head(v):
    size = lax.axis_size("head")
    if size == 4:
        half = v.shape[0] // 2
        one, two = swap(v, "head", 1), swap(v, "head", 2)
        low = swap(two[:half], "head", 1)
        high = swap(one[half:], "head", 2)
        return [v, one, two, jnp.concatenate([low, high], axis=0)]
    held = [v]
    for bit in bits_of(size):
        held = held + [swap(part, "head", bit) for part in held]
    return held


def scatter_head(chunk):
    size = lax.axis_size("head")
    if size == 4:
        far = chunk(3).astype(bf16)
        half = far.shape[0] // 2
        low = swap(far[:half], "head", 1)
        high = swap(far[half:], "head", 2)
        one, two = chunk(1), chunk(2)
        one = jnp.concatenate([one[:half], one[half:] + high.astype(f32)], axis=0)
        two = jnp.concatenate([two[:half] + low.astype(f32), two[half:]], axis=0)
        one = swap(one.astype(bf16), "head", 1)
        two = swap(two.astype(bf16), "head", 2)
        return chunk(0) + one.astype(f32) + two.astype(f32)
    terms = [chunk(m) for m in range(size)]
    for bit in reversed(bits_of(size)):
        terms = [
            terms[m] + swap(terms[m | bit].astype(bf16), "head", bit).astype(f32) for m in range(bit)
        ]
    return terms[0]


def exchange(pieces, axis, mine, group):
    out = pieces
    for mask in range(1, group):
        out = put(out, swap(pick(pieces, mine ^ mask), axis, mask), mine ^ mask)
    return out


def scalars(*values):
    return jnp.stack([jnp.asarray(v, jnp.int32) for v in values])


def local_call(kernel, out_shapes, scalar, *arrays, name, vmem=None):
    return pl.pallas_call(
        kernel,
        in_specs=[pl.BlockSpec(memory_space=pltpu.SMEM)]
        + [pl.BlockSpec(memory_space=pltpu.VMEM)] * len(arrays),
        out_specs=[pl.BlockSpec(memory_space=pltpu.VMEM)] * len(out_shapes),
        out_shape=[jax.ShapeDtypeStruct(shape, dtype) for shape, dtype in out_shapes],
        compiler_params=pltpu.CompilerParams(vmem_limit_bytes=vmem or vmem_small),
        name=name,
    )(scalar, *arrays)


def place(blocks, at):
    count = len(blocks)

    def kernel(at_ref, *refs):
        for k in range(count):
            refs[count][at_ref[k]] = refs[k][...]

    shape = ((count,) + blocks[0].shape, blocks[0].dtype)
    return local_call(kernel, [shape], at, *blocks, name="place")[0]


def place_halves(first, parts, low, high, at):
    count, rows, width = first.shape

    def kernel(at_ref, first_ref, *refs):
        out = refs[-1]
        for k in range(count):
            out[k, 0] = first_ref[k]
        for m in range(count - 1):
            out[at_ref[m], 1] = refs[m][...]
        out[at_ref[count - 1], 1, : rows // 2] = refs[count - 1][...]
        out[at_ref[count - 1], 1, rows // 2 :] = refs[count][...]

    shape = ((count, 2, rows, width), first.dtype)
    return local_call(kernel, [shape], at, first, *parts, low, high, name="place_halves")[0]


def pack_sums(at, first, early, up_row, d_query, d_values, n_head, n_blk, wide, w_rows):
    ff = up_row.shape[1] // n_head
    own = d_query.shape[1]
    each = own // DH

    team = DH // w_rows

    def kernel(at_ref, first_ref, *refs):
        earlies, up_ref, query_ref, value_ref, out = refs[:-4], *refs[-4:]
        vectors = [first_ref[0:1, :], first_ref[1:2, :]] + [ref[...] for ref in earlies]
        totals = [
            jnp.sum(ref[...].astype(bf16).astype(f32), axis=0, keepdims=True)
            for ref in (query_ref, value_ref)
        ]
        for h in range(n_head):
            for b in range(n_blk):
                low = (h * n_blk + b) * w_rows
                row = [v[:, low : low + w_rows] for v in vectors]
                mine = jnp.where(at_ref[0] == b, 1.0, 0.0)
                row.append(up_ref[:, h * ff : (h + 1) * ff] * mine)
                for total in totals:
                    part = jnp.zeros((1, w_rows), f32)
                    for i in range(each):
                        for k in range(team):
                            here = (at_ref[1] + i == h) & (at_ref[2] + k == b)
                            low = i * DH + k * w_rows
                            part += total[:, low : low + w_rows] * jnp.where(here, 1.0, 0.0)
                    row.append(part)
                used = sum(part.shape[1] for part in row)
                if used < wide:
                    row.append(jnp.zeros((1, wide - used), f32))
                out[h, b : b + 1, :] = jnp.concatenate(row, axis=1)

    shape = ((n_head, n_blk, wide), f32)
    return local_call(
        kernel, [shape], at, first, *early, up_row, d_query, d_values, name="pack_sums"
    )[0]


def place_cores(pieces, at):
    count = len(pieces)

    def kernel(at_ref, *refs):
        for k in range(count):
            for c in range(2):
                refs[count + c][at_ref[k]] = refs[k][c]

    shape = ((count,) + pieces[0].shape[1:], pieces[0].dtype)
    return local_call(kernel, [shape, shape], at, *pieces, name="place_cores")


def lanes(start, size):
    return pl.ds(pl.multiple_of(start, DH), size)


def split_columns(arrays, width, columns_of, core, chips, name):
    rows = arrays[0].shape[0]

    def kernel(core_ref, *refs):
        sources, (mine, other) = refs[:-2], refs[-2:]
        me = core_ref[0]
        for chip in range(chips):
            for out, index in ((mine, me), (other, 1 - me)):
                starts, run = columns_of(2 * chip + index)
                for p, source in enumerate(sources):
                    for i, start in enumerate(starts):
                        low = p * width + i * run
                        out[chip, :, low : low + run] = source[:, lanes(start, run)]

    shape = ((chips, rows, len(arrays) * width), arrays[0].dtype)
    return local_call(
        kernel, [shape, shape], scalars(core), *arrays, name=name, vmem=vmem_bytes
    )


def pair_up(mine, other, chip, core):
    chips = mine.shape[0]

    def kernel(at, mine_ref, other_ref, *outs):
        for m in range(chips):
            outs[m][at[1]] = mine_ref[at[0] ^ m]
            outs[m][1 - at[1]] = other_ref[at[0] ^ m]

    shape = ((2,) + mine.shape[1:], mine.dtype)
    return local_call(kernel, [shape] * chips, scalars(chip, core), mine, other, name="pair_up")


def swap_chips(pieces):
    return [pieces[0]] + [swap(pieces[m], "blk", 2 * m) for m in range(1, len(pieces))]


def merge_columns(pieces, count, width, columns_of, chip, name, row=None):
    chips = len(pieces)
    rows = pieces[0].shape[1] if row is None else row
    total = 2 * chips * width

    def kernel(at, *refs):
        sources, outs = refs[:chips], refs[chips:]
        sums = None
        for m in range(chips):
            for core in range(2):
                starts, run = columns_of(2 * (at[0] ^ m) + core)
                for p in range(count):
                    for i, start in enumerate(starts):
                        low = p * width + i * run
                        part = sources[m][core, :rows, low : low + run]
                        outs[p][:, lanes(start, run)] = part.astype(f32)
                if row is not None:
                    part = sources[m][core, rows:, :].astype(f32)
                    sums = part if sums is None else sums + part
        if row is not None:
            outs[count][...] = sums

    shapes = [((rows, total), f32)] * count
    if row is not None:
        shapes.append(((pieces[0].shape[1] - row, count * width), f32))
    return local_call(kernel, shapes, scalars(chip), *pieces, name=name)


def each_tile(heads, tiles, whole, body):
    for i in range(heads):
        for t in range(tiles):
            if whole:
                body(i, t)
            else:
                pl.when(pl.program_id(0) == i * tiles + t)(functools.partial(body, i, t))


def fixed_blocks(arrays):
    return [
        pl.BlockSpec(array.shape, lambda i, n=len(array.shape): (0,) * n) for array in arrays
    ]


def attend(heads_at, which, first, tok, query, keys, values, state, final):
    rows, width = query.shape
    heads, tiles, ways = width // DH, rows // tile, heads_at.shape[0]
    factor = log2_e * DH**-0.5
    carried = state is not None
    arrays = []
    for array, _ in [keys[m] for m in which] + [values[m] for m in which]:
        if not any(array is other for other in arrays):
            arrays.append(array)

    def find(entry):
        return [array is entry[0] for array in arrays].index(True), entry[1]

    def kernel(heads_ref, first_ref, query_ref, *refs):
        parts = refs[: len(arrays)]
        outs = refs[-2:]

        def body(i, t):
            lane, here = pl.ds(i * DH, DH), pl.ds(t * tile, tile)
            seen = (t + 1) * tile
            row = t * tile + lax.broadcasted_iota(jnp.int32, (tile, 1), 0)
            column = lax.broadcasted_iota(jnp.int32, (1, seen), 1)
            row = (row // tok * ways + heads_ref[0]) * tok + row % tok
            start = jnp.transpose(jnp.broadcast_to(first_ref[:, here], (DH, tile)))[:, :1]
            if carried:
                stats = refs[len(arrays) + 1]
                high = jnp.transpose(jnp.broadcast_to(stats[i, 0:1, here], (DH, tile)))[:, :1]
                total = jnp.transpose(jnp.broadcast_to(stats[i, 1:2, here], (DH, tile)))[:, :1]
                top = high
            else:
                top = jnp.full((tile, 1), masked_fill, f32)
            scores = []
            for m in which:
                k, index = find(keys[m])
                raw = times_transposed(query_ref[here, lane], parts[k][index, :seen, lane])
                pos = (column // tok * ways + heads_ref[m]) * tok + column % tok
                keep = (pos[:, t * tile :] <= row) & (pos[:, t * tile :] >= start)
                last = jnp.where(keep, raw[:, t * tile :], masked_fill)
                if t > 0:
                    rest = jnp.where(pos[:, : t * tile] >= start, raw[:, : t * tile], masked_fill)
                    last = jnp.concatenate([rest, last], axis=1)
                scores.append(last)
                top = jnp.maximum(top, jnp.max(last, axis=-1, keepdims=True))
            if carried:
                shrink = jnp.exp2((high - top) * factor)
                total, acc = total * shrink, refs[len(arrays)][here, lane] * shrink
            else:
                total, acc = jnp.zeros((tile, 1), f32), jnp.zeros((tile, DH), f32)
            for m, part in zip(which, scores):
                weights = jnp.exp2((part - top) * factor)
                total = total + jnp.sum(weights, axis=-1, keepdims=True)
                k, index = find(values[m])
                acc = acc + matmul(weights.astype(bf16), parts[k][index, :seen, lane])

            def as_row(value):
                return jnp.transpose(jnp.broadcast_to(value, (tile, DH)))[0:1, :]

            if final:
                outs[0][here, lane] = (acc / total).astype(bf16)
                outs[1][i, :, here] = as_row(top * factor + jnp.log2(total))
            else:
                outs[0][here, lane] = acc
                outs[1][i, 0:1, here] = as_row(top)
                outs[1][i, 1:2, here] = as_row(total)

        each_tile(heads, tiles, rows * len(which) <= 4096, body)

    pairs = rows * rows * len(which) * heads // 2
    operands = [first, query, *arrays, *(state if carried else [])]
    shapes = [
        jax.ShapeDtypeStruct((rows, width), bf16 if final else f32),
        jax.ShapeDtypeStruct((heads, 1 if final else 2, rows), f32),
    ]
    return pl.pallas_call(
        kernel,
        grid=(1 if rows * len(which) <= 4096 else heads * tiles,),
        in_specs=[pl.BlockSpec(memory_space=pltpu.SMEM)] + fixed_blocks(operands),
        out_specs=fixed_blocks(shapes),
        out_shape=shapes,
        compiler_params=pltpu.CompilerParams(vmem_limit_bytes=vmem_bytes),
        cost_estimate=pl.CostEstimate(
            flops=4 * pairs * DH,
            bytes_accessed=4 * rows * width * len(which),
            transcendentals=pairs,
        ),
        name="attend",
    )(heads_at, *operands)


def attend_back(heads_at, m, first, tok, log_total, delta, query, d_out, key, value, dq_in):
    rows, width = query.shape
    heads, tiles, ways = width // DH, rows // tile, heads_at.shape[0]
    factor, scaling = log2_e * DH**-0.5, DH**-0.5
    carried = dq_in is not None
    parts = [key[0]] if key[0] is value[0] else [key[0], value[0]]

    def kernel(heads_ref, first_ref, log_ref, delta_ref, query_ref, out_ref, *refs):
        keys, values = refs[0], refs[len(parts) - 1]
        dq, dk, dv = refs[-3:]

        def body(i, t):
            lane, here = pl.ds(i * DH, DH), pl.ds(t * tile, tile)
            ahead = pl.ds(t * tile, rows - t * tile)
            k_tile, v_tile = keys[key[1], here, lane], values[value[1], here, lane]
            q_part, d_part = query_ref[ahead, lane], out_ref[ahead, lane]
            scores = times_transposed(k_tile, q_part) * factor
            pos = t * tile + lax.broadcasted_iota(jnp.int32, (tile, 1), 0)
            pos = (pos // tok * ways + heads_ref[m]) * tok + pos % tok
            row = t * tile + lax.broadcasted_iota(jnp.int32, (1, tile), 1)
            row = (row // tok * ways + heads_ref[0]) * tok + row % tok
            probs = jnp.exp2(scores - log_ref[i, :, ahead])
            start = first_ref[:, ahead]
            keep = (pos >= start[:, :tile]) & (pos <= row)
            near = jnp.where(keep, probs[:, :tile], 0.0)
            if rows > (t + 1) * tile:
                far = jnp.where(pos >= start[:, tile:], probs[:, tile:], 0.0)
                probs = jnp.concatenate([near, far], axis=1)
            else:
                probs = near
            dv[here, lane] = matmul(probs.astype(bf16), d_part).astype(bf16)
            d_probs = times_transposed(v_tile, d_part)
            d_scores = (probs * (d_probs - delta_ref[i, :, ahead])).astype(bf16)
            dk[here, lane] = (scaling * matmul(d_scores, q_part)).astype(bf16)
            term = scaling * cross_rows(d_scores, k_tile)
            if t > 0:
                dq[ahead, lane] += term
            elif carried:
                dq[:, lane] = refs[len(parts)][:, lane] + term
            else:
                dq[:, lane] = term

        each_tile(heads, tiles, rows <= 1024, body)

    pairs = rows * rows * heads // 2
    operands = [first, log_total, delta, query, d_out, *parts] + ([dq_in] if carried else [])
    shapes = [jax.ShapeDtypeStruct((rows, width), kind) for kind in (f32, bf16, bf16)]
    return pl.pallas_call(
        kernel,
        grid=(1 if rows <= 1024 else heads * tiles,),
        in_specs=[pl.BlockSpec(memory_space=pltpu.SMEM)] + fixed_blocks(operands),
        out_specs=fixed_blocks(shapes),
        out_shape=shapes,
        compiler_params=pltpu.CompilerParams(vmem_limit_bytes=vmem_bytes),
        cost_estimate=pl.CostEstimate(
            flops=10 * pairs * DH, bytes_accessed=20 * rows * width, transcendentals=pairs
        ),
        name="attend_back",
    )(heads_at, *operands)


def normalized(values):
    centered = values - jnp.mean(values, axis=-1, keepdims=True)
    return centered * lax.rsqrt(jnp.mean(centered * centered, axis=-1, keepdims=True) + norm_epsilon)


def project_in(at, mine, other, gain, shift, weights, bias):
    chips, count = len(mine), len(weights)
    tok, width = mine[0].shape
    columns = weights[0].shape[2]
    own = columns // 3

    def body(at_ref, *refs):
        mine_refs, other_refs = refs[:chips], refs[chips : 2 * chips]
        gain_ref, shift_ref, bias_ref = refs[2 * chips : 2 * chips + 3]
        weight_refs = refs[2 * chips + 3 : 2 * chips + 3 + count]
        query, key_value, normed, whole = refs[2 * chips + 3 + count :]
        core = at_ref[chips]

        @pl.when(pl.program_id(0) == 0)
        def _():
            for k, part in enumerate(weight_refs):
                for z in range(chips):
                    low = pl.multiple_of(at_ref[chips + 1 + k] + z * 2 * part.shape[1], 16)
                    whole[pl.ds(low, part.shape[1]), :] = part[z]

        for step in range(chips):

            @pl.when(pl.program_id(0) == step)
            def _():
                for part, place in ((mine_refs[step], core), (other_refs[step], 1 - core)):
                    hat = normalized(part[...].astype(f32))
                    low = pl.multiple_of(place * tok, tok)
                    normed[pl.ds(low, tok), :] = (hat * gain_ref[...] + shift_ref[...]).astype(bf16)

        product = matmul(normed[...], whole[...]) + bias_ref[...]
        product = product.astype(bf16)
        query[...] = product[:, :own]
        key_value[0] = product[:, own : 2 * own]
        key_value[1] = product[:, 2 * own :]

    def fixed(shape):
        return pl.BlockSpec(shape, lambda i, at_ref: (0,) * len(shape))

    rows = 2 * tok * chips
    arrays = [*mine, *other, gain, shift, bias, *weights]
    return pl.pallas_call(
        body,
        grid_spec=pltpu.PrefetchScalarGridSpec(
            num_scalar_prefetch=1,
            grid=(chips,),
            in_specs=[fixed(array.shape) for array in arrays],
            out_specs=[
                pl.BlockSpec((2 * tok, own), lambda i, at_ref: (at_ref[i], 0)),
                pl.BlockSpec((2, 2 * tok, own), lambda i, at_ref: (0, at_ref[i], 0)),
                pl.BlockSpec((2 * tok, width), lambda i, at_ref: (at_ref[i], 0)),
                fixed((width, columns)),
            ],
        ),
        out_shape=[
            jax.ShapeDtypeStruct((rows, own), bf16),
            jax.ShapeDtypeStruct((2, rows, own), bf16),
            jax.ShapeDtypeStruct((rows, width), bf16),
            jax.ShapeDtypeStruct((width, columns), bf16),
        ],
        compiler_params=pltpu.CompilerParams(vmem_limit_bytes=vmem_bytes),
        cost_estimate=pl.CostEstimate(
            flops=2 * rows * width * columns, bytes_accessed=8 * rows * width, transcendentals=0
        ),
        name="project_in",
    )(at, *arrays)


def terms_out(at, array, weights, transposed):
    steps = at.shape[0] // 2
    rows, width = array.shape
    tok = rows // (2 * steps)
    out_width = weights.shape[0] if transposed else weights.shape[1]
    run = out_width // 4

    def body(at_ref, source, part, mine, other, held):
        @pl.when(pl.program_id(0) == 0)
        def _():
            for k in range(2 * steps):
                low = pl.multiple_of(at_ref[k] * tok, tok)
                row = (k % 2) * (rows // 2) + (k // 2) * tok
                held[row : row + tok, :] = source[pl.ds(low, tok), :]

        for e, out in ((1, other), (0, mine)):
            left = held[e * (rows // 2) : (e + 1) * (rows // 2), :]
            term = (times_transposed if transposed else matmul)(left, part[...])
            out[...] = term.astype(bf16).reshape(steps, tok, run)

    stacked = pl.BlockSpec((steps, tok, run), lambda i, at_ref: (0, 0, i))
    shape = jax.ShapeDtypeStruct((steps, tok, out_width), bf16)
    if transposed:
        part = pl.BlockSpec((run, width), lambda i, at_ref: (i, 0))
    else:
        part = pl.BlockSpec((width, run), lambda i, at_ref: (0, i))
    return pl.pallas_call(
        body,
        grid_spec=pltpu.PrefetchScalarGridSpec(
            num_scalar_prefetch=1,
            grid=(4,),
            in_specs=[pl.BlockSpec((rows, width), lambda i, at_ref: (0, 0)), part],
            out_specs=[stacked, stacked],
            scratch_shapes=[pltpu.VMEM((rows, width), bf16)],
        ),
        out_shape=[shape, shape],
        compiler_params=pltpu.CompilerParams(vmem_limit_bytes=vmem_bytes),
        cost_estimate=pl.CostEstimate(
            flops=2 * rows * width * out_width,
            bytes_accessed=4 * rows * out_width,
            transcendentals=0,
        ),
        name="terms_out",
    )(at, array, weights)


def norm_sums(own, other, mine, others):
    chips, tok, width = own.shape

    def body(*refs):
        terms, pieces, out = refs[:2], refs[2 : 2 + 2 * chips], refs[-1]
        step = pl.program_id(0)

        @pl.when(step == 0)
        def _():
            out[...] = jnp.zeros_like(out)

        for k in range(chips):

            @pl.when(step == k)
            def _():
                for e in (0, 1):
                    term = terms[e][0].astype(f32)
                    hat = normalized(pieces[e * chips + k][...].astype(f32))
                    out[0:1, :] += jnp.sum(term * hat, axis=0, keepdims=True)
                    out[1:2, :] += jnp.sum(term, axis=0, keepdims=True)

    stacked = pl.BlockSpec((1, tok, width), lambda i: (i, 0, 0))
    return pl.pallas_call(
        body,
        grid=(chips,),
        in_specs=[stacked, stacked] + fixed_blocks([*mine, *others]),
        out_specs=pl.BlockSpec((2, width), lambda i: (0, 0)),
        out_shape=jax.ShapeDtypeStruct((2, width), f32),
        compiler_params=pltpu.CompilerParams(vmem_limit_bytes=vmem_bytes),
        name="norm_sums",
    )(own, other, *mine, *others)


def mix_back(at, parts, weights, mixed, earlier):
    count = len(parts)
    tok = parts[0].shape[0]
    rows, own = mixed.shape
    heads = own // DH

    def kernel(at_ref, *refs):
        whole, outs = refs[count], refs[count + 1 :]
        d_mixed = outs[2] if earlier is not None else outs[0]
        if earlier is not None:
            mixed_ref, before, _, delta = outs
            d_mixed[...] = before[...]
        for k in range(count):
            here = pl.ds(pl.multiple_of(at_ref[k] * tok, tok), tok)
            d_mixed[here, :] = times_transposed(refs[k][...], whole[...]).astype(bf16)
        if earlier is not None:
            products = d_mixed[...].astype(f32) * mixed_ref[...].astype(f32)
            for k in range(heads):
                turned = jnp.transpose(products[:, k * DH : (k + 1) * DH])
                delta[k] = jnp.sum(turned, axis=0, keepdims=True)

    shapes = [((rows, own), bf16)]
    if earlier is None:
        return local_call(kernel, shapes, at, *parts, weights, name="mix_back", vmem=vmem_bytes)[0]
    shapes.append(((heads, 1, rows), f32))
    return local_call(
        kernel, shapes, at, *parts, weights, mixed, earlier, name="mix_back", vmem=vmem_bytes
    )


def mix_grad(at, mine, other, mixed, each, team):
    chips = len(mine)
    tok, width = mine[0].shape
    own = mixed.shape[1]
    w_rows = own // (each * team)

    def kernel(at_ref, *refs):
        parts = [refs[e * chips + k] for k in range(chips) for e in (0, 1)]
        mixed_ref, out = refs[2 * chips :]
        total = None
        for k, part in enumerate(parts):
            here = pl.ds(pl.multiple_of(at_ref[k] * tok, tok), tok)
            term = cross_rows(mixed_ref[here, :], part[...])
            total = term if total is None else total + term
        total = total.astype(bf16)
        for i in range(each):
            for j in range(team):
                low = (i * team + j) * w_rows
                out[j, i] = total[low : low + w_rows]

    shape = ((team, each, w_rows, width), bf16)
    return local_call(kernel, [shape], at, *mine, *other, mixed, name="mix_grad", vmem=vmem_bytes)[0]


def reorder(array, at):
    def kernel(at_ref, source, out):
        for k in range(array.shape[0]):
            out[k] = source[at_ref[k]]

    return local_call(kernel, [(array.shape, array.dtype)], at, array, name="reorder")[0]


def local(
    tokens,
    segments,
    cotangent,
    first_gain,
    first_shift,
    query_proj,
    key_proj,
    value_proj,
    query_bias,
    value_bias,
    out_proj,
    out_bias,
    second_gain,
    second_shift,
    up_proj,
    up_bias,
    down_proj,
    down_bias,
):
    n_head, n_blk = lax.axis_size("head"), lax.axis_size("blk")
    head, blk = lax.axis_index("head"), lax.axis_index("blk")
    chips = n_blk // 2
    chip, core = blk // 2, blk % 2
    tok = tokens.shape[0]
    rows = tok * n_blk
    w_rows = query_proj.shape[0]
    ff_rows = down_proj.shape[0]
    team = DH // w_rows
    sets = n_blk // team
    each = n_head // team
    place_in = blk % team
    own_heads = each * DH

    ring = ring_order(chips)
    behind = jnp.array(
        [[ring[(ring.index(z) - k) % chips] for k in range(chips)] for z in range(chips)], jnp.int32
    )
    behind_all = pick(behind, chip)
    behind = [behind_all[k] for k in range(chips)]

    def spot(step, other):
        return (2 * behind[step] + (core ^ other)) * tok

    def fill_pair(buffer, mine, other, step):
        buffer = lax.dynamic_update_slice_in_dim(buffer, mine, spot(step, 0), 0)
        return lax.dynamic_update_slice_in_dim(buffer, other, spot(step, 1), 0)

    square = n_head == 4

    def head_columns(b):
        at = (b % team) * each
        return [((at + i) * sets + b // team) * DH for i in range(each)], DH

    def ff_columns(b):
        return [(h * n_blk + b) * ff_rows for h in range(n_head)], ff_rows

    ways, two_cores = jnp.arange(n_head, dtype=jnp.int32), jnp.arange(2, dtype=jnp.int32)
    heads_at = head ^ ways
    chips_at = chip ^ jnp.arange(chips, dtype=jnp.int32)
    blocks_at = (2 * behind_all[:, None] + (core ^ two_cores)[None, :]).reshape(-1)
    weights_at = (heads_at[:, None] * n_blk + two_cores[None, :]).reshape(-1) * w_rows
    weights_at = jnp.concatenate([behind_all, core[None], weights_at])

    with jax.named_scope("tokens_gather"):
        tok_mine, tok_other = [tokens], []
        tok_mine.append(next_chip(tokens))

    with jax.named_scope("tokens_gather"):
        tok_other.append(swap(tokens, "blk", 1))

    with jax.named_scope("vectors"):
        small = [
            first_gain,
            first_shift,
            query_bias,
            value_bias,
            out_bias,
            second_gain,
            second_shift,
            down_bias,
            up_bias,
            segments.astype(bf16),
        ]
        small = [v.reshape(-1, w_rows).astype(f32) for v in small]
        height = sum(v.shape[0] for v in small)
        above, packed = 0, 0.0
        for v in small:
            packed = packed + lax.pad(
                v, f32(0), ((above, height - above - v.shape[0], 0), (0, 0, 0))
            )
            above += v.shape[0]
        small = packed.astype(bf16)[None]
    with jax.named_scope("qkv_weights"):
        mine, other = split_columns(
            [query_proj, key_proj, value_proj], own_heads, head_columns, core, chips, "split_heads"
        )
    with jax.named_scope("down_weights"):
        half = ff_rows // 2
        if square:
            down_first = lax.all_gather(down_proj[:half], "head", axis=0, tiled=False)
        else:
            down_first = down_proj
    with jax.named_scope("qkv_weights"):
        pieces = pair_up(mine, swap(other, "blk", 1), chip, core)

    places = (heads_at, chips_at, blocks_at, weights_at)
    pieces, small, up_proj, tok_mine, tok_other, places = hold(
        pieces, small, up_proj, tok_mine, tok_other, places
    )
    heads_at, chips_at, blocks_at, weights_at = places

    with jax.named_scope("qkv_weights"):
        pieces = swap_chips(pieces)
        fused = place_cores(pieces, chips_at)
    with jax.named_scope("vectors"):
        for bit in bits_of(n_head):
            small = jnp.concatenate([small, swap(small, "head", bit)])
        small = jnp.concatenate([small, swap(small, "blk", 1)])
        for bit in bits_of(chips)[:1]:
            small = jnp.concatenate([small, swap(small, "blk", 2 * bit)])

    fused, small, tok_mine, tok_other, up_proj, down_first = hold(
        fused, small, tok_mine, tok_other, up_proj, down_first
    )

    def small_table():
        height, width = small.shape[1:]
        source = small.reshape(n_head * n_blk, height * width)
        index = jnp.arange(n_head * n_blk, dtype=jnp.int32)
        from_chip = chip ^ (index // (2 * n_head))
        from_core = core ^ (index // n_head % 2)
        from_row = (head ^ (index % n_head)) * n_blk + 2 * from_chip + from_core
        select = (from_row[None, :] == index[:, None]).astype(bf16)
        return matmul(select, source).reshape(n_head, n_blk, height * width)

    def vector(index):
        return table[:, :, index * w_rows : (index + 1) * w_rows].reshape(1, D)

    for step in range(1, chips - 1):
        with jax.named_scope("tokens_gather"):
            tok_mine.append(next_chip(tok_mine[step]))
            tok_other.append(swap(tok_mine[step], "blk", 1))
        with jax.named_scope("qkv_weights"):
            if step == 1 and square:
                one = [swap(part, "head", 1) for part in fused]
                two = [swap(part, "head", 2) for part in fused]
            if step == 2 and square:
                low, high = swap(two[0], "head", 1), swap(one[1], "head", 2)
            if step == 1 and not square:
                fused_parts = [gather_head(part) for part in fused]
                fused_parts = [part[m] for m in range(n_head) for part in fused_parts]
        if step == chips - 2:
            with jax.named_scope("vectors"):
                for bit in bits_of(chips)[1:]:
                    small = jnp.concatenate([small, swap(small, "blk", 2 * bit)])
        if step == 1:
            with jax.named_scope("up_weights"):
                up_mine, up_other = split_columns(
                    [up_proj], n_head * ff_rows, ff_columns, core, chips, "split_up"
                )
        if step == 1:
            tok_mine, tok_other, up_mine, up_other, small = hold(
                tok_mine, tok_other, up_mine, up_other, small
            )
        elif step < chips - 2:
            tok_mine, small = hold(tok_mine, small)
    if square:
        fused_parts = [*fused, *one, *two, low, high]
    with jax.named_scope("vectors"):
        table = small_table()
    with jax.named_scope("vectors"):

        def own_head_part(full):
            part = full.reshape(n_head, sets, DH)
            part = lax.dynamic_index_in_dim(part, blk // team, 1, keepdims=False)
            return lax.dynamic_slice_in_dim(part, place_in * each, each, 0).reshape(1, own_heads)

        gain_first, shift_first = vector(0), vector(1)
        q_bias, v_bias = own_head_part(vector(2)), own_head_part(vector(3))
        qkv_bias = jnp.concatenate([q_bias, jnp.zeros_like(q_bias), v_bias], axis=1)
    first_vectors = (gain_first, shift_first, qkv_bias)
    fused_parts, tok_mine, tok_other, cotangent, up_other, out_proj, first_vectors = hold(
        fused_parts, tok_mine, tok_other, cotangent, up_other, out_proj, first_vectors
    )
    gain_first, shift_first, qkv_bias = first_vectors

    with jax.named_scope("tokens_gather"):
        tok_other.append(swap(tok_mine[chips - 1], "blk", 1))
    with jax.named_scope("qkv"):
        query, kv, normed, qkv_w = project_in(
            weights_at,
            tok_mine,
            tok_other,
            gain_first,
            shift_first,
            fused_parts,
            qkv_bias,
        )
    with jax.named_scope("up_weights"):
        up_pieces = pair_up(up_mine, swap(up_other, "blk", 1), chip, core)
    with jax.named_scope("out_weights"):
        out_parts = [out_proj] + [swap(out_proj, "head", m) for m in range(1, n_head)]
    query, kv, up_pieces, normed, out_parts, cotangent, qkv_w, table = hold(
        query, kv, up_pieces, normed, out_parts, cotangent, qkv_w, table
    )

    with jax.named_scope("kv_gather"):
        keys, values = [(kv, 0)], [(kv, 1)]
        if square:
            kv_parts = [swap(kv, "head", 1), swap(kv, "head", 2)]
        else:
            kv_parts = gather_head(kv)[1:]
    with jax.named_scope("up_weights"):
        up_pieces = swap_chips(up_pieces)
    with jax.named_scope("vectors"):
        seq = table[:, :, 8 * w_rows + ff_rows :]
        seg_all = seq.transpose(1, 0, 2).reshape(-1)
        seg_rows = pick(seq, head).reshape(rows)
        first_pos = jnp.sum((seg_all[:, None] < seg_rows[None, :]).astype(jnp.int32), axis=0)[None]
    with jax.named_scope("attention"):
        state = attend(heads_at, [0], first_pos, tok, query, keys, values, None, False)
    if square:
        down_second = down_proj[half:]
    else:
        down_second = down_proj
    kv_parts, state, up_pieces, cotangent, out_parts, first_pos, down_second = hold(
        kv_parts, state, up_pieces, cotangent, out_parts, first_pos, down_second
    )

    with jax.named_scope("dy_gather"):
        dy_all = lax.all_gather(cotangent, "blk", axis=0, tiled=True)
    with jax.named_scope("up_weights"):
        up_part = place(up_pieces, chips_at).reshape(n_blk * w_rows, n_head * ff_rows)
    with jax.named_scope("kv_gather"):
        keys += [(part, 0) for part in kv_parts]
        values += [(part, 1) for part in kv_parts]
        if square:
            low = swap(kv_parts[1][:1], "head", 1)
            high = swap(kv_parts[0][1:], "head", 2)
    with jax.named_scope("out_weights"):
        out_w = place(out_parts, heads_at).reshape(team, each, w_rows, D)
        out_w = exchange(out_w, "blk", place_in, team)
        out_w = out_w.transpose(1, 0, 2, 3).reshape(own_heads, D)
    if square:
        low, high, out_w, state, up_part, down_second = hold(
            low, high, out_w, state, up_part, down_second
        )
        keys.append((low, 0))
        values.append((high, 0))
    else:
        out_w, state, up_part, down_second = hold(out_w, state, up_part, down_second)
    with jax.named_scope("up_weights"):
        up_w = lax.all_gather(up_part, "head", axis=0, tiled=True)

    with jax.named_scope("attention"):
        left = list(range(1, n_head))
        mixed, log_total = attend(
            heads_at, left, first_pos, tok, query, keys, values, state, True
        )
    with jax.named_scope("down_weights"):
        if square:
            downs = [down_second, swap(down_second, "head", 1), swap(down_second, "head", 2)]
        else:
            downs = gather_head(down_second)
    mixed, out_w, table, downs = hold(mixed, out_w, table, downs)

    def cross(term):
        return (term[0], swap(term[1], "blk", 1))

    def onward(pair, moving):
        return next_chip(sum_of(pair, moving).astype(bf16))

    def sum_of(pair, moving):
        total = pair[0].astype(f32) + pair[1].astype(f32)
        return total if moving is None else total + moving.astype(f32)

    def met(own, other):
        return (own, swap(other, "blk", 1))

    def entry(pair, step):
        return (pair[0][step], pair[1][step])

    with jax.named_scope("branch"):
        ready = met(*terms_out(blocks_at, mixed, out_w, False))
        (ready,) = hold(ready)
        moving = None
        for step in range(1, chips):
            moving = onward(entry(ready, step), moving)
            with jax.named_scope("vectors"):
                if step == 1:
                    o_bias, gain_second, shift_second, d_bias = [vector(k) for k in range(4, 8)]
                    u_bias = table[:, :, 8 * w_rows : 8 * w_rows + ff_rows]
                    u_bias = lax.dynamic_index_in_dim(u_bias, blk, 1, keepdims=False)
                    vectors = (o_bias, gain_second, shift_second, d_bias, u_bias.reshape(1, -1))
            with jax.named_scope("down_weights"):
                if square and step == 2:
                    low = swap(downs[2][: half // 2], "head", 1)
                    high = swap(downs[1][half // 2 :], "head", 2)
                if not square and step == 1:
                    down_w = place(downs, heads_at).reshape(n_head * ff_rows, D)
            if step == 1:
                moving, ready, vectors, dy_all = hold(moving, ready, vectors, dy_all)
                o_bias, gain_second, shift_second, d_bias, u_bias = vectors
            elif square and step == 2:
                moving, ready, low, high = hold(moving, ready, low, high)
            else:
                moving, ready = hold(moving, ready)
        own = tokens.astype(f32)
        hidden = own + (sum_of(entry(ready, 0), moving) + o_bias)
        hat_second, inv_second = norm_parts(hidden)
        second_own = (hat_second * gain_second + shift_second).astype(bf16)
    hidden, second_own, inv_second = hold(hidden, second_own, inv_second)

    with jax.named_scope("down_weights"):
        if square:
            down_w = place_halves(down_first, downs, low, high, heads_at)
            down_w = down_w.reshape(n_head * ff_rows, D)

    with jax.named_scope("mlp"):
        second_all = blank((rows, D), bf16)
        active_all = blank((rows, n_head * ff_rows), bf16)
        d_upper_all = blank((rows, n_head * ff_rows), bf16)
        sec_mine, sec_other = [second_own], []
        terms = {}

        def mlp_chunk(step, second_all, active_all, d_upper_all):
            base = 2 * behind[step] * tok

            def chunk_of(array):
                return lax.dynamic_slice_in_dim(array, base, 2 * tok, 0)

            def fill(buffer, chunk):
                return lax.dynamic_update_slice_in_dim(buffer, chunk, base, 0)

            second_all = fill_pair(second_all, sec_mine[step], sec_other[step], step)
            upper = matmul(chunk_of(second_all), up_w) + u_bias
            phi = 0.5 * (1.0 + lax.erf(upper * 0.7071067811865476))
            active = (upper * phi).astype(bf16)
            slope = phi + upper * jnp.exp(-0.5 * upper * upper) * 0.3989422804014327
            d_active = times_transposed(chunk_of(dy_all), down_w)
            d_upper = (d_active * slope).astype(bf16)
            terms[step] = [
                times_transposed(
                    lax.dynamic_slice_in_dim(d_upper, (core ^ other) * tok, tok, 0), up_w
                ).astype(bf16)
                for other in (0, 1)
            ]
            return second_all, fill(active_all, active), fill(d_upper_all, d_upper)

        for step in range(chips):
            if step < chips - 1:
                sec_mine.append(next_chip(sec_mine[step]))
            if step > 0:
                second_all, active_all, d_upper_all = mlp_chunk(
                    step - 1, second_all, active_all, d_upper_all
                )
                if step == chips - 1:
                    ready = cross(terms[1])
            sec_other.append(swap(sec_mine[step], "blk", 1))
            ready, sec_mine, sec_other, terms, second_all, active_all, d_upper_all = hold(
                ready, sec_mine, sec_other, terms, second_all, active_all, d_upper_all
            )
        moving = None
        for step in range(1, chips):
            moving = onward(ready, moving)
            if step == 1:
                second_all, active_all, d_upper_all = mlp_chunk(
                    chips - 1, second_all, active_all, d_upper_all
                )
            ready = cross(terms[(step + 1) % chips])
            if step == 2:
                with jax.named_scope("up_grad"):
                    up_term = cross_rows(second_all, d_upper_all).astype(bf16)
                moving, ready, terms, active_all, d_upper_all, up_term = hold(
                    moving, ready, terms, active_all, d_upper_all, up_term
                )
            elif step == 3:
                with jax.named_scope("down_grad"):
                    down_term = cross_rows(active_all, dy_all).astype(bf16)
                moving, ready, terms, down_term, active_all = hold(
                    moving, ready, terms, down_term, active_all
                )
            else:
                moving, ready, terms, second_all, active_all, d_upper_all = hold(
                    moving, ready, terms, second_all, active_all, d_upper_all
                )
        d_second = sum_of(ready, moving)
        upstream = cotangent.astype(f32)
        d_hidden = upstream + norm_back(d_second, hat_second, inv_second, gain_second)
        d_branch_own = d_hidden.astype(bf16)

    def sum_heads(terms):
        return lax.psum_scatter(terms, "head", scatter_dimension=0, tiled=True)

    with jax.named_scope("up_grad"):
        up_sum = sum_heads(up_term)
    d_hidden, d_branch_own, active_all, d_second, d_upper_all, hat_second, cotangent = hold(
        d_hidden, d_branch_own, active_all, d_second, d_upper_all, hat_second, cotangent
    )
    mine, other = [d_branch_own], []

    with jax.named_scope("d_branch_gather"):
        half = tok // 2
        halves = [[d_branch_own[:half]], [d_branch_own[half:]]]
        with jax.named_scope("output"):
            out_term = matmul(active_all, down_w).astype(bf16)
        for step in range(chips - 1):
            for chain in halves:
                if step > 0:
                    (held,) = hold(chain[step])
                    chain[step] = held
                chain.append(next_chip(chain[step]))
            if step > 0:
                mine.append(jnp.concatenate([chain[step] for chain in halves], axis=0))
        mine.append(jnp.concatenate([chain[-1] for chain in halves], axis=0))
        with jax.named_scope("vector_grads"):
            early = [
                jnp.sum(d_branch_own.astype(f32), axis=0, keepdims=True),
                jnp.sum(d_second * hat_second, axis=0, keepdims=True),
                jnp.sum(d_second, axis=0, keepdims=True),
                jnp.sum(cotangent.astype(f32), axis=0, keepdims=True),
                jnp.sum(d_upper_all.astype(f32), axis=0, keepdims=True),
            ]
        mine, up_sum, out_term, early = hold(mine, up_sum, out_term, early)
        with jax.named_scope("output"):
            out_sum = lax.psum_scatter(out_term, "blk", scatter_dimension=0, tiled=True)
        other = [swap(piece, "blk", 1) for piece in mine]
        by_core = blocks_at.reshape(chips, 2)
        d_mixed = mix_back(by_core[:, 0], mine, out_w, mixed, None)
        d_mixed, delta = mix_back(by_core[:, 1], other, out_w, mixed, d_mixed)
    d_mixed, delta, mine, other = hold(d_mixed, delta, mine, other)

    dq = None

    def kv_grad(m):
        return attend_back(
            heads_at, m, first_pos, tok, log_total, delta, query, d_mixed, keys[m], values[m], dq
        )

    d_keys, d_values = {}, {}
    for m in reversed(range(n_head)):
        with jax.named_scope("attention_back"):
            if square and m == 2:
                low = swap(d_keys[3], "head", 1)
                high = swap(d_values[3], "head", 2)
            if square and m == 0:
                one = [d_keys[1], (d_values[1].astype(f32) + high.astype(f32)).astype(bf16)]
                two = [(d_keys[2].astype(f32) + low.astype(f32)).astype(bf16), d_values[2]]
                one, two, dq, up_sum = hold(one, two, dq, up_sum)
                one[0], two[0] = swap(one[0], "head", 1), swap(two[0], "head", 2)
            dq, d_keys[m], d_values[m] = kv_grad(m)
        if square and m == 1:
            low, high, dq, d_keys, d_values, d_mixed = hold(
                low, high, dq, d_keys, d_values, d_mixed
            )
        elif m > 0:
            dq, d_keys, d_values, d_mixed = hold(dq, d_keys, d_values, d_mixed)
    with jax.named_scope("up_grad"):
        up_sum = up_sum.reshape(chips, 2, w_rows, n_head * ff_rows)
        up_mine = lax.dynamic_index_in_dim(up_sum, core, 1, keepdims=False)
        up_other = lax.dynamic_index_in_dim(up_sum, 1 - core, 1, keepdims=False)
        up_pieces = pair_up(up_mine, swap(up_other, "blk", 1), chip, core)
    if square:
        one, two, dq, mine, other, mixed, out_sum, down_term, up_pieces = hold(
            one, two, dq, mine, other, mixed, out_sum, down_term, up_pieces
        )
    with jax.named_scope("up_grad"):
        up_pieces = swap_chips(up_pieces)
    if square:
        with jax.named_scope("attention_back"):
            one[1], two[1] = swap(one[1], "head", 1), swap(two[1], "head", 2)
    with jax.named_scope("out_grad"):
        mix_term = mix_grad(blocks_at, mine, other, mixed, each, team)
    with jax.named_scope("down_grad"):
        down_grad = sum_heads(down_term)
    with jax.named_scope("attention_back"):
        if square:
            d_keys, d_values = [
                (total[0].astype(f32) + one[k].astype(f32) + two[k].astype(f32)).astype(bf16)
                for k, total in enumerate((d_keys, d_values))
            ]
        else:
            d_keys, d_values = [
                scatter_head(lambda m: total[m].astype(f32)).astype(bf16)
                for total in (d_keys, d_values)
            ]
        d_qkv = jnp.concatenate([dq.astype(bf16), d_keys, d_values], axis=1)
    d_qkv, up_pieces, mix_term = hold(d_qkv, up_pieces, mix_term)

    slab, wide = n_blk * w_rows, 3 * own_heads
    with jax.named_scope("d_normed"):
        own_terms, other_terms = terms_out(blocks_at, d_qkv, qkv_w, True)
        ready = met(own_terms, other_terms)
    ready, normed, d_qkv, mix_term, up_pieces = hold(ready, normed, d_qkv, mix_term, up_pieces)
    moving = None
    for step in range(1, chips):
        with jax.named_scope("d_normed"):
            moving = onward(entry(ready, step), moving)
        if step == 1:
            with jax.named_scope("qkv_grad"):
                qkv_term = cross_rows(normed, d_qkv).astype(bf16).reshape(n_head, slab, wide)
            late = (other_terms, mix_term, tok_mine, tok_other, dq, d_values)
            moving, ready, qkv_term, late = hold(moving, ready, qkv_term, late)
            other_terms, mix_term, tok_mine, tok_other, dq, d_values = late
        elif step == 2:
            with jax.named_scope("qkv_grad"):
                if square:
                    half = slab // 2
                    far = pick(qkv_term, head ^ 3)
                    low, high = swap(far[:half], "head", 1), swap(far[half:], "head", 2)
                else:
                    low = high = qkv_term
            with jax.named_scope("out_grad"):
                mix_term = exchange(mix_term, "blk", place_in, team)
            moving, ready, low, high, mix_term = hold(moving, ready, low, high, mix_term)
        elif step == 3:
            with jax.named_scope("qkv_grad"):
                if square:
                    one, two = pick(qkv_term, head ^ 1), pick(qkv_term, head ^ 2)
                    one = jnp.concatenate([one[:half], one[half:] + high])
                    two = jnp.concatenate([two[:half] + low, two[half:]])
                    one, two = swap(one, "head", 1), swap(two, "head", 2)
            with jax.named_scope("vector_grads"):
                first_sums = norm_sums(ready[0], other_terms, tok_mine, tok_other)
                parts = pack_sums(
                    scalars(blk, place_in * each, blk - place_in),
                    first_sums,
                    early[:4],
                    early[4],
                    dq,
                    d_values,
                    n_head,
                    n_blk,
                    wide,
                    w_rows,
                )
            moving, ready, parts, mix_term, down_grad = hold(
                moving, ready, parts, mix_term, down_grad
            )
        else:
            moving, ready = hold(moving, ready)
    deep = 1
    with jax.named_scope("out_grad"):
        out_grad = sum_heads(mix_term.reshape(n_head * w_rows, D))
    with jax.named_scope("vector_grads"):
        sums = scatter_head(lambda m: pick(parts, head ^ m))
        sums = sums.astype(bf16)
    with jax.named_scope("qkv_grad"):
        if square:
            qkv_grad = pick(qkv_term, head).astype(f32) + one.astype(f32) + two.astype(f32)
        else:
            qkv_grad = scatter_head(lambda m: pick(qkv_term, head ^ m).astype(f32))
        qkv_grad = qkv_grad.astype(bf16).reshape(chips, 2, w_rows, wide)
        extra = sums.reshape(chips, 2, deep, wide)
        extra = jnp.pad(extra, ((0, 0), (0, 0), (0, -deep % 16), (0, 0)))
        qkv_grad = jnp.concatenate([qkv_grad, extra], axis=2)
        qkv_mine = lax.dynamic_index_in_dim(qkv_grad, core, 1, keepdims=False)
        qkv_other = lax.dynamic_index_in_dim(qkv_grad, 1 - core, 1, keepdims=False)
        pieces = pair_up(qkv_mine, swap(qkv_other, "blk", 1), chip, core)
    pieces, up_pieces, down_grad, out_sum, moving = hold(
        pieces, up_pieces, down_grad, out_sum, moving
    )
    with jax.named_scope("qkv_grad"):
        pieces = swap_chips(pieces)
    with jax.named_scope("d_normed"):
        d_normed = sum_of(entry(ready, 0), moving)
        hat_first, inv_first = norm_parts(own)
        tokens_grad = (d_hidden + norm_back(d_normed, hat_first, inv_first, gain_first)).astype(bf16)
    with jax.named_scope("output"):
        output = (hidden + (out_sum.astype(f32) + d_bias)).astype(bf16)
    with jax.named_scope("up_grad"):
        (up_grad,) = merge_columns(up_pieces, 1, n_head * ff_rows, ff_columns, chip, "merge_up")
    with jax.named_scope("down_grad"):
        down_grad = down_grad.astype(f32)
    with jax.named_scope("qkv_grad"):
        *qkv_grad, sums = merge_columns(
            pieces, 3, own_heads, head_columns, chip, "merge_heads", row=w_rows
        )
    with jax.named_scope("vector_grads"):
        sums = sums[:deep].reshape(-1)
        cuts = [sums[i * w_rows : (i + 1) * w_rows] for i in range(6)]
        up_bias_grad = sums[6 * w_rows : 6 * w_rows + ff_rows]
        rest = sums[6 * w_rows + ff_rows : 8 * w_rows + ff_rows]

    return (
        output,
        tokens_grad,
        cuts[0],
        cuts[1],
        qkv_grad[0],
        qkv_grad[1],
        qkv_grad[2],
        rest[:w_rows],
        rest[w_rows:],
        out_grad.astype(f32),
        cuts[2],
        cuts[3],
        cuts[4],
        up_grad,
        up_bias_grad,
        down_grad,
        cuts[5],
    )


def solution(mesh):
    by_token = P(("blk", "head"), None)
    matrix = P(("head", "blk"), None)
    vector = P(("head", "blk"))
    return jax.shard_map(
        local,
        mesh=mesh,
        in_specs=(
            by_token,
            P(("blk", "head")),
            by_token,
            vector,
            vector,
            matrix,
            matrix,
            matrix,
            vector,
            vector,
            matrix,
            vector,
            vector,
            vector,
            matrix,
            vector,
            matrix,
            vector,
        ),
        out_specs=(
            by_token,
            by_token,
            vector,
            vector,
            matrix,
            matrix,
            matrix,
            vector,
            vector,
            matrix,
            vector,
            vector,
            vector,
            matrix,
            vector,
            matrix,
            vector,
        ),
        check_vma=False,
    )
```
